512 devices in a mesh: seq: 8 (over y, core), tp: 16 (over z), dp: 4 (over x).
Axes of the slice: x: 4, y: 4, z: 16, core: 2. Of those that a mesh axis runs over, the one named last changes fastest.
Arguments:
- query_rows: bfloat16 [4, 1024, 8192], P('dp', 'seq', 'tp'), may hold values from -8 to 8
- key_rows: bfloat16 [4, 1024, 1024], P('dp', 'seq', 'tp'), may hold values from -6 to 6
- value_rows: bfloat16 [4, 1024, 1024], P('dp', 'seq', 'tp'), may hold values from -6 to 6
- gate_rows: bfloat16 [4, 1024, 8192], P('dp', 'seq', 'tp'), may hold values from -6 to 6
- write_vec: bfloat16 [4, 1024, 128], P('dp', 'seq'), may hold values from -0.5 to 0.5
- read_vec: bfloat16 [4, 1024, 128], P('dp', 'seq'), may hold values from -0.5 to 0.5
- dt_raw: float32 [4, 128, 1024], P('dp', 'tp', 'seq'), may hold values from -4 to 4
- a_log: float32 [128], P('tp')
- skip_gain: float32 [128], P('tp'), may hold values from 0.5 to 1.5
- dt_bias: float32 [128], P('tp'), may hold values from -1 to 1
- out_grad: bfloat16 [4, 1024, 8192], P('dp', 'seq', 'tp'), may hold values from -6 to 6
Outputs:
- grad_query: float32 [4, 1024, 8192], P('dp', 'seq', 'tp')
- grad_key: float32 [4, 1024, 1024], P('dp', 'seq', 'tp')
- grad_value: float32 [4, 1024, 1024], P('dp', 'seq', 'tp')
- grad_gate: float32 [4, 1024, 8192], P('dp', 'seq', 'tp')
- grad_write: float32 [4, 1024, 128], P('dp', 'seq')
- grad_read: float32 [4, 1024, 128], P('dp', 'seq')
- grad_dt: float32 [4, 128, 1024], P('dp', 'tp', 'seq')
- grad_alog: float32 [128], P('tp')
- grad_skip: float32 [128], P('tp')
- grad_bias: float32 [128], P('tp')
The draws below stay inside these ranges and needn't reach their ends.
All inputs are finite; a program needn't handle non-finite values.
Results may differ from the reference program's by a relative error of at most 0.024.
Values may be sent and summed in bfloat16 or wider, within the bound.
A program may use at most 64 MiB of HBM per device.

```python
import math
import jax
import jax.numpy as jnp
from jax import lax

HD = 128
MP = 64
NS = 128
QH = 64
KVH = 8
MH = 128
LEN = 1024
SEQS = 4


def draw_query_rows(key, part):
    key = jax.random.fold_in(key, 101)
    values = 2.0 * jax.random.truncated_normal(key, -4.0, 4.0, (SEQS, LEN, QH * HD), jnp.float32)
    return values.astype(jnp.bfloat16)


def draw_key_rows(key, part):
    key = jax.random.fold_in(key, 202)
    values = jax.random.truncated_normal(key, -4.0, 4.0, (SEQS, LEN, KVH * HD), jnp.float32)
    return values.astype(jnp.bfloat16)


def draw_a_log(key, part):
    key = jax.random.fold_in(key, 303)
    spread = jax.random.uniform(key, (MH,), jnp.float32)
    lowest = jnp.log(0.05 / LEN)
    highest = jnp.log(0.05)
    return (lowest + spread * (highest - lowest)).astype(jnp.float32)


def block_levels(key, extent, cuts, low, largest):
    factor_of = 1.0
    for axis_at, shards_of in cuts:
        draws = jax.random.uniform(jax.random.fold_in(jax.random.fold_in(key, 6), axis_at), (shards_of,), jnp.float32, low / len(cuts), largest / len(cuts))
        factor_of = factor_of * jnp.repeat(jnp.exp(draws), extent[axis_at] // shards_of).reshape((-1,) + (1,) * (len(extent) - 1 - axis_at))
    return factor_of


def scatter_about(stream_key, dims, scale, most, shards=(), held_as=jnp.bfloat16):
    level = block_levels(stream_key, dims, shards, -0.22, 0.18) if shards else 1.0
    result = jax.random.normal(stream_key, dims, jnp.float32) * scale * level
    return jnp.minimum(jnp.maximum(result, -most), most).astype(held_as)


def setup_inputs(seed: int = 0) -> dict:
    streams_of = jax.random.split(jax.random.key(seed), 12)
    return {
        "query_rows": draw_query_rows(jax.random.fold_in(streams_of[11], 71), 0),
        "key_rows": draw_key_rows(jax.random.fold_in(streams_of[11], 71), 0),
        "value_rows": scatter_about(streams_of[2], (SEQS, LEN, KVH * HD), 1.0, 6.0, ((0, 4), (1, 8), (2, 16))),
        "gate_rows": scatter_about(streams_of[3], (SEQS, LEN, MH * MP), 1.0, 6.0, ((0, 4), (1, 8), (2, 16))),
        "write_vec": scatter_about(streams_of[4], (SEQS, LEN, NS), NS ** -0.5, 0.5, ((0, 4), (1, 8))),
        "read_vec": scatter_about(streams_of[5], (SEQS, LEN, NS), NS ** -0.5, 0.5, ((0, 4), (1, 8))),
        "dt_raw": scatter_about(streams_of[6], (SEQS, MH, LEN), 1.0, 4.0, ((0, 4), (1, 16), (2, 8)), jnp.float32),
        "a_log": draw_a_log(jax.random.fold_in(streams_of[11], 71), 0),
        "skip_gain": jnp.clip(0.5 + 1.0 * jax.random.uniform(streams_of[8], (MH,), jnp.float32) ** block_levels(streams_of[8], (MH,), ((0, 16),), -0.2, 0.2), 0.5, 1.5),
        "dt_bias": jnp.clip(jax.random.uniform(streams_of[9], (MH,), jnp.float32, -1.0, 1.0) * block_levels(streams_of[9], (MH,), ((0, 16),), -0.4, 0.0), -1.0, 1.0),
        "out_grad": scatter_about(streams_of[10], (SEQS, LEN, MH * MP), 1.0, 6.0, ((0, 4), (1, 8), (2, 16))),
    }


NEG_FILL = -1e+30
HIGH = lax.Precision.HIGHEST

def block_scan(inner, gate_in, write_in, read_in, dt_raw, a_log, skip_gain, dt_bias):
    num_rows, num_heads, head_width = inner.shape
    num_states = write_in.shape[1]
    block_len = math.gcd(num_rows, 256)
    block_count = num_rows // block_len
    step_dt = jax.nn.softplus(dt_raw + dt_bias[:, None])
    rate_all = step_dt * jnp.exp(a_log)[:, None]
    rate_blocks = rate_all.reshape(num_heads, block_count, block_len).transpose(1, 0, 2)
    dt_blocks = step_dt.reshape(num_heads, block_count, block_len).transpose(1, 0, 2)
    inner_blocks = inner.reshape(block_count, block_len, num_heads, head_width)
    write_blocks = write_in.reshape(block_count, block_len, num_states)
    read_blocks = read_in.reshape(block_count, block_len, num_states)
    causal = jnp.arange(block_len)[:, None] >= jnp.arange(block_len)[None, :]

    def advance(carried, pieces):
        rate_now, dt_now, inner_now, write_now, read_now = pieces
        cum_rate = jnp.cumsum(rate_now, axis=1)
        intersection = jnp.dot(read_now, write_now.T, precision=HIGH)
        log_gap = cum_rate[:, :, None] - cum_rate[:, None, :]
        weight = jnp.where(causal, jnp.exp(-jnp.maximum(log_gap, 0.0)), 0.0) * intersection[None] * dt_now[:, None, :]
        output = jnp.einsum('hts,shp->thp', weight, inner_now, precision=HIGH)
        output = output + jnp.einsum('tn,hpn->thp', read_now, carried, precision=HIGH) * jnp.exp(-cum_rate).T[:, :, None]
        to_end = jnp.exp(-(cum_rate[:, -1:] - cum_rate)) * dt_now
        next_state = jnp.exp(-cum_rate[:, -1])[:, None, None] * carried + jnp.einsum('hs,shp,sn->hpn', to_end, inner_now, write_now, precision=HIGH)
        return (next_state, output)
    zero_state = jnp.zeros((num_heads, head_width, num_states), jnp.float32)
    end_state, outputs = lax.scan(advance, zero_state, (rate_blocks, dt_blocks, inner_blocks, write_blocks, read_blocks))
    mixed_out = outputs.reshape(num_rows, num_heads, head_width) + skip_gain[None, :, None] * inner
    gated_out = mixed_out.reshape(num_rows, num_heads * head_width) * jax.nn.silu(gate_in)
    return (gated_out, end_state, jnp.exp(-lax.optimization_barrier(jnp.sum(rate_all, axis=1))))

def sequence_grads(query_seq, key_seq, value_seq, gate_seq, write_seq, read_seq, raw_dt, a_log, skip_gain, dt_bias, cotangent):
    scale = HD ** (-0.5)
    group = QH // KVH
    heads_q = query_seq.reshape(LEN, QH, HD).transpose(1, 0, 2)
    heads_k = key_seq.reshape(LEN, KVH, HD).transpose(1, 0, 2)
    heads_v = value_seq.reshape(LEN, KVH, HD).transpose(1, 0, 2)
    position = jnp.arange(LEN)
    allowed = position[:, None] >= position[None, :]

    def head_scores(index):
        raw_scores = jnp.dot(heads_q[index], heads_k[index // group].T, preferred_element_type=jnp.float32) * scale
        return jnp.where(allowed, raw_scores, NEG_FILL)

    def forward_head(index):
        scores = head_scores(index)
        row_max = lax.optimization_barrier(jnp.max(scores, axis=1))
        exp_scores = jnp.exp(scores - row_max[:, None])
        row_total = lax.optimization_barrier(jnp.sum(exp_scores, axis=1))
        attn = jnp.dot(exp_scores.astype(jnp.bfloat16), heads_v[index // group], preferred_element_type=jnp.float32) / row_total[:, None]
        return (attn, row_max + jnp.log(row_total))
    attn, log_sum = lax.map(forward_head, jnp.arange(QH))
    inner = attn.transpose(1, 0, 2).reshape(LEN, MH, MP)
    primal_out, pullback = jax.vjp(block_scan, inner, gate_seq.astype(jnp.float32), write_seq.astype(jnp.float32), read_seq.astype(jnp.float32), raw_dt, a_log, skip_gain, dt_bias)
    zero_state = jnp.zeros((MH, MP, NS), jnp.float32)
    grads = pullback((cotangent.astype(jnp.float32), zero_state, jnp.zeros((MH,), jnp.float32)))
    grad_inner, grad_gate, grad_write, grad_read, grad_dt, grad_alog, grad_skip, grad_bias = grads
    grad_attn = grad_inner.reshape(LEN, QH, HD).transpose(1, 0, 2)
    delta = lax.optimization_barrier(jnp.sum(grad_attn * attn, axis=2))
    grad_low = grad_attn.astype(jnp.bfloat16)

    def backward_head(index):
        scores = head_scores(index)
        probs = jnp.exp(scores - log_sum[index][:, None])
        probs_low = probs.astype(jnp.bfloat16)
        key_one = heads_k[index // group]
        value_one = heads_v[index // group]
        grad_value = jnp.dot(probs_low.T, grad_low[index], preferred_element_type=jnp.float32)
        grad_probs = jnp.dot(grad_low[index], value_one.T, preferred_element_type=jnp.float32)
        grad_scores = (probs * (grad_probs - delta[index][:, None])).astype(jnp.bfloat16)
        grad_query = jnp.dot(grad_scores, key_one, preferred_element_type=jnp.float32) * scale
        grad_key = jnp.dot(grad_scores.T, heads_q[index], preferred_element_type=jnp.float32) * scale
        return (grad_query, grad_key, grad_value)
    grad_query, grad_key, grad_value = lax.map(backward_head, jnp.arange(QH))
    grad_query = grad_query.transpose(1, 0, 2).reshape(LEN, QH * HD)
    grad_key = grad_key.reshape(KVH, group, LEN, HD).sum(axis=1).transpose(1, 0, 2).reshape(LEN, KVH * HD)
    grad_value = grad_value.reshape(KVH, group, LEN, HD).sum(axis=1).transpose(1, 0, 2).reshape(LEN, KVH * HD)
    return (grad_query, grad_key, grad_value, grad_gate, grad_write, grad_read, grad_dt, grad_alog, grad_skip, grad_bias)

def reference(query_rows, key_rows, value_rows, gate_rows, write_vec, read_vec, dt_raw, a_log, skip_gain, dt_bias, out_grad):

    def one_sequence(pieces):
        query_seq, key_seq, value_seq, gate_seq, write_seq, read_seq, raw_dt, cotangent = pieces
        return sequence_grads(query_seq, key_seq, value_seq, gate_seq, write_seq, read_seq, raw_dt, a_log, skip_gain, dt_bias, cotangent)
    results = lax.map(one_sequence, (query_rows, key_rows, value_rows, gate_rows, write_vec, read_vec, dt_raw, out_grad))
    return (results[0], results[1], results[2], results[3], results[4], results[5], results[6], lax.optimization_barrier(jnp.sum(results[7], axis=0)), lax.optimization_barrier(jnp.sum(results[8], axis=0)), lax.optimization_barrier(jnp.sum(results[9], axis=0)))
```

```python
import functools

import jax
import jax.numpy as jnp
from jax import lax
from jax.experimental import pallas as pl
from jax.experimental.pallas import tpu as pltpu
from jax.sharding import PartitionSpec as P

HIGH = lax.Precision.HIGHEST
MESH = pl.DeviceIdType.MESH
F32 = jnp.float32
BF16 = jnp.bfloat16
NEG_FILL = -1e30


def mm(a, b, precision=None):
    return lax.dot_general(a, b, (((1,), (0,)), ((), ())), precision=precision, preferred_element_type=F32)


def mm_nt(a, b, precision=None):
    return lax.dot_general(a, b, (((1,), (1,)), ((), ())), precision=precision, preferred_element_type=F32)


def mm_tn(a, b, precision=None):
    return lax.dot_general(a, b, (((0,), (0,)), ((), ())), precision=precision, preferred_element_type=F32)


def kernel(
    dims,
    q_hbm, k_hbm, v_hbm, gate_hbm, write_hbm, read_hbm, dt_hbm, cot_hbm,
    alog_s, skip_s, bias_s,
    gq_hbm, gk_hbm, gv_hbm, gg_hbm, gw_hbm, gr_hbm, gdt_hbm, galog_s, gskip_s, gbias_s,
    q_v, k_v, v_v, gate_v, write_v, read_v, dt_v, cot_v,
    kv_buf, kf, vf, q_st, s_buf, m_buf, l_buf, acc, gl_st, delta_b,
    gy, dsc, ecx, w2x, dx, x_v, dtl_b, w_b, gym_b,
    cl_all, es_send, es_recv, es_out, ex_recv, fs_send, fs_recv, fs_out, fi_recv,
    kg_send, kg_recv, ps_send, ps_recv, ps_out, pp_all, pd_all, pf, pp_smem,
    gq_o, gk_o, gv_o, gg_o, gw_o, gr_o, gdt_o,
    in_sem, out_sem, kv_ss, kv_rs, cl_ss, cl_rs, es_ss, es_rs, ex_ss, ex_rs, fs_ss, fs_rs, fi_ss, fi_rs,
    kg_ss, kg_rs, p1_ss, p1_rs, p2_ss, p2_rs, pa_ss, pa_rs, pb_ss, pb_rs, sm_sem,
):
    nseq, ntp, ndp, nheads, nq = dims
    rows = 128
    s = lax.axis_index("seq")
    z = lax.axis_index("tp")
    x = lax.axis_index("dp")
    par = lax.rem(z, 2)
    base = z - par
    other = base + 1 - par
    chunk = lax.div(s, 2)
    scale = 128 ** (-0.5)

    def rcopy(src, dst, ssem, rsem, **where):
        return pltpu.make_async_remote_copy(
            src_ref=src, dst_ref=dst, send_sem=ssem, recv_sem=rsem, device_id=where, device_id_type=MESH
        )

    def seq_block(ref, i, n):
        return ref.at[pl.ds(pl.multiple_of(i * n, n), n)]

    loads = []
    for at, (src, dst) in enumerate((
        (k_hbm.at[0], k_v), (v_hbm.at[0], v_v), (dt_hbm.at[0], dt_v), (gate_hbm.at[0], gate_v),
        (cot_hbm.at[0], cot_v), (read_hbm.at[0], read_v), (write_hbm.at[0], write_v), (q_hbm.at[0], q_v),
    )):
        copy = pltpu.make_async_copy(src, dst, in_sem.at[at])
        copy.start()
        loads.append(copy)

    barrier = pltpu.get_barrier_semaphore()
    for d in range(1, nseq):
        to = lax.rem(s + d, nseq)
        pl.semaphore_signal(barrier, inc=1, device_id={"seq": to, "tp": z}, device_id_type=MESH)
        pl.semaphore_signal(barrier, inc=1, device_id={"seq": to, "tp": other}, device_id_type=MESH)
    for d in range(1, ntp):
        pl.semaphore_signal(barrier, inc=1, device_id={"tp": lax.rem(z + d, ntp)}, device_id_type=MESH)
    for d in range(1, ndp):
        pl.semaphore_signal(barrier, inc=1, device_id={"dp": lax.rem(x + d, ndp)}, device_id_type=MESH)

    loads[0].wait()
    loads[1].wait()
    own_rows = pl.ds(pl.multiple_of(s * rows, rows), rows)
    kv_buf[par, own_rows, :] = jnp.concatenate([k_v[...], v_v[...]], axis=1)

    @pl.when(lax.rem(s, 2) == 0)
    def _():
        blank = pl.ds(pl.multiple_of((s + 1) * rows, rows), rows)
        kv_buf[0, blank, :] = jnp.zeros((rows, 128), BF16)
        kv_buf[1, blank, :] = jnp.zeros((rows, 128), BF16)

    pl.semaphore_wait(barrier, 2 * (nseq - 1) + (ntp - 1) + (ndp - 1))

    def kv_copy(d, p, to_seq, to_tp):
        here = kv_buf.at[par, own_rows]
        return rcopy(here, here, kv_ss.at[d, p], kv_rs.at[par, s], seq=to_seq, tp=to_tp)

    kv_copy(0, 0, s, other).start()
    for d in range(1, nseq):
        @pl.when(s + d < nseq)
        def _(d=d):
            kv_copy(d, 0, s + d, base).start()
            kv_copy(d, 1, s + d, base + 1).start()

    row_i = lax.broadcasted_iota(jnp.int32, (rows, rows), 0)
    col_i = lax.broadcasted_iota(jnp.int32, (rows, rows), 1)
    causal = row_i >= col_i
    head_i = lax.broadcasted_iota(jnp.int32, (nheads, rows), 0)

    def head_rows(ref):
        out = jnp.zeros((nheads, rows), F32)
        for h in range(nheads):
            out = jnp.where(head_i == h, ref[h], out)
        return out

    wide = nheads * 64
    eb64 = jnp.where(
        lax.broadcasted_iota(jnp.int32, (nheads, wide), 1) // 64
        == lax.broadcasted_iota(jnp.int32, (nheads, wide), 0), 1.0, 0.0,
    ).astype(F32)
    eb128 = jnp.where(
        lax.broadcasted_iota(jnp.int32, (nheads, nheads * 128), 1) // 128
        == lax.broadcasted_iota(jnp.int32, (nheads, nheads * 128), 0), 1.0, 0.0,
    ).astype(F32)

    loads[2].wait()
    zdt = dt_v[...] + head_rows(bias_s)
    dt = jnp.maximum(zdt, 0.0) + jnp.log1p(jnp.exp(-jnp.abs(zdt)))
    sig_z = 1.0 / (1.0 + jnp.exp(-zdt))
    ea = jnp.exp(head_rows(alog_s))
    rate = dt * ea
    cum = mm(rate, jnp.where(row_i <= col_i, 1.0, 0.0).astype(F32), HIGH)
    cum_last = jnp.broadcast_to(cum[:, rows - 1:rows], (nheads, rows))
    cl_all[s] = cum_last

    def cl_copy(d, to):
        return rcopy(cl_all.at[s], cl_all.at[s], cl_ss.at[d], cl_rs.at[s], seq=to)

    for d in range(1, nseq):
        cl_copy(d, lax.rem(s + d, nseq)).start()

    ecum = jnp.exp(-cum)
    w2 = dt * jnp.exp(-(cum_last - cum))
    ecx[...] = mm_tn(ecum, eb64, HIGH)
    w2x[...] = mm_tn(w2, eb64, HIGH)
    cum_b = mm_tn(cum, eb128, HIGH)

    loads[3].wait()
    loads[4].wait()
    gate = gate_v[...].astype(F32)
    cot = cot_v[...].astype(F32)
    sig = 1.0 / (1.0 + jnp.exp(-gate))
    gy[...] = cot * gate * sig
    dsc[...] = cot * sig * (1.0 + gate * (1.0 - sig))
    loads[5].wait()
    gye = (gy[...] * ecx[...]).astype(BF16)
    es_send[...] = mm_tn(gye, read_v[...]).astype(BF16)

    def all_to_all(send, recv, ss, rs):
        def copy(d):
            to = lax.rem(s + d, nseq)
            return rcopy(seq_block(send, to, 64), recv.at[s], ss.at[d], rs.at[s], seq=to)
        for d in range(1, nseq):
            copy(d).start()
        recv[s] = send[pl.ds(pl.multiple_of(s * 64, 64), 64), :]
        return copy

    es_copy = all_to_all(es_send, es_recv, es_ss, es_rs)

    loads[6].wait()
    cb = mm_nt(read_v[...], write_v[...])
    lane_lo = lax.broadcasted_iota(jnp.int32, (rows, 128), 1) < 64
    skip_row = jnp.zeros((1, wide), F32)
    lane_head = lax.broadcasted_iota(jnp.int32, (1, wide), 1) // 64
    for h in range(nheads):
        skip_row = jnp.where(lane_head == h, skip_s[h], skip_row)
    for p in range(nheads // 2):
        lanes = slice(128 * p, 128 * p + 128)
        ws = []
        for c in range(2):
            h = 2 * p + c
            gap = cum_b[:, 128 * h:128 * h + 128] - cum[h:h + 1, :]
            dtl = jnp.where(causal, jnp.exp(-jnp.maximum(gap, 0.0)), 0.0) * dt[h:h + 1, :]
            dtl_b[p, 128 * c:128 * c + 128, :] = dtl
            ws.append((dtl * cb).astype(BF16))
        gp = gy[:, lanes]
        gym = jnp.concatenate([jnp.where(lane_lo, gp, 0.0), jnp.where(lane_lo, 0.0, gp)], axis=0).astype(BF16)
        gym_b[p] = gym
        w_b[p] = jnp.concatenate(ws, axis=1)
        dx[:, lanes] = mm_tn(jnp.concatenate(ws, axis=0), gym) + skip_row[:, lanes] * gp

    def wait_from(make, skip_self=True):
        for d in range(1, nseq):
            make(lax.rem(s + d, nseq)).wait_recv()

    wait_from(lambda j: rcopy(cl_all.at[j], cl_all.at[j], cl_ss.at[0], cl_rs.at[j], seq=j))
    wait_from(lambda j: rcopy(es_recv.at[j], es_recv.at[j], es_ss.at[0], es_rs.at[j], seq=j))

    def back_copy(out, recv, ss, rs, i):
        here = seq_block(recv, s, 64)
        return rcopy(out.at[i], here, ss.at[i], rs.at[s], seq=i)

    own_head = pl.ds(pl.multiple_of(s * 64, 64), 64)

    def send_back(out, recv, ss, rs, i):
        @pl.when(s != i)
        def _():
            back_copy(out, recv, ss, rs, i).start()

        @pl.when(s == i)
        def _():
            recv[own_head, :] = out[i]

    state = jnp.zeros((64, 128), F32)
    for i in reversed(range(nseq)):
        es_out[i] = state.astype(BF16)
        send_back(es_out, ex_recv, ex_ss, ex_rs, i)
        state = es_recv[i].astype(F32) + jnp.exp(-cl_all[i, pl.ds(s, 1), :]) * state

    loads[7].wait()
    for p in range(nq):
        q_st[128 * p:128 * p + 128, :] = q_v[:, 128 * p:128 * p + 128]
    m_buf[...] = jnp.full((nq * rows, 128), NEG_FILL, F32)
    l_buf[...] = jnp.zeros((nq * rows, 128), F32)
    acc[...] = jnp.zeros((nq * rows, 128), F32)

    def scores(i, carry):
        here = pl.ds(pl.multiple_of(i * 256, 256), 256)
        for c in range(2):
            j = 2 * i + c
            for p in range(2):
                @pl.when(jnp.logical_and(j <= s, jnp.logical_or(j != s, p != par)))
                def _(p=p, j=j):
                    slot = kv_buf.at[p, pl.ds(pl.multiple_of(j * rows, rows), rows)]
                    rcopy(slot, slot, kv_ss.at[0, 0], kv_rs.at[p, j], tp=other).wait_recv()
        kv0 = kv_buf[0, here, :]
        kv1 = kv_buf[1, here, :]
        kk = jnp.concatenate([kv0[:, :64], kv1[:, :64]], axis=1)
        kf[here, :] = kk
        vf[here, :] = jnp.concatenate([kv0[:, 64:], kv1[:, 64:]], axis=1)
        allowed = (
            i * 256 + lax.broadcasted_iota(jnp.int32, (rows, 256), 1)
            <= s * rows + lax.broadcasted_iota(jnp.int32, (rows, 256), 0)
        )
        for p in range(nq):
            r = slice(rows * p, rows * p + rows)
            sc = jnp.where(allowed, mm_nt(q_st[r, :], kk) * scale, NEG_FILL)
            s_buf[i, r, :] = sc
            m_buf[r, :] = jnp.maximum(m_buf[r, :], jnp.maximum(sc[:, :128], sc[:, 128:]))
        return carry

    lax.fori_loop(0, chunk + 1, scores, 0)
    m_buf[...] = jnp.broadcast_to(jnp.max(m_buf[...], axis=1, keepdims=True), (nq * rows, 128))

    def weights(i, carry):
        here = pl.ds(pl.multiple_of(i * 256, 256), 256)
        vv = vf[here, :]
        for p in range(nq):
            r = slice(rows * p, rows * p + rows)
            m = m_buf[r, :]
            e = jnp.exp(s_buf[i, r, :] - jnp.concatenate([m, m], axis=1))
            s_buf[i, r, :] = e
            l_buf[r, :] += e[:, :128] + e[:, 128:]
            acc[r, :] += mm(e.astype(BF16), vv)
        return carry

    lax.fori_loop(0, chunk + 1, weights, 0)
    total = jnp.sum(l_buf[...], axis=1, keepdims=True)
    inv = jnp.broadcast_to(1.0 / total, (nq * rows, 128))
    l_buf[...] = inv
    acc[...] = acc[...] * inv
    for p in range(nq):
        x_v[:, 128 * p:128 * p + 128] = acc[128 * p:128 * p + 128, :]

    xw = (x_v[...] * w2x[...]).astype(BF16)
    fs_send[...] = mm_tn(xw, write_v[...]).astype(BF16)
    fs_copy = all_to_all(fs_send, fs_recv, fs_ss, fs_rs)

    m_sum = jnp.zeros((rows, rows), F32)
    col_r = jnp.zeros((nheads, rows), F32)
    row_r = jnp.zeros((nheads, rows), F32)
    ones8 = jnp.ones((8, 128), F32)
    for p in range(nheads // 2):
        lanes = slice(128 * p, 128 * p + 128)
        xp = x_v[:, lanes]
        g = mm_nt(gym_b[p], xp.astype(BF16))
        mp = dtl_b[p] * g
        m_sum = m_sum + mp[:rows] + mp[rows:]
        r0 = mp[:rows] * cb
        r1 = mp[rows:] * cb
        rs = mm_nt(ones8, jnp.concatenate([r0, r1], axis=0), HIGH)
        col_r = jnp.where(head_i == 2 * p, jnp.sum(r0, axis=0, keepdims=True), col_r)
        col_r = jnp.where(head_i == 2 * p + 1, jnp.sum(r1, axis=0, keepdims=True), col_r)
        row_r = jnp.where(head_i == 2 * p, rs[0:1, :rows], row_r)
        row_r = jnp.where(head_i == 2 * p + 1, rs[0:1, rows:], row_r)

    wait_from(lambda j: rcopy(seq_block(ex_recv, j, 64), seq_block(ex_recv, j, 64), ex_ss.at[0], ex_rs.at[j], seq=j))
    exit_g = ex_recv[...]
    dx_exit = mm_nt(write_v[...], exit_g) * w2x[...]
    r_s = mm_nt(eb64, x_v[...] * dx_exit, HIGH)
    gyx = mm_nt(eb64, x_v[...] * gy[...], HIGH)
    dx[...] = dx[...] + dx_exit
    grad_w = mm_tn(m_sum.astype(BF16), read_v[...]) + mm(xw, exit_g)
    ps_send[:rows, :] = grad_w.astype(BF16)

    wait_from(lambda j: rcopy(fs_recv.at[j], fs_recv.at[j], fs_ss.at[0], fs_rs.at[j], seq=j))
    state = jnp.zeros((64, 128), F32)
    for i in range(nseq):
        fs_out[i] = state.astype(BF16)
        send_back(fs_out, fi_recv, fi_ss, fi_rs, i)
        state = fs_recv[i].astype(F32) + jnp.exp(-cl_all[i, pl.ds(s, 1), :]) * state

    for p in range(nq):
        r = slice(rows * p, rows * p + rows)
        ga = dx[:, 128 * p:128 * p + 128]
        gl_st[r, :] = ga.astype(BF16)
        delta_b[r, :] = jnp.broadcast_to(
            jnp.sum(ga * x_v[:, 128 * p:128 * p + 128], axis=1, keepdims=True), (rows, 128)
        )
    acc[...] = jnp.zeros((nq * rows, 128), F32)

    def kg_copy(p, j):
        return rcopy(
            kg_send.at[p, pl.ds(pl.multiple_of(j * rows, rows), rows)], kg_recv.at[par, s],
            kg_ss.at[p, j], kg_rs.at[par, s], seq=j, tp=base + p,
        )

    def kg_mine(p, j):
        return jnp.logical_and(j == s, p == par)

    def backward(i, carry):
        here = pl.ds(pl.multiple_of(i * 256, 256), 256)
        kk = kf[here, :]
        vv = vf[here, :]
        gk = jnp.zeros((256, 128), F32)
        gv = jnp.zeros((256, 128), F32)
        for p in range(nq):
            r = slice(rows * p, rows * p + rows)
            iv = l_buf[r, :]
            de = delta_b[r, :]
            pr = s_buf[i, r, :] * jnp.concatenate([iv, iv], axis=1)
            gl = gl_st[r, :]
            ds = (pr * (mm_nt(gl, vv) - jnp.concatenate([de, de], axis=1))).astype(BF16)
            acc[r, :] += mm(ds, kk)
            gv = gv + mm_tn(pr.astype(BF16), gl)
            gk = gk + mm_tn(ds, q_st[r, :])
        gk = gk * scale
        kg_send[0, here, :] = jnp.concatenate([gk[:, :64], gv[:, :64]], axis=1).astype(BF16)
        kg_send[1, here, :] = jnp.concatenate([gk[:, 64:], gv[:, 64:]], axis=1).astype(BF16)
        for c in range(2):
            j = 2 * i + c
            for p in range(2):
                @pl.when(jnp.logical_and(j <= s, jnp.logical_not(kg_mine(p, j))))
                def _(p=p, j=j):
                    kg_copy(p, j).start()
        return carry

    lax.fori_loop(0, chunk + 1, backward, 0)
    kg_recv[par, s] = kg_send[par, own_rows, :]
    for p in range(nq):
        gq_o[:, 128 * p:128 * p + 128] = acc[128 * p:128 * p + 128, :] * scale
    outs = []

    def put(src, dst):
        copy = pltpu.make_async_copy(src, dst, out_sem.at[len(outs)])
        copy.start()
        outs.append(copy)

    put(gq_o, gq_hbm.at[0])

    wait_from(lambda j: rcopy(seq_block(fi_recv, j, 64), seq_block(fi_recv, j, 64), fi_ss.at[0], fi_rs.at[j], seq=j))
    entry = fi_recv[...]
    gye = (gy[...] * ecx[...]).astype(BF16)
    grad_r = mm(m_sum.astype(BF16), write_v[...]) + mm(gye, entry)
    ps_send[rows:, :] = grad_r.astype(BF16)
    part = 2 * rows // ntp

    def p1_copy(d):
        to = lax.rem(z + d, ntp)
        return rcopy(seq_block(ps_send, to, part), ps_recv.at[z], p1_ss.at[d], p1_rs.at[z], tp=to)

    for d in range(1, ntp):
        p1_copy(d).start()
    own_part = pl.ds(pl.multiple_of(z * part, part), part)
    ps_recv[z] = ps_send[own_part, :]

    y_ent = mm_nt(read_v[...], entry) * ecx[...]
    q_t = mm_nt(eb64, gy[...] * y_ent, HIGH)
    for p in range(nheads // 2):
        lanes = slice(128 * p, 128 * p + 128)
        xp = x_v[:, lanes]
        xm = jnp.concatenate([jnp.where(lane_lo, xp, 0.0), jnp.where(lane_lo, 0.0, xp)], axis=0).astype(BF16)
        y = mm(w_b[p], xm) + y_ent[:, lanes] + skip_row[:, lanes] * xp
        gg_o[:, lanes] = dsc[:, lanes] * y
    put(gg_o, gg_hbm.at[0])

    es_prod = exit_g.astype(F32) * entry.astype(F32)
    c_h = jnp.sum(mm(eb64, es_prod, HIGH), axis=1, keepdims=True) * jnp.exp(-cum_last)
    tail = jnp.where(row_i >= col_i, 1.0, 0.0).astype(F32)
    before = jnp.where(row_i < col_i, 1.0, 0.0).astype(F32)
    drate = mm(col_r - row_r - q_t, tail, HIGH) - mm(r_s, before, HIGH) - c_h
    ddt = (col_r + r_s) / dt + drate * ea
    draw = ddt * sig_z
    gdt_o[...] = draw
    put(gdt_o, gdt_hbm.at[0])

    lane8 = lax.broadcasted_iota(jnp.int32, (nheads, 128), 1)
    pp_all[s] = jnp.where(
        lane8 == 0, jnp.sum(drate * rate, axis=1, keepdims=True),
        jnp.where(
            lane8 == 1, jnp.sum(gyx, axis=1, keepdims=True),
            jnp.where(lane8 == 2, jnp.sum(draw, axis=1, keepdims=True), 0.0),
        ),
    )

    def pa_copy(d):
        return rcopy(pp_all.at[s], pp_all.at[s], pa_ss.at[d], pa_rs.at[s], seq=lax.rem(s + d, nseq))

    for d in range(1, nseq):
        pa_copy(d).start()

    for d in range(1, ntp):
        j = lax.rem(z + d, ntp)
        rcopy(ps_recv.at[j], ps_recv.at[j], p1_ss.at[0], p1_rs.at[j], tp=j).wait_recv()
    red = ps_recv[0].astype(F32)
    for j in range(1, ntp):
        red = red + ps_recv[j].astype(F32)
    ps_out[own_part, :] = red.astype(BF16)

    def p2_copy(d):
        here = seq_block(ps_out, z, part)
        return rcopy(here, here, p2_ss.at[d], p2_rs.at[z], tp=lax.rem(z + d, ntp))

    for d in range(1, ntp):
        p2_copy(d).start()

    wait_from(lambda j: rcopy(pp_all.at[j], pp_all.at[j], pa_ss.at[0], pa_rs.at[j], seq=j))
    pd = pp_all[0]
    for j in range(1, nseq):
        pd = pd + pp_all[j]
    pd_all[x] = pd

    def pb_copy(d):
        return rcopy(pd_all.at[x], pd_all.at[x], pb_ss.at[d], pb_rs.at[x], dp=lax.rem(x + d, ndp))

    for d in range(1, ndp):
        pb_copy(d).start()

    def kg_add(j, total):
        for p in range(2):
            @pl.when(jnp.logical_not(kg_mine(p, j)))
            def _(p=p):
                rcopy(kg_recv.at[p, j], kg_recv.at[p, j], kg_ss.at[0, 0], kg_rs.at[p, j], tp=other).wait_recv()
        return total + kg_recv[0, j].astype(F32) + kg_recv[1, j].astype(F32)

    kg = lax.fori_loop(s, nseq, kg_add, jnp.zeros((rows, 128), F32))
    gk_o[...] = kg[:, :64]
    gv_o[...] = kg[:, 64:]
    put(gk_o, gk_hbm.at[0])
    put(gv_o, gv_hbm.at[0])

    for d in range(1, ndp):
        j = lax.rem(x + d, ndp)
        rcopy(pd_all.at[j], pd_all.at[j], pb_ss.at[0], pb_rs.at[j], dp=j).wait_recv()
    pd = pd_all[0]
    for j in range(1, ndp):
        pd = pd + pd_all[j]
    pf[...] = pd
    to_smem = pltpu.make_async_copy(pf, pp_smem, sm_sem)
    to_smem.start()

    for d in range(1, ntp):
        j = lax.rem(z + d, ntp)
        there = seq_block(ps_out, j, part)
        rcopy(there, there, p2_ss.at[0], p2_rs.at[j], tp=j).wait_recv()
    gw_o[...] = ps_out[:rows, :].astype(F32)
    gr_o[...] = ps_out[rows:, :].astype(F32)
    put(gw_o, gw_hbm.at[0])
    put(gr_o, gr_hbm.at[0])

    to_smem.wait()
    for h in range(nheads):
        galog_s[h] = pp_smem[h, 0]
        gskip_s[h] = pp_smem[h, 1]
        gbias_s[h] = pp_smem[h, 2]

    kv_copy(0, 0, s, other).wait_send()
    for d in range(1, nseq):
        @pl.when(s + d < nseq)
        def _(d=d):
            kv_copy(d, 0, s + d, base).wait_send()
            kv_copy(d, 1, s + d, base + 1).wait_send()
        cl_copy(d, lax.rem(s + d, nseq)).wait_send()
        es_copy(d).wait_send()
        fs_copy(d).wait_send()
        pa_copy(d).wait_send()
    for i in range(nseq):
        @pl.when(s != i)
        def _(i=i):
            back_copy(es_out, ex_recv, ex_ss, ex_rs, i).wait_send()
            back_copy(fs_out, fi_recv, fi_ss, fi_rs, i).wait_send()
        for p in range(2):
            @pl.when(jnp.logical_and(i <= s, jnp.logical_not(kg_mine(p, i))))
            def _(p=p, i=i):
                kg_copy(p, i).wait_send()
    for d in range(1, ntp):
        p1_copy(d).wait_send()
        p2_copy(d).wait_send()
    for d in range(1, ndp):
        pb_copy(d).wait_send()
    for copy in outs:
        copy.wait()


def body(
    dims, query_rows, key_rows, value_rows, gate_rows, write_vec, read_vec, dt_raw, a_log, skip_gain, dt_bias, out_grad
):
    nseq, ntp, ndp, nheads, nq = dims
    rows = 128
    wide = nheads * 64
    dma = pltpu.SemaphoreType.DMA

    def vm(shape, kind=F32):
        return pltpu.VMEM(shape, kind)

    any_spec = pl.BlockSpec(memory_space=pl.ANY)
    smem_spec = pl.BlockSpec(memory_space=pltpu.SMEM)
    outs = (
        (1, rows, wide), (1, rows, 64), (1, rows, 64), (1, rows, wide), (1, rows, 128), (1, rows, 128),
        (1, nheads, rows), (nheads,), (nheads,), (nheads,),
    )
    tall = nq * rows
    scratch = [
        vm((rows, wide), BF16), vm((rows, 64), BF16), vm((rows, 64), BF16), vm((rows, wide), BF16),
        vm((rows, 128), BF16), vm((rows, 128), BF16), vm((nheads, rows)), vm((rows, wide), BF16),
        vm((2, nseq * rows, 128), BF16), vm((nseq * rows, 128), BF16), vm((nseq * rows, 128), BF16),
        vm((tall, 128), BF16), vm((nseq // 2, tall, 256)), vm((tall, 128)), vm((tall, 128)), vm((tall, 128)),
        vm((tall, 128), BF16), vm((tall, 128)),
        vm((rows, wide)), vm((rows, wide)), vm((rows, wide)), vm((rows, wide)), vm((rows, wide)), vm((rows, wide)),
        vm((nheads // 2, 2 * rows, rows)), vm((nheads // 2, rows, 2 * rows), BF16),
        vm((nheads // 2, 2 * rows, 128), BF16),
        vm((nseq, nheads, 128)),
        vm((wide, 128), BF16), vm((nseq, 64, 128), BF16), vm((nseq, 64, 128), BF16), vm((wide, 128), BF16),
        vm((wide, 128), BF16), vm((nseq, 64, 128), BF16), vm((nseq, 64, 128), BF16), vm((wide, 128), BF16),
        vm((2, nseq * rows, 128), BF16), vm((2, nseq, rows, 128), BF16),
        vm((2 * rows, 128), BF16), vm((ntp, 2 * rows // ntp, 128), BF16), vm((2 * rows, 128), BF16),
        vm((nseq, nheads, 128)), vm((ndp, nheads, 128)), vm((nheads, 128)), pltpu.SMEM((nheads, 128), F32),
        vm((rows, wide)), vm((rows, 64)), vm((rows, 64)), vm((rows, wide)), vm((rows, 128)), vm((rows, 128)),
        vm((nheads, rows)),
        dma((8,)), dma((7,)), dma((nseq, 2)), dma((2, nseq)), dma((nseq,)), dma((nseq,)),
        dma((nseq,)), dma((nseq,)), dma((nseq,)), dma((nseq,)),
        dma((nseq,)), dma((nseq,)), dma((nseq,)), dma((nseq,)),
        dma((2, nseq)), dma((2, nseq)), dma((ntp,)), dma((ntp,)), dma((ntp,)), dma((ntp,)),
        dma((nseq,)), dma((nseq,)), dma((ndp,)), dma((ndp,)), dma(()),
    ]
    return pl.pallas_call(
        functools.partial(kernel, dims),
        out_shape=tuple(jax.ShapeDtypeStruct(o, F32) for o in outs),
        in_specs=[any_spec] * 8 + [smem_spec] * 3,
        out_specs=tuple([any_spec] * 7 + [smem_spec] * 3),
        scratch_shapes=scratch,
        compiler_params=pltpu.CompilerParams(
            collective_id=0, has_side_effects=True, vmem_limit_bytes=48 * 1024 * 1024
        ),
    )(query_rows, key_rows, value_rows, gate_rows, write_vec, read_vec, dt_raw, out_grad, a_log, skip_gain, dt_bias)


def solution(mesh):
    dims = (mesh.shape["seq"], mesh.shape["tp"], mesh.shape["dp"], 8, 4)
    wide = P("dp", "seq", "tp")
    shared = P("dp", "seq", None)
    steps = P("dp", "tp", "seq")
    head = P("tp")
    return jax.shard_map(
        functools.partial(body, dims),
        mesh=mesh,
        in_specs=(wide, wide, wide, wide, shared, shared, steps, head, head, head, wide),
        out_specs=(wide, wide, wide, wide, shared, shared, steps, head, head, head),
        check_vma=False,
    )
```

```python
import functools

import jax
import jax.numpy as jnp
from jax import lax
from jax.experimental import pallas as pl
from jax.experimental.pallas import tpu as pltpu
from jax.sharding import PartitionSpec as P

HIGH = lax.Precision.HIGHEST
MESH = pl.DeviceIdType.MESH
F32 = jnp.float32
BF16 = jnp.bfloat16
NEG_FILL = -1e30
VMEM = 60 * 1024 * 1024


def mm(a, b, precision=None):
    return lax.dot_general(a, b, (((1,), (0,)), ((), ())), precision=precision, preferred_element_type=F32)


def mm_nt(a, b, precision=None):
    return lax.dot_general(a, b, (((1,), (1,)), ((), ())), precision=precision, preferred_element_type=F32)


def mm_tn(a, b, precision=None):
    return lax.dot_general(a, b, (((0,), (0,)), ((), ())), precision=precision, preferred_element_type=F32)


def kernel(
    dims,
    q_hbm, k_hbm, v_hbm, gate_hbm, write_hbm, read_hbm, dt_hbm, cot_hbm,
    alog_s, skip_s, bias_s,
    gq_hbm, gk_hbm, gv_hbm, gg_hbm, gw_hbm, gr_hbm, gdt_hbm, pf_hbm,
    q_v, k_v, v_v, gate_v, write_v, read_v, dt_v, cot_v,
    kv_buf, kf, vf, q_st, q_t, s_buf, m_buf, l_buf, acc, gl_st, gl_t, delta_b,
    gy, dsc, ecx, w2x, dx, x_v, dtl_b, w_b, gym_b,
    cl_all, es_send, es_recv, es_out, ex_recv, fs_send, fs_recv, fs_out, fi_recv,
    kg_send, kg_recv, ps_send, ps_recv, ps_out, pp_all, pd_all,
    gq_o, gk_o, gv_o, gg_o, gw_o, gr_o, gdt_o, pf,
    in_sem, out_sem, kv_ss, kv_rs, cl_ss, cl_rs, es_ss, es_rs, ex_ss, ex_rs, fs_ss, fs_rs, fi_ss, fi_rs,
    kg_ss, kg_rs, p1_ss, p1_rs, p2_ss, p2_rs, pa_ss, pa_rs, pb_ss, pb_rs,
):
    nseq, ntp, ndp, nheads, nq = dims
    rows = 128
    s = lax.axis_index("seq")
    z = lax.axis_index("tp")
    x = lax.axis_index("dp")
    par = lax.rem(z, 2)
    base = z - par
    other = base + 1 - par
    chunk = lax.div(s, 2)
    scale = 128 ** (-0.5)

    def rcopy(src, dst, ssem, rsem, **where):
        return pltpu.make_async_remote_copy(
            src_ref=src, dst_ref=dst, send_sem=ssem, recv_sem=rsem, device_id=where, device_id_type=MESH
        )

    def seq_block(ref, i, n):
        return ref.at[pl.ds(pl.multiple_of(i * n, n), n)]

    outs = []

    def put(src, dst):
        copy = pltpu.make_async_copy(src, dst, out_sem.at[len(outs)])
        copy.start()
        outs.append(copy)

    loads = []
    for at, (src, dst) in enumerate((
        (k_hbm.at[0], k_v), (v_hbm.at[0], v_v), (dt_hbm.at[0], dt_v), (gate_hbm.at[0], gate_v),
        (cot_hbm.at[0], cot_v), (read_hbm.at[0], read_v), (write_hbm.at[0], write_v), (q_hbm.at[0], q_v),
    )):
        copy = pltpu.make_async_copy(src, dst, in_sem.at[at])
        copy.start()
        loads.append(copy)

    barrier = pltpu.get_barrier_semaphore()
    for d in range(1, nseq):
        to = lax.rem(s + d, nseq)
        pl.semaphore_signal(barrier, inc=1, device_id={"seq": to, "tp": z}, device_id_type=MESH)
        pl.semaphore_signal(barrier, inc=1, device_id={"seq": to, "tp": other}, device_id_type=MESH)
    for d in range(1, ntp):
        pl.semaphore_signal(barrier, inc=1, device_id={"tp": lax.rem(z + d, ntp)}, device_id_type=MESH)
    for d in range(1, ndp):
        pl.semaphore_signal(barrier, inc=1, device_id={"dp": lax.rem(x + d, ndp)}, device_id_type=MESH)

    loads[0].wait()
    loads[1].wait()
    kv_buf[par, s] = jnp.concatenate([k_v[...], v_v[...]], axis=0)

    @pl.when(lax.rem(s, 2) == 0)
    def _():
        kv_buf[0, s + 1] = jnp.zeros((rows, 128), BF16)
        kv_buf[1, s + 1] = jnp.zeros((rows, 128), BF16)

    pl.semaphore_wait(barrier, 2 * (nseq - 1) + (ntp - 1) + (ndp - 1))

    def kv_copy(d, p, to_seq, to_tp):
        here = kv_buf.at[par, s]
        return rcopy(here, here, kv_ss.at[d, p], kv_rs.at[par, s], seq=to_seq, tp=to_tp)

    kv_copy(0, 0, s, other).start()
    for d in range(1, nseq):
        @pl.when(s + d < nseq)
        def _(d=d):
            kv_copy(d, 0, s + d, base).start()
            kv_copy(d, 1, s + d, base + 1).start()

    row_i = lax.broadcasted_iota(jnp.int32, (rows, rows), 0)
    col_i = lax.broadcasted_iota(jnp.int32, (rows, rows), 1)
    causal = row_i >= col_i
    head_i = lax.broadcasted_iota(jnp.int32, (nheads, rows), 0)

    def head_rows(ref):
        out = jnp.zeros((nheads, rows), F32)
        for h in range(nheads):
            out = jnp.where(head_i == h, ref[h], out)
        return out

    wide = nheads * 64
    eb64 = jnp.where(
        lax.broadcasted_iota(jnp.int32, (nheads, wide), 1) // 64
        == lax.broadcasted_iota(jnp.int32, (nheads, wide), 0), 1.0, 0.0,
    ).astype(F32)
    eb128 = jnp.where(
        lax.broadcasted_iota(jnp.int32, (nheads, nheads * 128), 1) // 128
        == lax.broadcasted_iota(jnp.int32, (nheads, nheads * 128), 0), 1.0, 0.0,
    ).astype(F32)

    loads[2].wait()
    zdt = dt_v[...] + head_rows(bias_s)
    dt = jnp.maximum(zdt, 0.0) + jnp.log1p(jnp.exp(-jnp.abs(zdt)))
    sig_z = 1.0 / (1.0 + jnp.exp(-zdt))
    ea = jnp.exp(head_rows(alog_s))
    rate = dt * ea
    cum = mm(rate, jnp.where(row_i <= col_i, 1.0, 0.0).astype(F32), HIGH)
    cum_last = jnp.broadcast_to(cum[:, rows - 1:rows], (nheads, rows))
    cl_all[s] = cum_last

    def cl_copy(d, to):
        return rcopy(cl_all.at[s], cl_all.at[s], cl_ss.at[d], cl_rs.at[s], seq=to)

    for d in range(1, nseq):
        cl_copy(d, lax.rem(s + d, nseq)).start()

    ecum = jnp.exp(-cum)
    w2 = dt * jnp.exp(-(cum_last - cum))
    ecx[...] = mm_tn(ecum, eb64, HIGH)
    w2x[...] = mm_tn(w2, eb64, HIGH)
    cum_b = mm_tn(cum, eb128, HIGH)

    loads[3].wait()
    loads[4].wait()
    gate = gate_v[...].astype(F32)
    cot = cot_v[...].astype(F32)
    sig = 1.0 / (1.0 + jnp.exp(-gate))
    gy[...] = cot * gate * sig
    dsc[...] = cot * sig * (1.0 + gate * (1.0 - sig))
    loads[5].wait()
    gye = (gy[...] * ecx[...]).astype(BF16)
    es_send[...] = mm_tn(gye, read_v[...]).astype(BF16)

    def all_to_all(send, recv, ss, rs):
        def copy(d):
            to = lax.rem(s + d, nseq)
            return rcopy(seq_block(send, to, 64), recv.at[s], ss.at[d], rs.at[s], seq=to)
        for d in range(1, nseq):
            copy(d).start()
        recv[s] = send[pl.ds(pl.multiple_of(s * 64, 64), 64), :]
        return copy

    es_copy = all_to_all(es_send, es_recv, es_ss, es_rs)

    loads[6].wait()
    cb = mm_nt(read_v[...], write_v[...])
    lane_lo = lax.broadcasted_iota(jnp.int32, (rows, 128), 1) < 64
    skip_row = jnp.zeros((1, wide), F32)
    lane_head = lax.broadcasted_iota(jnp.int32, (1, wide), 1) // 64
    for h in range(nheads):
        skip_row = jnp.where(lane_head == h, skip_s[h], skip_row)
    for p in range(nheads // 2):
        lanes = slice(128 * p, 128 * p + 128)
        ws = []
        for c in range(2):
            h = 2 * p + c
            gap = cum_b[:, 128 * h:128 * h + 128] - cum[h:h + 1, :]
            dtl = jnp.where(causal, jnp.exp(-jnp.maximum(gap, 0.0)), 0.0) * dt[h:h + 1, :]
            dtl_b[p, 128 * c:128 * c + 128, :] = dtl
            ws.append((dtl * cb).astype(BF16))
        gp = gy[:, lanes]
        gym = jnp.concatenate([jnp.where(lane_lo, gp, 0.0), jnp.where(lane_lo, 0.0, gp)], axis=0).astype(BF16)
        gym_b[p] = gym
        w_b[p] = jnp.concatenate(ws, axis=1)
        dx[:, lanes] = mm_tn(jnp.concatenate(ws, axis=0), gym) + skip_row[:, lanes] * gp

    def wait_from(make, skip_self=True):
        for d in range(1, nseq):
            make(lax.rem(s + d, nseq)).wait_recv()

    wait_from(lambda j: rcopy(cl_all.at[j], cl_all.at[j], cl_ss.at[0], cl_rs.at[j], seq=j))
    wait_from(lambda j: rcopy(es_recv.at[j], es_recv.at[j], es_ss.at[0], es_rs.at[j], seq=j))

    def back_copy(out, recv, ss, rs, i):
        here = seq_block(recv, s, 64)
        return rcopy(out.at[i], here, ss.at[i], rs.at[s], seq=i)

    own_head = pl.ds(pl.multiple_of(s * 64, 64), 64)

    def send_back(out, recv, ss, rs, i):
        @pl.when(s != i)
        def _():
            back_copy(out, recv, ss, rs, i).start()

        @pl.when(s == i)
        def _():
            recv[own_head, :] = out[i]

    state = jnp.zeros((64, 128), F32)
    for i in reversed(range(nseq)):
        es_out[i] = state.astype(BF16)
        send_back(es_out, ex_recv, ex_ss, ex_rs, i)
        state = es_recv[i].astype(F32) + jnp.exp(-cl_all[i, pl.ds(s, 1), :]) * state

    loads[7].wait()
    for p in range(nq):
        q_st[128 * p:128 * p + 128, :] = q_v[:, 128 * p:128 * p + 128]
        q_t[:, 128 * p:128 * p + 128] = q_v[:, 128 * p:128 * p + 128].T
    m_buf[...] = jnp.full((nq * rows, 128), NEG_FILL, F32)
    l_buf[...] = jnp.zeros((nq * rows, 128), F32)
    acc[...] = jnp.zeros((nq * rows, 128), F32)

    def scores(i, carry):
        for c in range(2):
            j = 2 * i + c
            for p in range(2):
                @pl.when(jnp.logical_and(j <= s, jnp.logical_or(j != s, p != par)))
                def _(p=p, j=j):
                    slot = kv_buf.at[p, j]
                    rcopy(slot, slot, kv_ss.at[0, 0], kv_rs.at[p, j], tp=other).wait_recv()
        lo = jnp.concatenate([kv_buf[0, 2 * i], kv_buf[0, 2 * i + 1]], axis=1)
        hi = jnp.concatenate([kv_buf[1, 2 * i], kv_buf[1, 2 * i + 1]], axis=1)
        kk = jnp.concatenate([lo[:64], hi[:64]], axis=0)
        kf[i] = kk
        vf[i] = jnp.concatenate([lo[64:], hi[64:]], axis=0)
        allowed = (
            i * 256 + lax.broadcasted_iota(jnp.int32, (rows, 256), 1)
            <= s * rows + lax.broadcasted_iota(jnp.int32, (rows, 256), 0)
        )
        for p in range(nq):
            r = slice(rows * p, rows * p + rows)
            sc = jnp.where(allowed, mm(q_st[r, :], kk) * scale, NEG_FILL)
            s_buf[i, r, :] = sc
            m_buf[r, :] = jnp.maximum(m_buf[r, :], jnp.maximum(sc[:, :128], sc[:, 128:]))
        return carry

    lax.fori_loop(0, chunk + 1, scores, 0)
    m_buf[...] = jnp.broadcast_to(jnp.max(m_buf[...], axis=1, keepdims=True), (nq * rows, 128))

    def weights(i, carry):
        vv = vf[i]
        for p in range(nq):
            r = slice(rows * p, rows * p + rows)
            m = m_buf[r, :]
            e = jnp.exp(s_buf[i, r, :] - jnp.concatenate([m, m], axis=1))
            s_buf[i, r, :] = e
            l_buf[r, :] += e[:, :128] + e[:, 128:]
            acc[r, :] += mm_nt(e.astype(BF16), vv)
        return carry

    lax.fori_loop(0, chunk + 1, weights, 0)
    total = jnp.sum(l_buf[...], axis=1, keepdims=True)
    inv = jnp.broadcast_to(1.0 / total, (nq * rows, 128))
    l_buf[...] = inv
    acc[...] = acc[...] * inv
    for p in range(nq):
        x_v[:, 128 * p:128 * p + 128] = acc[128 * p:128 * p + 128, :]

    xw = (x_v[...] * w2x[...]).astype(BF16)
    fs_send[...] = mm_tn(xw, write_v[...]).astype(BF16)
    fs_copy = all_to_all(fs_send, fs_recv, fs_ss, fs_rs)

    m_sum = jnp.zeros((rows, rows), F32)
    col_r = jnp.zeros((nheads, rows), F32)
    row_r = jnp.zeros((nheads, rows), F32)
    ones8 = jnp.ones((8, 128), F32)
    for p in range(nheads // 2):
        lanes = slice(128 * p, 128 * p + 128)
        xp = x_v[:, lanes]
        g = mm_nt(gym_b[p], xp.astype(BF16))
        mp = dtl_b[p] * g
        m_sum = m_sum + mp[:rows] + mp[rows:]
        r0 = mp[:rows] * cb
        r1 = mp[rows:] * cb
        rs = mm_nt(ones8, jnp.concatenate([r0, r1], axis=0), HIGH)
        col_r = jnp.where(head_i == 2 * p, jnp.sum(r0, axis=0, keepdims=True), col_r)
        col_r = jnp.where(head_i == 2 * p + 1, jnp.sum(r1, axis=0, keepdims=True), col_r)
        row_r = jnp.where(head_i == 2 * p, rs[0:1, :rows], row_r)
        row_r = jnp.where(head_i == 2 * p + 1, rs[0:1, rows:], row_r)

    wait_from(lambda j: rcopy(seq_block(ex_recv, j, 64), seq_block(ex_recv, j, 64), ex_ss.at[0], ex_rs.at[j], seq=j))
    exit_g = ex_recv[...]
    dx_exit = mm_nt(write_v[...], exit_g) * w2x[...]
    r_s = mm_nt(eb64, x_v[...] * dx_exit, HIGH)
    gyx = mm_nt(eb64, x_v[...] * gy[...], HIGH)
    dx[...] = dx[...] + dx_exit
    grad_w = mm_tn(m_sum.astype(BF16), read_v[...]) + mm(xw, exit_g)
    ps_send[:rows, :] = grad_w.astype(BF16)

    wait_from(lambda j: rcopy(fs_recv.at[j], fs_recv.at[j], fs_ss.at[0], fs_rs.at[j], seq=j))
    state = jnp.zeros((64, 128), F32)
    for i in range(nseq):
        fs_out[i] = state.astype(BF16)
        send_back(fs_out, fi_recv, fi_ss, fi_rs, i)
        state = fs_recv[i].astype(F32) + jnp.exp(-cl_all[i, pl.ds(s, 1), :]) * state

    for p in range(nq):
        r = slice(rows * p, rows * p + rows)
        ga = dx[:, 128 * p:128 * p + 128]
        gl_st[r, :] = ga.astype(BF16)
        gl_t[:, r] = ga.astype(BF16).T
        delta_b[r, :] = jnp.broadcast_to(
            jnp.sum(ga * x_v[:, 128 * p:128 * p + 128], axis=1, keepdims=True), (rows, 128)
        )
    acc[...] = jnp.zeros((nq * rows, 128), F32)

    def kg_copy(p, j):
        return rcopy(
            kg_send.at[p, j], kg_recv.at[par, s],
            kg_ss.at[p, j], kg_rs.at[par, s], seq=j, tp=base + p,
        )

    def kg_mine(p, j):
        return jnp.logical_and(j == s, p == par)

    def backward(i, carry):
        kk = kf[i]
        vv = vf[i]
        gk = jnp.zeros((128, 256), F32)
        gv = jnp.zeros((128, 256), F32)
        for p in range(nq):
            r = slice(rows * p, rows * p + rows)
            iv = l_buf[r, :]
            de = delta_b[r, :]
            pr = s_buf[i, r, :] * jnp.concatenate([iv, iv], axis=1)
            ds = (pr * (mm(gl_st[r, :], vv) - jnp.concatenate([de, de], axis=1))).astype(BF16)
            acc[r, :] += mm_nt(ds, kk)
            gv = gv + mm(gl_t[:, r], pr.astype(BF16))
            gk = gk + mm(q_t[:, r], ds)
        gk = (gk * scale).astype(BF16)
        gv = gv.astype(BF16)
        for c in range(2):
            for p in range(2):
                kg_send[p, 2 * i + c] = jnp.concatenate(
                    [gk[64 * p:64 * p + 64, 128 * c:128 * c + 128], gv[64 * p:64 * p + 64, 128 * c:128 * c + 128]], axis=0
                )
        for c in range(2):
            j = 2 * i + c
            for p in range(2):
                @pl.when(jnp.logical_and(j <= s, jnp.logical_not(kg_mine(p, j))))
                def _(p=p, j=j):
                    kg_copy(p, j).start()
        return carry

    lax.fori_loop(0, chunk + 1, backward, 0)
    kg_recv[par, s] = kg_send[par, s]
    for p in range(nq):
        gq_o[:, 128 * p:128 * p + 128] = acc[128 * p:128 * p + 128, :] * scale
    put(gq_o, gq_hbm.at[0])
    wait_from(lambda j: rcopy(seq_block(fi_recv, j, 64), seq_block(fi_recv, j, 64), fi_ss.at[0], fi_rs.at[j], seq=j))
    entry = fi_recv[...]
    gye = (gy[...] * ecx[...]).astype(BF16)
    grad_r = mm(m_sum.astype(BF16), write_v[...]) + mm(gye, entry)
    ps_send[rows:, :] = grad_r.astype(BF16)
    part = 2 * rows // ntp

    def p1_copy(d):
        to = lax.rem(z + d, ntp)
        return rcopy(seq_block(ps_send, to, part), ps_recv.at[z], p1_ss.at[d], p1_rs.at[z], tp=to)

    for d in range(1, ntp):
        p1_copy(d).start()
    own_part = pl.ds(pl.multiple_of(z * part, part), part)
    ps_recv[z] = ps_send[own_part, :]

    y_ent = mm_nt(read_v[...], entry) * ecx[...]
    q_sum = mm_nt(eb64, gy[...] * y_ent, HIGH)
    for p in range(nheads // 2):
        lanes = slice(128 * p, 128 * p + 128)
        xp = x_v[:, lanes]
        xm = jnp.concatenate([jnp.where(lane_lo, xp, 0.0), jnp.where(lane_lo, 0.0, xp)], axis=0).astype(BF16)
        y = mm(w_b[p], xm) + y_ent[:, lanes] + skip_row[:, lanes] * xp
        gg_o[:, lanes] = dsc[:, lanes] * y
    put(gg_o, gg_hbm.at[0])

    es_prod = exit_g.astype(F32) * entry.astype(F32)
    c_h = jnp.sum(mm(eb64, es_prod, HIGH), axis=1, keepdims=True) * jnp.exp(-cum_last)
    tail = jnp.where(row_i >= col_i, 1.0, 0.0).astype(F32)
    before = jnp.where(row_i < col_i, 1.0, 0.0).astype(F32)
    drate = mm(col_r - row_r - q_sum, tail, HIGH) - mm(r_s, before, HIGH) - c_h
    ddt = (col_r + r_s) / dt + drate * ea
    draw = ddt * sig_z
    gdt_o[...] = draw
    put(gdt_o, gdt_hbm.at[0])

    lane8 = lax.broadcasted_iota(jnp.int32, (nheads, 128), 1)
    pp_all[s] = jnp.where(
        lane8 == 0, jnp.sum(drate * rate, axis=1, keepdims=True),
        jnp.where(
            lane8 == 1, jnp.sum(gyx, axis=1, keepdims=True),
            jnp.where(lane8 == 2, jnp.sum(draw, axis=1, keepdims=True), 0.0),
        ),
    )

    def pa_copy(d):
        return rcopy(pp_all.at[s], pp_all.at[s], pa_ss.at[d], pa_rs.at[s], seq=lax.rem(s + d, nseq))

    for d in range(1, nseq):
        pa_copy(d).start()

    for d in range(1, ntp):
        j = lax.rem(z + d, ntp)
        rcopy(ps_recv.at[j], ps_recv.at[j], p1_ss.at[0], p1_rs.at[j], tp=j).wait_recv()
    red = ps_recv[0].astype(F32)
    for j in range(1, ntp):
        red = red + ps_recv[j].astype(F32)
    ps_out[own_part, :] = red.astype(BF16)

    def p2_copy(d):
        here = seq_block(ps_out, z, part)
        return rcopy(here, here, p2_ss.at[d], p2_rs.at[z], tp=lax.rem(z + d, ntp))

    for d in range(1, ntp):
        p2_copy(d).start()

    wait_from(lambda j: rcopy(pp_all.at[j], pp_all.at[j], pa_ss.at[0], pa_rs.at[j], seq=j))
    pd = pp_all[0]
    for j in range(1, nseq):
        pd = pd + pp_all[j]
    pd_all[x] = pd

    def pb_copy(d):
        return rcopy(pd_all.at[x], pd_all.at[x], pb_ss.at[d], pb_rs.at[x], dp=lax.rem(x + d, ndp))

    for d in range(1, ndp):
        pb_copy(d).start()

    def kg_add(j, total):
        for p in range(2):
            @pl.when(jnp.logical_not(kg_mine(p, j)))
            def _(p=p):
                rcopy(kg_recv.at[p, j], kg_recv.at[p, j], kg_ss.at[0, 0], kg_rs.at[p, j], tp=other).wait_recv()
        return total + kg_recv[0, j].astype(F32) + kg_recv[1, j].astype(F32)

    kg = lax.fori_loop(s, nseq, kg_add, jnp.zeros((rows, 128), F32))
    gk_o[...] = kg[:64]
    gv_o[...] = kg[64:]
    put(gk_o, gk_hbm.at[0])
    put(gv_o, gv_hbm.at[0])

    for d in range(1, ndp):
        j = lax.rem(x + d, ndp)
        rcopy(pd_all.at[j], pd_all.at[j], pb_ss.at[0], pb_rs.at[j], dp=j).wait_recv()
    pd = pd_all[0]
    for j in range(1, ndp):
        pd = pd + pd_all[j]
    pf[...] = pd
    put(pf, pf_hbm)

    for d in range(1, ntp):
        j = lax.rem(z + d, ntp)
        there = seq_block(ps_out, j, part)
        rcopy(there, there, p2_ss.at[0], p2_rs.at[j], tp=j).wait_recv()
    gw_o[...] = ps_out[:rows, :].astype(F32)
    gr_o[...] = ps_out[rows:, :].astype(F32)
    put(gw_o, gw_hbm.at[0])
    put(gr_o, gr_hbm.at[0])

    kv_copy(0, 0, s, other).wait_send()
    for d in range(1, nseq):
        @pl.when(s + d < nseq)
        def _(d=d):
            kv_copy(d, 0, s + d, base).wait_send()
            kv_copy(d, 1, s + d, base + 1).wait_send()
        cl_copy(d, lax.rem(s + d, nseq)).wait_send()
        es_copy(d).wait_send()
        fs_copy(d).wait_send()
        pa_copy(d).wait_send()
    for i in range(nseq):
        @pl.when(s != i)
        def _(i=i):
            back_copy(es_out, ex_recv, ex_ss, ex_rs, i).wait_send()
            back_copy(fs_out, fi_recv, fi_ss, fi_rs, i).wait_send()
        for p in range(2):
            @pl.when(jnp.logical_and(i <= s, jnp.logical_not(kg_mine(p, i))))
            def _(p=p, i=i):
                kg_copy(p, i).wait_send()
    for d in range(1, ntp):
        p1_copy(d).wait_send()
        p2_copy(d).wait_send()
    for d in range(1, ndp):
        pb_copy(d).wait_send()
    for copy in outs:
        copy.wait()


def body(
    dims, query_rows, key_rows, value_rows, gate_rows, write_vec, read_vec, dt_raw, a_log, skip_gain, dt_bias, out_grad
):
    nseq, ntp, ndp, nheads, nq = dims
    rows = 128
    wide = nheads * 64
    dma = pltpu.SemaphoreType.DMA

    def vm(shape, kind=F32):
        return pltpu.VMEM(shape, kind)

    any_spec = pl.BlockSpec(memory_space=pl.ANY)
    smem_spec = pl.BlockSpec(memory_space=pltpu.SMEM)
    outs = (
        (1, rows, wide), (1, 64, rows), (1, 64, rows), (1, rows, wide), (1, rows, 128), (1, rows, 128),
        (1, nheads, rows), (nheads, 128),
    )
    tall = nq * rows
    scratch = [
        vm((rows, wide), BF16), vm((64, rows), BF16), vm((64, rows), BF16), vm((rows, wide), BF16),
        vm((rows, 128), BF16), vm((rows, 128), BF16), vm((nheads, rows)), vm((rows, wide), BF16),
        vm((2, nseq, 128, rows), BF16), vm((nseq // 2, 128, 2 * rows), BF16), vm((nseq // 2, 128, 2 * rows), BF16),
        vm((tall, 128), BF16), vm((128, tall), BF16), vm((nseq // 2, tall, 256)), vm((tall, 128)), vm((tall, 128)), vm((tall, 128)),
        vm((tall, 128), BF16), vm((128, tall), BF16), vm((tall, 128)),
        vm((rows, wide)), vm((rows, wide)), vm((rows, wide)), vm((rows, wide)), vm((rows, wide)), vm((rows, wide)),
        vm((nheads // 2, 2 * rows, rows)), vm((nheads // 2, rows, 2 * rows), BF16),
        vm((nheads // 2, 2 * rows, 128), BF16),
        vm((nseq, nheads, 128)),
        vm((wide, 128), BF16), vm((nseq, 64, 128), BF16), vm((nseq, 64, 128), BF16), vm((wide, 128), BF16),
        vm((wide, 128), BF16), vm((nseq, 64, 128), BF16), vm((nseq, 64, 128), BF16), vm((wide, 128), BF16),
        vm((2, nseq, 128, rows), BF16), vm((2, nseq, 128, rows), BF16),
        vm((2 * rows, 128), BF16), vm((ntp, 2 * rows // ntp, 128), BF16), vm((2 * rows, 128), BF16),
        vm((nseq, nheads, 128)), vm((ndp, nheads, 128)),
        vm((rows, wide)), vm((64, rows)), vm((64, rows)), vm((rows, wide)), vm((rows, 128)), vm((rows, 128)),
        vm((nheads, rows)), vm((nheads, 128)),
        dma((8,)), dma((8,)), dma((nseq, 2)), dma((2, nseq)), dma((nseq,)), dma((nseq,)),
        dma((nseq,)), dma((nseq,)), dma((nseq,)), dma((nseq,)),
        dma((nseq,)), dma((nseq,)), dma((nseq,)), dma((nseq,)),
        dma((2, nseq)), dma((2, nseq)), dma((ntp,)), dma((ntp,)), dma((ntp,)), dma((ntp,)),
        dma((nseq,)), dma((nseq,)), dma((ndp,)), dma((ndp,)),
    ]
    results = pl.pallas_call(
        functools.partial(kernel, dims),
        out_shape=tuple(jax.ShapeDtypeStruct(o, F32) for o in outs),
        in_specs=[any_spec] * 8 + [smem_spec] * 3,
        out_specs=tuple([any_spec] * 8),
        scratch_shapes=scratch,
        compiler_params=pltpu.CompilerParams(
            collective_id=0, has_side_effects=True, vmem_limit_bytes=VMEM
        ),
    )(
        query_rows, jnp.swapaxes(key_rows, 1, 2), jnp.swapaxes(value_rows, 1, 2), gate_rows, write_vec, read_vec, dt_raw,
        out_grad, a_log, skip_gain, dt_bias,
    )
    per_head = jax.ShapeDtypeStruct((nheads,), F32)
    written = pl.pallas_call(
        functools.partial(write_out, nheads),
        out_shape=tuple([jax.ShapeDtypeStruct(o, F32) for o in outs[:7]] + [per_head] * 3),
        in_specs=[any_spec] * 8,
        out_specs=tuple([any_spec] * 7 + [smem_spec] * 3),
        scratch_shapes=[dma((8,)), pltpu.SMEM((nheads, 128), F32)],
        compiler_params=pltpu.CompilerParams(vmem_limit_bytes=VMEM),
    )(*results)
    return (
        written[0], jnp.swapaxes(written[1], 1, 2), jnp.swapaxes(written[2], 1, 2), *written[3:],
    )


def write_out(nheads, *refs):
    sources, targets, (sems, small) = refs[:8], refs[8:18], refs[18:]
    copies = [pltpu.make_async_copy(sources[7], small, sems.at[7])]
    copies += [pltpu.make_async_copy(a, b, sems.at[i]) for i, (a, b) in enumerate(zip(sources[:7], targets[:7]))]
    for copy in copies:
        copy.start()
    copies[0].wait()
    for h in range(nheads):
        for i in range(3):
            targets[7 + i][h] = small[h, i]
    for copy in copies[1:]:
        copy.wait()


def solution(mesh):
    dims = (mesh.shape["seq"], mesh.shape["tp"], mesh.shape["dp"], 8, 4)
    wide = P("dp", "seq", "tp")
    shared = P("dp", "seq", None)
    steps = P("dp", "tp", "seq")
    head = P("tp")
    return jax.shard_map(
        functools.partial(body, dims),
        mesh=mesh,
        in_specs=(wide, wide, wide, wide, shared, shared, steps, head, head, head, wide),
        out_specs=(wide, wide, wide, wide, shared, shared, steps, head, head, head),
        check_vma=False,
    )
```

```python
import functools

import jax
import jax.numpy as jnp
from jax import lax
from jax.experimental import pallas as pl
from jax.experimental.pallas import tpu as pltpu
from jax.sharding import PartitionSpec as P

HIGH = lax.Precision.HIGHEST
MESH = pl.DeviceIdType.MESH
F32 = jnp.float32
BF16 = jnp.bfloat16
NEG_FILL = -1e30
VMEM = 60 * 1024 * 1024


def mm(a, b, precision=None):
    return lax.dot_general(a, b, (((1,), (0,)), ((), ())), precision=precision, preferred_element_type=F32)


def mm_nt(a, b, precision=None):
    return lax.dot_general(a, b, (((1,), (1,)), ((), ())), precision=precision, preferred_element_type=F32)


def mm_tn(a, b, precision=None):
    return lax.dot_general(a, b, (((0,), (0,)), ((), ())), precision=precision, preferred_element_type=F32)


def kernel(
    dims,
    q_hbm, k_hbm, v_hbm, gate_hbm, write_hbm, read_hbm, dt_hbm, cot_hbm,
    alog_s, skip_s, bias_s,
    gq_hbm, gk_hbm, gv_hbm, gg_hbm, gw_hbm, gr_hbm, gdt_hbm, pf_hbm,
    q_v, k_v, v_v, gate_v, write_v, read_v, dt_v, cot_v,
    kv_buf, kf, vf, q_st, q_t, s_buf, m_buf, l_buf, acc, gl_st, gl_t, delta_b,
    gy, dsc, ecx, w2x, dx, x_v, dtl_b, w_b, gym_b,
    cl_all, es_send, es_recv, es_out, ex_recv, fs_send, fs_recv, fs_out, fi_recv,
    kg_send, kg_recv, gw_send, gr_send, ps_recv, ps_out, pp_all, pd_all,
    gq_o, gk_o, gv_o, gg_o, gw_o, gr_o, gdt_o, pf,
    in_sem, out_sem, kv_ss, kv_rs, cl_ss, cl_rs, es_ss, es_rs, ex_ss, ex_rs, fs_ss, fs_rs, fi_ss, fi_rs,
    kg_ss, kg_rs, p1_ss, p1_rs, p2_ss, p2_rs, pa_ss, pa_rs, pb_ss, pb_rs,
):
    nseq, ntp, ndp, nheads, nq = dims
    rows = 128
    s = lax.axis_index("seq")
    z = lax.axis_index("tp")
    x = lax.axis_index("dp")
    par = lax.rem(z, 2)
    base = z - par
    other = base + 1 - par
    chunk = lax.div(s, 2)
    core = lax.rem(s, 2)
    sibling = s + 1 - 2 * core
    nchip = nseq // 2
    scale = 128 ** (-0.5)

    def rcopy(src, dst, ssem, rsem, **where):
        return pltpu.make_async_remote_copy(
            src_ref=src, dst_ref=dst, send_sem=ssem, recv_sem=rsem, device_id=where, device_id_type=MESH
        )

    def seq_block(ref, i, n):
        return ref.at[pl.ds(pl.multiple_of(i * n, n), n)]

    outs = []

    def put(src, dst):
        copy = pltpu.make_async_copy(src, dst, out_sem.at[len(outs)])
        copy.start()
        outs.append(copy)

    loads = []
    for at, (src, dst) in enumerate((
        (k_hbm.at[0], k_v), (v_hbm.at[0], v_v), (dt_hbm.at[0], dt_v), (gate_hbm.at[0], gate_v),
        (cot_hbm.at[0], cot_v), (read_hbm.at[0], read_v), (write_hbm.at[0], write_v), (q_hbm.at[0], q_v),
    )):
        copy = pltpu.make_async_copy(src, dst, in_sem.at[at])
        copy.start()
        loads.append(copy)

    barrier = pltpu.get_barrier_semaphore()
    for d in range(1, nseq):
        to = lax.rem(s + d, nseq)
        pl.semaphore_signal(barrier, inc=1, device_id={"seq": to, "tp": z}, device_id_type=MESH)
        pl.semaphore_signal(barrier, inc=1, device_id={"seq": to, "tp": other}, device_id_type=MESH)
    for d in range(1, ntp):
        pl.semaphore_signal(barrier, inc=1, device_id={"tp": lax.rem(z + d, ntp)}, device_id_type=MESH)
    for d in range(1, ndp):
        pl.semaphore_signal(barrier, inc=1, device_id={"dp": lax.rem(x + d, ndp)}, device_id_type=MESH)

    loads[0].wait()
    loads[1].wait()
    kv_buf[par, s] = jnp.concatenate([k_v[...], v_v[...]], axis=0)

    @pl.when(lax.rem(s, 2) == 0)
    def _():
        kv_buf[0, s + 1] = jnp.zeros((rows, 128), BF16)
        kv_buf[1, s + 1] = jnp.zeros((rows, 128), BF16)

    pl.semaphore_wait(barrier, 2 * (nseq - 1) + (ntp - 1) + (ndp - 1))

    def kv_copy(kind, at, p, j, **where):
        here = kv_buf.at[p, j]
        return rcopy(here, here, kv_ss.at[kind, at], kv_rs.at[p, j], **where)

    def kv_along(d):
        return kv_copy(0, d, par, s, seq=s + 2 * d)

    def kv_partner(y):
        return kv_copy(1, y, par, 2 * y + core, tp=other)

    for d in range(1, nchip):
        @pl.when(chunk + d < nchip)
        def _(d=d):
            kv_along(d).start()
    kv_partner(chunk).start()

    @pl.when(core == 0)
    def _():
        kv_copy(2, chunk, par, s, seq=sibling).start()

    row_i = lax.broadcasted_iota(jnp.int32, (rows, rows), 0)
    col_i = lax.broadcasted_iota(jnp.int32, (rows, rows), 1)
    causal = row_i >= col_i
    head_i = lax.broadcasted_iota(jnp.int32, (nheads, rows), 0)

    def head_rows(ref):
        out = jnp.zeros((nheads, rows), F32)
        for h in range(nheads):
            out = jnp.where(head_i == h, ref[h], out)
        return out

    wide = nheads * 64
    eb64 = jnp.where(
        lax.broadcasted_iota(jnp.int32, (nheads, wide), 1) // 64
        == lax.broadcasted_iota(jnp.int32, (nheads, wide), 0), 1.0, 0.0,
    ).astype(F32)
    eb128 = jnp.where(
        lax.broadcasted_iota(jnp.int32, (nheads, nheads * 128), 1) // 128
        == lax.broadcasted_iota(jnp.int32, (nheads, nheads * 128), 0), 1.0, 0.0,
    ).astype(F32)

    loads[2].wait()
    zdt = dt_v[...] + head_rows(bias_s)
    dt = jnp.maximum(zdt, 0.0) + jnp.log1p(jnp.exp(-jnp.abs(zdt)))
    sig_z = 1.0 / (1.0 + jnp.exp(-zdt))
    ea = jnp.exp(head_rows(alog_s))
    rate = dt * ea
    cum = mm(rate, jnp.where(row_i <= col_i, 1.0, 0.0).astype(F32), HIGH)
    cum_last = jnp.broadcast_to(cum[:, rows - 1:rows], (nheads, rows))
    cl_all[s] = cum_last

    def cl_copy(d, to):
        return rcopy(cl_all.at[s], cl_all.at[s], cl_ss.at[d], cl_rs.at[s], seq=to)

    for d in range(1, nseq):
        cl_copy(d, lax.rem(s + d, nseq)).start()

    ecum = jnp.exp(-cum)
    w2 = dt * jnp.exp(-(cum_last - cum))
    ecx[...] = mm_tn(ecum, eb64, HIGH)
    w2x[...] = mm_tn(w2, eb64, HIGH)
    cum_b = mm_tn(cum, eb128, HIGH)

    loads[3].wait()
    loads[4].wait()
    gate = gate_v[...].astype(F32)
    cot = cot_v[...].astype(F32)
    sig = 1.0 / (1.0 + jnp.exp(-gate))
    gy[...] = cot * gate * sig
    dsc[...] = cot * sig * (1.0 + gate * (1.0 - sig))
    loads[5].wait()
    gye = (gy[...] * ecx[...]).astype(BF16)
    es_send[...] = mm_tn(gye, read_v[...]).astype(BF16)

    def all_to_all(send, recv, ss, rs):
        def copy(d):
            to = lax.rem(s + d, nseq)
            return rcopy(seq_block(send, to, 64), recv.at[s], ss.at[d], rs.at[s], seq=to)
        for d in range(1, nseq):
            copy(d).start()
        recv[s] = send[pl.ds(pl.multiple_of(s * 64, 64), 64), :]
        return copy

    es_copy = all_to_all(es_send, es_recv, es_ss, es_rs)

    loads[6].wait()
    cb = mm_nt(read_v[...], write_v[...])
    lane_lo = lax.broadcasted_iota(jnp.int32, (rows, 128), 1) < 64
    skip_row = jnp.zeros((1, wide), F32)
    lane_head = lax.broadcasted_iota(jnp.int32, (1, wide), 1) // 64
    for h in range(nheads):
        skip_row = jnp.where(lane_head == h, skip_s[h], skip_row)
    for p in range(nheads // 2):
        lanes = slice(128 * p, 128 * p + 128)
        ws = []
        for c in range(2):
            h = 2 * p + c
            gap = cum_b[:, 128 * h:128 * h + 128] - cum[h:h + 1, :]
            dtl = jnp.where(causal, jnp.exp(-jnp.maximum(gap, 0.0)), 0.0) * dt[h:h + 1, :]
            dtl_b[p, 128 * c:128 * c + 128, :] = dtl
            ws.append((dtl * cb).astype(BF16))
        gp = gy[:, lanes]
        gym = jnp.concatenate([jnp.where(lane_lo, gp, 0.0), jnp.where(lane_lo, 0.0, gp)], axis=0).astype(BF16)
        gym_b[p] = gym
        w_b[p] = jnp.concatenate(ws, axis=1)
        dx[:, lanes] = mm_tn(jnp.concatenate(ws, axis=0), gym) + skip_row[:, lanes] * gp

    for d in (1, 3, 2) if nchip == 4 else range(1, nchip):
        @pl.when(chunk >= d)
        def _(d=d):
            y = chunk - d
            kv_copy(0, 0, par, 2 * y + core, tp=other).wait_recv()
            kv_partner(y).start()
            kv_copy(2, y, par, 2 * y + core, seq=sibling).start()

    def wait_from(make, skip_self=True):
        for d in range(1, nseq):
            make(lax.rem(s + d, nseq)).wait_recv()

    wait_from(lambda j: rcopy(cl_all.at[j], cl_all.at[j], cl_ss.at[0], cl_rs.at[j], seq=j))
    wait_from(lambda j: rcopy(es_recv.at[j], es_recv.at[j], es_ss.at[0], es_rs.at[j], seq=j))

    def back_copy(out, recv, ss, rs, i):
        here = seq_block(recv, s, 64)
        return rcopy(out.at[i], here, ss.at[i], rs.at[s], seq=i)

    own_head = pl.ds(pl.multiple_of(s * 64, 64), 64)

    def send_back(out, recv, ss, rs, i):
        @pl.when(s != i)
        def _():
            back_copy(out, recv, ss, rs, i).start()

        @pl.when(s == i)
        def _():
            recv[own_head, :] = out[i]

    state = jnp.zeros((64, 128), F32)
    for i in reversed(range(nseq)):
        es_out[i] = state.astype(BF16)
        send_back(es_out, ex_recv, ex_ss, ex_rs, i)
        state = es_recv[i].astype(F32) + jnp.exp(-cl_all[i, pl.ds(s, 1), :]) * state

    def from_partner(y):
        kv_copy(0, 0, 1 - par, 2 * y + core, tp=other).wait_recv()

        @pl.when(jnp.logical_or(y < chunk, core == 0))
        def _():
            kv_copy(3, y, 1 - par, 2 * y + core, seq=sibling).start()

    from_partner(chunk)
    for d in (1, 3, 2) if nchip == 4 else range(1, nchip):
        @pl.when(chunk >= d)
        def _(d=d):
            from_partner(chunk - d)

    loads[7].wait()
    for p in range(nq):
        q_st[128 * p:128 * p + 128, :] = q_v[:, 128 * p:128 * p + 128]
        q_t[:, 128 * p:128 * p + 128] = q_v[:, 128 * p:128 * p + 128].T
    m_buf[...] = jnp.full((nq * rows, 128), NEG_FILL, F32)
    l_buf[...] = jnp.zeros((nq * rows, 128), F32)
    acc[...] = jnp.zeros((nq * rows, 128), F32)

    def scores(i, carry):
        @pl.when(jnp.logical_or(i < chunk, core == 1))
        def _():
            for p in range(2):
                kv_copy(0, 0, p, 2 * i + 1 - core, tp=other).wait_recv()

        lo = jnp.concatenate([kv_buf[0, 2 * i], kv_buf[0, 2 * i + 1]], axis=1)
        hi = jnp.concatenate([kv_buf[1, 2 * i], kv_buf[1, 2 * i + 1]], axis=1)
        kk = jnp.concatenate([lo[:64], hi[:64]], axis=0)
        kf[i] = kk
        vf[i] = jnp.concatenate([lo[64:], hi[64:]], axis=0)
        allowed = (
            i * 256 + lax.broadcasted_iota(jnp.int32, (rows, 256), 1)
            <= s * rows + lax.broadcasted_iota(jnp.int32, (rows, 256), 0)
        )
        for p in range(nq):
            r = slice(rows * p, rows * p + rows)
            sc = jnp.where(allowed, mm(q_st[r, :], kk) * scale, NEG_FILL)
            s_buf[i, r, :] = sc
            m_buf[r, :] = jnp.maximum(m_buf[r, :], jnp.maximum(sc[:, :128], sc[:, 128:]))
        return carry

    lax.fori_loop(0, chunk + 1, scores, 0)
    m_buf[...] = jnp.broadcast_to(jnp.max(m_buf[...], axis=1, keepdims=True), (nq * rows, 128))

    def weights(i, carry):
        vv = vf[i]
        for p in range(nq):
            r = slice(rows * p, rows * p + rows)
            m = m_buf[r, :]
            e = jnp.exp(s_buf[i, r, :] - jnp.concatenate([m, m], axis=1))
            s_buf[i, r, :] = e
            l_buf[r, :] += e[:, :128] + e[:, 128:]
            acc[r, :] += mm_nt(e.astype(BF16), vv)
        return carry

    lax.fori_loop(0, chunk + 1, weights, 0)
    total = jnp.sum(l_buf[...], axis=1, keepdims=True)
    inv = jnp.broadcast_to(1.0 / total, (nq * rows, 128))
    l_buf[...] = inv
    acc[...] = acc[...] * inv
    for p in range(nq):
        x_v[:, 128 * p:128 * p + 128] = acc[128 * p:128 * p + 128, :]

    xw = (x_v[...] * w2x[...]).astype(BF16)
    fs_send[...] = mm_tn(xw, write_v[...]).astype(BF16)
    fs_copy = all_to_all(fs_send, fs_recv, fs_ss, fs_rs)

    m_sum = jnp.zeros((rows, rows), F32)
    col_r = jnp.zeros((nheads, rows), F32)
    row_r = jnp.zeros((nheads, rows), F32)
    ones8 = jnp.ones((8, 128), F32)
    for p in range(nheads // 2):
        lanes = slice(128 * p, 128 * p + 128)
        xp = x_v[:, lanes]
        g = mm_nt(gym_b[p], xp.astype(BF16))
        mp = dtl_b[p] * g
        m_sum = m_sum + mp[:rows] + mp[rows:]
        r0 = mp[:rows] * cb
        r1 = mp[rows:] * cb
        rs = mm_nt(ones8, jnp.concatenate([r0, r1], axis=0), HIGH)
        col_r = jnp.where(head_i == 2 * p, jnp.sum(r0, axis=0, keepdims=True), col_r)
        col_r = jnp.where(head_i == 2 * p + 1, jnp.sum(r1, axis=0, keepdims=True), col_r)
        row_r = jnp.where(head_i == 2 * p, rs[0:1, :rows], row_r)
        row_r = jnp.where(head_i == 2 * p + 1, rs[0:1, rows:], row_r)

    wait_from(lambda j: rcopy(seq_block(ex_recv, j, 64), seq_block(ex_recv, j, 64), ex_ss.at[0], ex_rs.at[j], seq=j))
    exit_g = ex_recv[...]
    dx_exit = mm_nt(write_v[...], exit_g) * w2x[...]
    r_s = mm_nt(eb64, x_v[...] * dx_exit, HIGH)
    gyx = mm_nt(eb64, x_v[...] * gy[...], HIGH)
    dx[...] = dx[...] + dx_exit
    grad_w = mm_tn(m_sum.astype(BF16), read_v[...]) + mm(xw, exit_g)
    gw_send[...] = grad_w.astype(BF16)

    part = 2 * rows // ntp

    def p1_copy(send, o, odd):
        return rcopy(send.at[pl.ds(part * o, part)], ps_recv.at[z], p1_ss.at[odd, o], p1_rs.at[z], tp=2 * o + odd)

    def p1_start(send, odd):
        for o in range(ntp // 2):
            @pl.when(z != 2 * o + odd)
            def _(o=o):
                p1_copy(send, o, odd).start()

            @pl.when(z == 2 * o + odd)
            def _(o=o):
                ps_recv[z] = send[part * o:part * o + part, :]

    p1_start(gw_send, 1)

    wait_from(lambda j: rcopy(fs_recv.at[j], fs_recv.at[j], fs_ss.at[0], fs_rs.at[j], seq=j))
    state = jnp.zeros((64, 128), F32)
    for i in range(nseq):
        fs_out[i] = state.astype(BF16)
        send_back(fs_out, fi_recv, fi_ss, fi_rs, i)
        state = fs_recv[i].astype(F32) + jnp.exp(-cl_all[i, pl.ds(s, 1), :]) * state

    for p in range(nq):
        r = slice(rows * p, rows * p + rows)
        ga = dx[:, 128 * p:128 * p + 128]
        gl_st[r, :] = ga.astype(BF16)
        gl_t[:, r] = ga.astype(BF16).T
        delta_b[r, :] = jnp.broadcast_to(
            jnp.sum(ga * x_v[:, 128 * p:128 * p + 128], axis=1, keepdims=True), (rows, 128)
        )
    acc[...] = jnp.zeros((nq * rows, 128), F32)

    def kg_copy(p, j):
        return rcopy(
            kg_send.at[p, j], kg_recv.at[par, s],
            kg_ss.at[p, j], kg_rs.at[par, s], seq=j, tp=base + p,
        )

    def kg_mine(p, j):
        return jnp.logical_and(j == s, p == par)

    def backward(i, carry):
        kk = kf[i]
        vv = vf[i]
        gk = jnp.zeros((128, 256), F32)
        gv = jnp.zeros((128, 256), F32)
        for p in range(nq):
            r = slice(rows * p, rows * p + rows)
            iv = l_buf[r, :]
            de = delta_b[r, :]
            pr = s_buf[i, r, :] * jnp.concatenate([iv, iv], axis=1)
            ds = (pr * (mm(gl_st[r, :], vv) - jnp.concatenate([de, de], axis=1))).astype(BF16)
            acc[r, :] += mm_nt(ds, kk)
            gv = gv + mm(gl_t[:, r], pr.astype(BF16))
            gk = gk + mm(q_t[:, r], ds)
        gk = (gk * scale).astype(BF16)
        gv = gv.astype(BF16)
        for c in range(2):
            for p in range(2):
                kg_send[p, 2 * i + c] = jnp.concatenate(
                    [gk[64 * p:64 * p + 64, 128 * c:128 * c + 128], gv[64 * p:64 * p + 64, 128 * c:128 * c + 128]], axis=0
                )
        return carry

    lax.fori_loop(0, chunk + 1, backward, 0)
    kg_recv[par, s] = kg_send[par, s]
    for p in range(nq):
        gq_o[:, 128 * p:128 * p + 128] = acc[128 * p:128 * p + 128, :] * scale
    put(gq_o, gq_hbm.at[0])
    wait_from(lambda j: rcopy(seq_block(fi_recv, j, 64), seq_block(fi_recv, j, 64), fi_ss.at[0], fi_rs.at[j], seq=j))
    entry = fi_recv[...]
    gye = (gy[...] * ecx[...]).astype(BF16)
    grad_r = mm(m_sum.astype(BF16), write_v[...]) + mm(gye, entry)
    gr_send[...] = grad_r.astype(BF16)
    p1_start(gr_send, 0)
    for j in range(nseq):
        for p in range(2):
            @pl.when(jnp.logical_and(j <= s, jnp.logical_not(kg_mine(p, j))))
            def _(p=p, j=j):
                kg_copy(p, j).start()

    y_ent = mm_nt(read_v[...], entry) * ecx[...]
    q_sum = mm_nt(eb64, gy[...] * y_ent, HIGH)
    for p in range(nheads // 2):
        lanes = slice(128 * p, 128 * p + 128)
        xp = x_v[:, lanes]
        xm = jnp.concatenate([jnp.where(lane_lo, xp, 0.0), jnp.where(lane_lo, 0.0, xp)], axis=0).astype(BF16)
        y = mm(w_b[p], xm) + y_ent[:, lanes] + skip_row[:, lanes] * xp
        gg_o[:, lanes] = dsc[:, lanes] * y
    put(gg_o, gg_hbm.at[0])

    es_prod = exit_g.astype(F32) * entry.astype(F32)
    c_h = jnp.sum(mm(eb64, es_prod, HIGH), axis=1, keepdims=True) * jnp.exp(-cum_last)
    tail = jnp.where(row_i >= col_i, 1.0, 0.0).astype(F32)
    before = jnp.where(row_i < col_i, 1.0, 0.0).astype(F32)
    drate = mm(col_r - row_r - q_sum, tail, HIGH) - mm(r_s, before, HIGH) - c_h
    ddt = (col_r + r_s) / dt + drate * ea
    draw = ddt * sig_z
    gdt_o[...] = draw
    put(gdt_o, gdt_hbm.at[0])

    lane8 = lax.broadcasted_iota(jnp.int32, (nheads, 128), 1)
    pp_all[s] = jnp.where(
        lane8 == 0, jnp.sum(drate * rate, axis=1, keepdims=True),
        jnp.where(
            lane8 == 1, jnp.sum(gyx, axis=1, keepdims=True),
            jnp.where(lane8 == 2, jnp.sum(draw, axis=1, keepdims=True), 0.0),
        ),
    )

    def pa_copy(d):
        return rcopy(pp_all.at[s], pp_all.at[s], pa_ss.at[d], pa_rs.at[s], seq=lax.rem(s + d, nseq))

    for d in range(1, nseq):
        pa_copy(d).start()

    for d in range(1, ntp):
        j = lax.rem(z + d, ntp)
        rcopy(ps_recv.at[j], ps_recv.at[j], p1_ss.at[0, 0], p1_rs.at[j], tp=j).wait_recv()
    red = ps_recv[0].astype(F32)
    for j in range(1, ntp):
        red = red + ps_recv[j].astype(F32)
    ps_out[z] = red.astype(BF16)

    def p2_copy(d):
        return rcopy(ps_out.at[z], ps_out.at[z], p2_ss.at[d], p2_rs.at[z], tp=lax.rem(z + d, ntp))

    for d in range(1, ntp):
        p2_copy(d).start()

    wait_from(lambda j: rcopy(pp_all.at[j], pp_all.at[j], pa_ss.at[0], pa_rs.at[j], seq=j))
    pd = pp_all[0]
    for j in range(1, nseq):
        pd = pd + pp_all[j]
    pd_all[x] = pd

    def pb_copy(d):
        return rcopy(pd_all.at[x], pd_all.at[x], pb_ss.at[d], pb_rs.at[x], dp=lax.rem(x + d, ndp))

    for d in range(1, ndp):
        pb_copy(d).start()

    def kg_add(j, total):
        for p in range(2):
            @pl.when(jnp.logical_not(kg_mine(p, j)))
            def _(p=p):
                rcopy(kg_recv.at[p, j], kg_recv.at[p, j], kg_ss.at[0, 0], kg_rs.at[p, j], tp=other).wait_recv()
        return total + kg_recv[0, j].astype(F32) + kg_recv[1, j].astype(F32)

    kg = lax.fori_loop(s, nseq, kg_add, jnp.zeros((rows, 128), F32))
    gk_o[...] = kg[:64]
    gv_o[...] = kg[64:]
    put(gk_o, gk_hbm.at[0])
    put(gv_o, gv_hbm.at[0])

    for d in range(1, ndp):
        j = lax.rem(x + d, ndp)
        rcopy(pd_all.at[j], pd_all.at[j], pb_ss.at[0], pb_rs.at[j], dp=j).wait_recv()
    pd = pd_all[0]
    for j in range(1, ndp):
        pd = pd + pd_all[j]
    pf[...] = pd
    put(pf, pf_hbm)

    for d in range(1, ntp):
        j = lax.rem(z + d, ntp)
        rcopy(ps_out.at[j], ps_out.at[j], p2_ss.at[0], p2_rs.at[j], tp=j).wait_recv()
    for o in range(ntp // 2):
        gw_o[part * o:part * o + part, :] = ps_out[2 * o + 1].astype(F32)
        gr_o[part * o:part * o + part, :] = ps_out[2 * o].astype(F32)
    put(gw_o, gw_hbm.at[0])
    put(gr_o, gr_hbm.at[0])

    for d in range(1, nchip):
        @pl.when(chunk + d < nchip)
        def _(d=d):
            kv_along(d).wait_send()
    for y in range(nchip):
        @pl.when(y <= chunk)
        def _(y=y):
            kv_partner(y).wait_send()

        @pl.when(jnp.logical_or(y < chunk, jnp.logical_and(y == chunk, core == 0)))
        def _(y=y):
            kv_copy(2, y, par, 2 * y + core, seq=sibling).wait_send()
            kv_copy(3, y, 1 - par, 2 * y + core, seq=sibling).wait_send()
    for d in range(1, nseq):
        cl_copy(d, lax.rem(s + d, nseq)).wait_send()
        es_copy(d).wait_send()
        fs_copy(d).wait_send()
        pa_copy(d).wait_send()
    for i in range(nseq):
        @pl.when(s != i)
        def _(i=i):
            back_copy(es_out, ex_recv, ex_ss, ex_rs, i).wait_send()
            back_copy(fs_out, fi_recv, fi_ss, fi_rs, i).wait_send()
        for p in range(2):
            @pl.when(jnp.logical_and(i <= s, jnp.logical_not(kg_mine(p, i))))
            def _(p=p, i=i):
                kg_copy(p, i).wait_send()
    for d in range(1, ntp):
        p2_copy(d).wait_send()
    for o in range(ntp // 2):
        for odd, send in ((1, gw_send), (0, gr_send)):
            @pl.when(z != 2 * o + odd)
            def _(o=o, odd=odd, send=send):
                p1_copy(send, o, odd).wait_send()
    for d in range(1, ndp):
        pb_copy(d).wait_send()
    for copy in outs:
        copy.wait()


def body(
    dims, query_rows, key_rows, value_rows, gate_rows, write_vec, read_vec, dt_raw, a_log, skip_gain, dt_bias, out_grad
):
    nseq, ntp, ndp, nheads, nq = dims
    rows = 128
    wide = nheads * 64
    dma = pltpu.SemaphoreType.DMA

    def vm(shape, kind=F32):
        return pltpu.VMEM(shape, kind)

    any_spec = pl.BlockSpec(memory_space=pl.ANY)
    smem_spec = pl.BlockSpec(memory_space=pltpu.SMEM)
    outs = (
        (1, rows, wide), (1, 64, rows), (1, 64, rows), (1, rows, wide), (1, rows, 128), (1, rows, 128),
        (1, nheads, rows), (nheads, 128),
    )
    tall = nq * rows
    scratch = [
        vm((rows, wide), BF16), vm((64, rows), BF16), vm((64, rows), BF16), vm((rows, wide), BF16),
        vm((rows, 128), BF16), vm((rows, 128), BF16), vm((nheads, rows)), vm((rows, wide), BF16),
        vm((2, nseq, 128, rows), BF16), vm((nseq // 2, 128, 2 * rows), BF16), vm((nseq // 2, 128, 2 * rows), BF16),
        vm((tall, 128), BF16), vm((128, tall), BF16), vm((nseq // 2, tall, 256)), vm((tall, 128)), vm((tall, 128)), vm((tall, 128)),
        vm((tall, 128), BF16), vm((128, tall), BF16), vm((tall, 128)),
        vm((rows, wide)), vm((rows, wide)), vm((rows, wide)), vm((rows, wide)), vm((rows, wide)), vm((rows, wide)),
        vm((nheads // 2, 2 * rows, rows)), vm((nheads // 2, rows, 2 * rows), BF16),
        vm((nheads // 2, 2 * rows, 128), BF16),
        vm((nseq, nheads, 128)),
        vm((wide, 128), BF16), vm((nseq, 64, 128), BF16), vm((nseq, 64, 128), BF16), vm((wide, 128), BF16),
        vm((wide, 128), BF16), vm((nseq, 64, 128), BF16), vm((nseq, 64, 128), BF16), vm((wide, 128), BF16),
        vm((2, nseq, 128, rows), BF16), vm((2, nseq, 128, rows), BF16),
        vm((rows, 128), BF16), vm((rows, 128), BF16),
        vm((ntp, 2 * rows // ntp, 128), BF16), vm((ntp, 2 * rows // ntp, 128), BF16),
        vm((nseq, nheads, 128)), vm((ndp, nheads, 128)),
        vm((rows, wide)), vm((64, rows)), vm((64, rows)), vm((rows, wide)), vm((rows, 128)), vm((rows, 128)),
        vm((nheads, rows)), vm((nheads, 128)),
        dma((8,)), dma((8,)), dma((4, max(nseq // 2, 4))), dma((2, nseq)), dma((nseq,)), dma((nseq,)),
        dma((nseq,)), dma((nseq,)), dma((nseq,)), dma((nseq,)),
        dma((nseq,)), dma((nseq,)), dma((nseq,)), dma((nseq,)),
        dma((2, nseq)), dma((2, nseq)), dma((2, ntp)), dma((ntp,)), dma((ntp,)), dma((ntp,)),
        dma((nseq,)), dma((nseq,)), dma((ndp,)), dma((ndp,)),
    ]
    results = pl.pallas_call(
        functools.partial(kernel, dims),
        out_shape=tuple(jax.ShapeDtypeStruct(o, F32) for o in outs),
        in_specs=[any_spec] * 8 + [smem_spec] * 3,
        out_specs=tuple([any_spec] * 8),
        scratch_shapes=scratch,
        compiler_params=pltpu.CompilerParams(
            collective_id=0, has_side_effects=True, vmem_limit_bytes=VMEM
        ),
    )(
        query_rows, jnp.swapaxes(key_rows, 1, 2), jnp.swapaxes(value_rows, 1, 2), gate_rows, write_vec, read_vec, dt_raw,
        out_grad, a_log, skip_gain, dt_bias,
    )
    per_head = jax.ShapeDtypeStruct((nheads,), F32)
    written = pl.pallas_call(
        functools.partial(write_out, nheads),
        out_shape=tuple([jax.ShapeDtypeStruct(o, F32) for o in outs[:7]] + [per_head] * 3),
        in_specs=[any_spec] * 8,
        out_specs=tuple([any_spec] * 7 + [smem_spec] * 3),
        scratch_shapes=[dma((8,)), dma((8,)), pltpu.SMEM((nheads, 128), F32)] + [vm(o) for o in outs[:7]],
        compiler_params=pltpu.CompilerParams(vmem_limit_bytes=VMEM),
    )(*results)
    return (
        written[0], jnp.swapaxes(written[1], 1, 2), jnp.swapaxes(written[2], 1, 2), *written[3:],
    )


def write_out(nheads, *refs):
    sources, targets, (load_sem, store_sem, small), staged = refs[:8], refs[8:18], refs[18:21], refs[21:]
    loads = [pltpu.make_async_copy(sources[7], small, load_sem.at[7])]
    loads += [pltpu.make_async_copy(sources[i], staged[i], load_sem.at[i]) for i in range(7)]
    for copy in loads:
        copy.start()
    stores = []
    for i in range(7):
        loads[1 + i].wait()
        stores.append(pltpu.make_async_copy(staged[i], targets[i], store_sem.at[i]))
        stores[i].start()
    loads[0].wait()
    for h in range(nheads):
        for i in range(3):
            targets[7 + i][h] = small[h, i]
    for copy in stores:
        copy.wait()


def solution(mesh):
    dims = (mesh.shape["seq"], mesh.shape["tp"], mesh.shape["dp"], 8, 4)
    wide = P("dp", "seq", "tp")
    shared = P("dp", "seq", None)
    steps = P("dp", "tp", "seq")
    head = P("tp")
    return jax.shard_map(
        functools.partial(body, dims),
        mesh=mesh,
        in_specs=(wide, wide, wide, wide, shared, shared, steps, head, head, head, wide),
        out_specs=(wide, wide, wide, wide, shared, shared, steps, head, head, head),
        check_vma=False,
    )
```

```python
import functools

import jax
import jax.numpy as jnp
from jax import lax
from jax.experimental import pallas as pl
from jax.experimental.pallas import tpu as pltpu
from jax.sharding import PartitionSpec as P

HIGH = lax.Precision.HIGHEST
MESH = pl.DeviceIdType.MESH
F32 = jnp.float32
BF16 = jnp.bfloat16
NEG_FILL = -1e30
VMEM = 60 * 1024 * 1024


def mm(a, b, precision=None):
    return lax.dot_general(a, b, (((1,), (0,)), ((), ())), precision=precision, preferred_element_type=F32)


def mm_nt(a, b, precision=None):
    return lax.dot_general(a, b, (((1,), (1,)), ((), ())), precision=precision, preferred_element_type=F32)


def mm_tn(a, b, precision=None):
    return lax.dot_general(a, b, (((0,), (0,)), ((), ())), precision=precision, preferred_element_type=F32)


def kernel(
    dims,
    q_hbm, k_hbm, v_hbm, gate_hbm, write_hbm, read_hbm, dt_hbm, cot_hbm,
    alog_s, skip_s, bias_s,
    gq_hbm, gk_hbm, gv_hbm, gg_hbm, gw_hbm, gr_hbm, gdt_hbm, pf_hbm,
    q_v, k_v, v_v, gate_v, write_v, read_v, dt_v, cot_v,
    kv_buf, kf, vf, q_st, q_t, s_buf, m_buf, l_buf, acc, gl_st, gl_t, delta_b,
    gy, dsc, ecx, w2x, dx, x_v, dtl_b, w_b, gym_b,
    cl_all, es_send, es_recv, es_out, ex_recv, fs_send, fs_recv, fs_out, fi_recv,
    kg_send, kg_sib, kg_recv, gw_send, gr_send, ps_recv, ps_out, pp_all, pd_all,
    gq_o, gk_o, gv_o, gg_o, gw_o, gr_o, gdt_o, pf,
    far_sem, in_sem, out_sem, kv_ss, kv_rs, cl_ss, cl_rs, es_ss, es_rs, ex_ss, ex_rs, fs_ss, fs_rs, fi_ss, fi_rs,
    sib_ss, sib_rs, kg_ss, kg_rs, p1_ss, p1_rs, p2_ss, p2_rs, pa_ss, pa_rs, pb_ss, pb_rs,
):
    nseq, ntp, ndp, nheads, nq = dims
    rows = 128
    s = lax.axis_index("seq")
    z = lax.axis_index("tp")
    x = lax.axis_index("dp")
    par = lax.rem(z, 2)
    base = z - par
    other = base + 1 - par
    chunk = lax.div(s, 2)
    core = lax.rem(s, 2)
    sibling = s + 1 - 2 * core
    nchip = nseq // 2
    scale = 128 ** (-0.5)

    def rcopy(src, dst, ssem, rsem, **where):
        return pltpu.make_async_remote_copy(
            src_ref=src, dst_ref=dst, send_sem=ssem, recv_sem=rsem, device_id=where, device_id_type=MESH
        )

    def seq_block(ref, i, n):
        return ref.at[pl.ds(pl.multiple_of(i * n, n), n)]

    outs = []

    def put(src, dst):
        copy = pltpu.make_async_copy(src, dst, out_sem.at[len(outs)])
        copy.start()
        outs.append(copy)

    loads = []
    for at, (src, dst) in enumerate((
        (k_hbm.at[0], k_v), (v_hbm.at[0], v_v), (dt_hbm.at[0], dt_v), (gate_hbm.at[0], gate_v),
        (cot_hbm.at[0], cot_v), (read_hbm.at[0], read_v), (write_hbm.at[0], write_v), (q_hbm.at[0], q_v),
    )):
        copy = pltpu.make_async_copy(src, dst, in_sem.at[at])
        copy.start()
        loads.append(copy)

    barrier = pltpu.get_barrier_semaphore()
    for d in range(1, nseq):
        to = lax.rem(s + d, nseq)
        pl.semaphore_signal(barrier, inc=1, device_id={"seq": to, "tp": z}, device_id_type=MESH)
        pl.semaphore_signal(barrier, inc=1, device_id={"seq": to, "tp": other}, device_id_type=MESH)
    for d in (1, ntp - 1):
        pl.semaphore_signal(barrier, inc=1, device_id={"tp": lax.rem(z + d, ntp)}, device_id_type=MESH)
    for d in range(1, ndp):
        pl.semaphore_signal(barrier, inc=1, device_id={"dp": lax.rem(x + d, ndp)}, device_id_type=MESH)

    loads[0].wait()
    loads[1].wait()
    kv_buf[par, s] = jnp.concatenate([k_v[...], v_v[...]], axis=0)

    @pl.when(lax.rem(s, 2) == 0)
    def _():
        kv_buf[0, s + 1] = jnp.zeros((rows, 128), BF16)
        kv_buf[1, s + 1] = jnp.zeros((rows, 128), BF16)

    pl.semaphore_wait(barrier, 2 * (nseq - 1) + 2 + (ndp - 1))

    rounds = [d for d in (1, 2, 4, 8) if d < ntp // 2]

    def tell(r):
        for d in (rounds[r], ntp - rounds[r]):
            pl.semaphore_signal(far_sem.at[r], inc=1, device_id={"tp": lax.rem(z + d, ntp)}, device_id_type=MESH)

    def hear(r):
        pl.semaphore_wait(far_sem.at[r], 2)

    if rounds:
        tell(0)

    def kv_copy(kind, at, p, j, **where):
        here = kv_buf.at[p, j]
        return rcopy(here, here, kv_ss.at[kind, at], kv_rs.at[p, j], **where)

    def kv_along(d):
        return kv_copy(0, d, par, s, seq=s + 2 * d)

    def kv_partner(y):
        return kv_copy(1, y, par, 2 * y + core, tp=other)

    for d in range(1, nchip):
        @pl.when(chunk + d < nchip)
        def _(d=d):
            kv_along(d).start()
    kv_partner(chunk).start()

    @pl.when(core == 0)
    def _():
        kv_copy(2, chunk, par, s, seq=sibling).start()

    row_i = lax.broadcasted_iota(jnp.int32, (rows, rows), 0)
    col_i = lax.broadcasted_iota(jnp.int32, (rows, rows), 1)
    causal = row_i >= col_i
    head_i = lax.broadcasted_iota(jnp.int32, (nheads, rows), 0)

    def head_rows(ref):
        out = jnp.zeros((nheads, rows), F32)
        for h in range(nheads):
            out = jnp.where(head_i == h, ref[h], out)
        return out

    wide = nheads * 64
    eb64 = jnp.where(
        lax.broadcasted_iota(jnp.int32, (nheads, wide), 1) // 64
        == lax.broadcasted_iota(jnp.int32, (nheads, wide), 0), 1.0, 0.0,
    ).astype(F32)
    eb128 = jnp.where(
        lax.broadcasted_iota(jnp.int32, (nheads, nheads * 128), 1) // 128
        == lax.broadcasted_iota(jnp.int32, (nheads, nheads * 128), 0), 1.0, 0.0,
    ).astype(F32)

    loads[2].wait()
    zdt = dt_v[...] + head_rows(bias_s)
    dt = jnp.maximum(zdt, 0.0) + jnp.log1p(jnp.exp(-jnp.abs(zdt)))
    sig_z = 1.0 / (1.0 + jnp.exp(-zdt))
    ea = jnp.exp(head_rows(alog_s))
    rate = dt * ea
    cum = mm(rate, jnp.where(row_i <= col_i, 1.0, 0.0).astype(F32), HIGH)
    cum_last = jnp.broadcast_to(cum[:, rows - 1:rows], (nheads, rows))
    cl_all[s] = cum_last

    def cl_copy(d, to):
        return rcopy(cl_all.at[s], cl_all.at[s], cl_ss.at[d], cl_rs.at[s], seq=to)

    for d in range(1, nseq):
        cl_copy(d, lax.rem(s + d, nseq)).start()

    ecum = jnp.exp(-cum)
    w2 = dt * jnp.exp(-(cum_last - cum))
    ecx[...] = mm_tn(ecum, eb64, HIGH)
    w2x[...] = mm_tn(w2, eb64, HIGH)
    cum_b = mm_tn(cum, eb128, HIGH)

    loads[3].wait()
    loads[4].wait()
    gate = gate_v[...].astype(F32)
    cot = cot_v[...].astype(F32)
    sig = 1.0 / (1.0 + jnp.exp(-gate))
    gy[...] = cot * gate * sig
    dsc[...] = cot * sig * (1.0 + gate * (1.0 - sig))
    loads[5].wait()
    gye = (gy[...] * ecx[...]).astype(BF16)
    es_send[...] = mm_tn(gye, read_v[...]).astype(BF16)

    def all_to_all(send, recv, ss, rs):
        def copy(d):
            to = lax.rem(s + d, nseq)
            return rcopy(seq_block(send, to, 64), recv.at[s], ss.at[d], rs.at[s], seq=to)
        for d in range(1, nseq):
            copy(d).start()
        recv[s] = send[pl.ds(pl.multiple_of(s * 64, 64), 64), :]
        return copy

    loads[6].wait()
    cb = mm_nt(read_v[...], write_v[...])
    lane_lo = lax.broadcasted_iota(jnp.int32, (rows, 128), 1) < 64
    skip_row = jnp.zeros((1, wide), F32)
    lane_head = lax.broadcasted_iota(jnp.int32, (1, wide), 1) // 64
    for h in range(nheads):
        skip_row = jnp.where(lane_head == h, skip_s[h], skip_row)
    for p in range(nheads // 2):
        lanes = slice(128 * p, 128 * p + 128)
        ws = []
        for c in range(2):
            h = 2 * p + c
            gap = cum_b[:, 128 * h:128 * h + 128] - cum[h:h + 1, :]
            dtl = jnp.where(causal, jnp.exp(-jnp.maximum(gap, 0.0)), 0.0) * dt[h:h + 1, :]
            dtl_b[p, 128 * c:128 * c + 128, :] = dtl
            ws.append((dtl * cb).astype(BF16))
        gp = gy[:, lanes]
        gym = jnp.concatenate([jnp.where(lane_lo, gp, 0.0), jnp.where(lane_lo, 0.0, gp)], axis=0).astype(BF16)
        gym_b[p] = gym
        w_b[p] = jnp.concatenate(ws, axis=1)
        dx[:, lanes] = mm_tn(jnp.concatenate(ws, axis=0), gym) + skip_row[:, lanes] * gp

    if len(rounds) > 1:
        hear(0)
        tell(1)

    for d in (1, 3, 2) if nchip == 4 else range(1, nchip):
        @pl.when(chunk >= d)
        def _(d=d):
            y = chunk - d
            kv_copy(0, 0, par, 2 * y + core, tp=other).wait_recv()
            kv_partner(y).start()
            kv_copy(2, y, par, 2 * y + core, seq=sibling).start()

    es_copy = all_to_all(es_send, es_recv, es_ss, es_rs)

    def wait_from(make, skip_self=True):
        for d in range(1, nseq):
            make(lax.rem(s + d, nseq)).wait_recv()

    def from_partner(y):
        kv_copy(0, 0, 1 - par, 2 * y + core, tp=other).wait_recv()

        @pl.when(jnp.logical_or(y < chunk, core == 0))
        def _():
            kv_copy(3, y, 1 - par, 2 * y + core, seq=sibling).start()

    from_partner(chunk)
    for d in (1, 3, 2) if nchip == 4 else range(1, nchip):
        @pl.when(chunk >= d)
        def _(d=d):
            from_partner(chunk - d)

    if len(rounds) > 2:
        hear(1)
        tell(2)

    loads[7].wait()
    for p in range(nq):
        q_st[128 * p:128 * p + 128, :] = q_v[:, 128 * p:128 * p + 128]
        q_t[:, 128 * p:128 * p + 128] = q_v[:, 128 * p:128 * p + 128].T
    m_buf[...] = jnp.full((nq * rows, 128), NEG_FILL, F32)
    l_buf[...] = jnp.zeros((nq * rows, 128), F32)
    acc[...] = jnp.zeros((nq * rows, 128), F32)

    def scores(i, carry):
        @pl.when(jnp.logical_or(i < chunk, core == 1))
        def _():
            for p in range(2):
                kv_copy(0, 0, p, 2 * i + 1 - core, tp=other).wait_recv()

        lo = jnp.concatenate([kv_buf[0, 2 * i], kv_buf[0, 2 * i + 1]], axis=1)
        hi = jnp.concatenate([kv_buf[1, 2 * i], kv_buf[1, 2 * i + 1]], axis=1)
        kk = jnp.concatenate([lo[:64], hi[:64]], axis=0)
        kf[i] = kk
        vf[i] = jnp.concatenate([lo[64:], hi[64:]], axis=0)
        allowed = (
            i * 256 + lax.broadcasted_iota(jnp.int32, (rows, 256), 1)
            <= s * rows + lax.broadcasted_iota(jnp.int32, (rows, 256), 0)
        )
        for p in range(nq):
            r = slice(rows * p, rows * p + rows)
            sc = jnp.where(allowed, mm(q_st[r, :], kk) * scale, NEG_FILL)
            s_buf[i, r, :] = sc
            m_buf[r, :] = jnp.maximum(m_buf[r, :], jnp.maximum(sc[:, :128], sc[:, 128:]))
        return carry

    lax.fori_loop(0, chunk + 1, scores, 0)
    wait_from(lambda j: rcopy(cl_all.at[j], cl_all.at[j], cl_ss.at[0], cl_rs.at[j], seq=j))
    wait_from(lambda j: rcopy(es_recv.at[j], es_recv.at[j], es_ss.at[0], es_rs.at[j], seq=j))

    def back_copy(out, recv, ss, rs, i):
        here = seq_block(recv, s, 64)
        return rcopy(out.at[i], here, ss.at[i], rs.at[s], seq=i)

    own_head = pl.ds(pl.multiple_of(s * 64, 64), 64)

    def send_back(out, recv, ss, rs, i):
        @pl.when(s != i)
        def _():
            back_copy(out, recv, ss, rs, i).start()

        @pl.when(s == i)
        def _():
            recv[own_head, :] = out[i]

    state = jnp.zeros((64, 128), F32)
    for i in reversed(range(nseq)):
        es_out[i] = state.astype(BF16)
        send_back(es_out, ex_recv, ex_ss, ex_rs, i)
        state = es_recv[i].astype(F32) + jnp.exp(-cl_all[i, pl.ds(s, 1), :]) * state

    m_buf[...] = jnp.broadcast_to(jnp.max(m_buf[...], axis=1, keepdims=True), (nq * rows, 128))

    def weights(i, carry):
        vv = vf[i]
        for p in range(nq):
            r = slice(rows * p, rows * p + rows)
            m = m_buf[r, :]
            e = jnp.exp(s_buf[i, r, :] - jnp.concatenate([m, m], axis=1))
            s_buf[i, r, :] = e
            l_buf[r, :] += e[:, :128] + e[:, 128:]
            acc[r, :] += mm_nt(e.astype(BF16), vv)
        return carry

    lax.fori_loop(0, chunk + 1, weights, 0)
    total = jnp.sum(l_buf[...], axis=1, keepdims=True)
    inv = jnp.broadcast_to(1.0 / total, (nq * rows, 128))
    l_buf[...] = inv
    acc[...] = acc[...] * inv
    for p in range(nq):
        x_v[:, 128 * p:128 * p + 128] = acc[128 * p:128 * p + 128, :]

    xw = (x_v[...] * w2x[...]).astype(BF16)
    fs_send[...] = mm_tn(xw, write_v[...]).astype(BF16)
    fs_copy = all_to_all(fs_send, fs_recv, fs_ss, fs_rs)

    m_sum = jnp.zeros((rows, rows), F32)
    col_r = jnp.zeros((nheads, rows), F32)
    row_r = jnp.zeros((nheads, rows), F32)
    ones8 = jnp.ones((8, 128), F32)
    for p in range(nheads // 2):
        lanes = slice(128 * p, 128 * p + 128)
        xp = x_v[:, lanes]
        g = mm_nt(gym_b[p], xp.astype(BF16))
        mp = dtl_b[p] * g
        m_sum = m_sum + mp[:rows] + mp[rows:]
        r0 = mp[:rows] * cb
        r1 = mp[rows:] * cb
        rs = mm_nt(ones8, jnp.concatenate([r0, r1], axis=0), HIGH)
        col_r = jnp.where(head_i == 2 * p, jnp.sum(r0, axis=0, keepdims=True), col_r)
        col_r = jnp.where(head_i == 2 * p + 1, jnp.sum(r1, axis=0, keepdims=True), col_r)
        row_r = jnp.where(head_i == 2 * p, rs[0:1, :rows], row_r)
        row_r = jnp.where(head_i == 2 * p + 1, rs[0:1, rows:], row_r)

    wait_from(lambda j: rcopy(fs_recv.at[j], fs_recv.at[j], fs_ss.at[0], fs_rs.at[j], seq=j))
    state = jnp.zeros((64, 128), F32)
    for i in range(nseq):
        fs_out[i] = state.astype(BF16)
        send_back(fs_out, fi_recv, fi_ss, fi_rs, i)
        state = fs_recv[i].astype(F32) + jnp.exp(-cl_all[i, pl.ds(s, 1), :]) * state

    wait_from(lambda j: rcopy(seq_block(ex_recv, j, 64), seq_block(ex_recv, j, 64), ex_ss.at[0], ex_rs.at[j], seq=j))
    exit_g = ex_recv[...]
    dx_exit = mm_nt(write_v[...], exit_g) * w2x[...]
    r_s = mm_nt(eb64, x_v[...] * dx_exit, HIGH)
    gyx = mm_nt(eb64, x_v[...] * gy[...], HIGH)
    dx[...] = dx[...] + dx_exit
    grad_w = mm_tn(m_sum.astype(BF16), read_v[...]) + mm(xw, exit_g)
    gw_send[...] = grad_w.astype(BF16)

    part = 2 * rows // ntp

    def p1_copy(send, o, odd):
        return rcopy(send.at[pl.ds(part * o, part)], ps_recv.at[z], p1_ss.at[odd, o], p1_rs.at[z], tp=2 * o + odd)

    def p1_start(send, odd):
        for o in range(ntp // 2):
            @pl.when(z != 2 * o + odd)
            def _(o=o):
                p1_copy(send, o, odd).start()

            @pl.when(z == 2 * o + odd)
            def _(o=o):
                ps_recv[z] = send[part * o:part * o + part, :]

    if rounds:
        hear(len(rounds) - 1)
    p1_start(gw_send, 1)

    for p in range(nq):
        r = slice(rows * p, rows * p + rows)
        ga = dx[:, 128 * p:128 * p + 128]
        gl_st[r, :] = ga.astype(BF16)
        gl_t[:, r] = ga.astype(BF16).T
        delta_b[r, :] = jnp.broadcast_to(
            jnp.sum(ga * x_v[:, 128 * p:128 * p + 128], axis=1, keepdims=True), (rows, 128)
        )
    acc[...] = jnp.zeros((nq * rows, 128), F32)

    def sib_copy(i):
        return rcopy(
            kg_send.at[1 - core, pl.ds(2 * i, 2)], kg_sib.at[i], sib_ss.at[i], sib_rs.at[i], seq=sibling
        )

    def kg_copy(j):
        return rcopy(kg_send.at[core, j], kg_recv.at[par, chunk], kg_ss.at[j], kg_rs.at[par, chunk], seq=j, tp=base + core)

    def kg_mine(j):
        return jnp.logical_and(j == s, par == core)

    def backward(i, carry):
        kk = kf[i]
        vv = vf[i]
        gk = jnp.zeros((128, 256), F32)
        gv = jnp.zeros((128, 256), F32)
        for p in range(nq):
            r = slice(rows * p, rows * p + rows)
            iv = l_buf[r, :]
            de = delta_b[r, :]
            pr = s_buf[i, r, :] * jnp.concatenate([iv, iv], axis=1)
            ds = (pr * (mm(gl_st[r, :], vv) - jnp.concatenate([de, de], axis=1))).astype(BF16)
            acc[r, :] += mm_nt(ds, kk)
            gv = gv + mm(gl_t[:, r], pr.astype(BF16))
            gk = gk + mm(q_t[:, r], ds)
        gk = (gk * scale).astype(BF16)
        gv = gv.astype(BF16)
        for c in range(2):
            for p in range(2):
                kg_send[p, 2 * i + c] = jnp.concatenate(
                    [gk[64 * p:64 * p + 64, 128 * c:128 * c + 128], gv[64 * p:64 * p + 64, 128 * c:128 * c + 128]], axis=0
                )
        sib_copy(i).start()
        return carry

    lax.fori_loop(0, chunk + 1, backward, 0)
    for p in range(nq):
        gq_o[:, 128 * p:128 * p + 128] = acc[128 * p:128 * p + 128, :] * scale
    put(gq_o, gq_hbm.at[0])
    wait_from(lambda j: rcopy(seq_block(fi_recv, j, 64), seq_block(fi_recv, j, 64), fi_ss.at[0], fi_rs.at[j], seq=j))
    entry = fi_recv[...]
    gye = (gy[...] * ecx[...]).astype(BF16)
    grad_r = mm(m_sum.astype(BF16), write_v[...]) + mm(gye, entry)
    gr_send[...] = grad_r.astype(BF16)
    p1_start(gr_send, 0)

    def kg_join(i, carry):
        sib_copy(i).wait()
        both = pl.ds(2 * i, 2)
        kg_send[core, both] = (kg_send[core, both].astype(F32) + kg_sib[i].astype(F32)).astype(BF16)
        for c in range(2):
            j = 2 * i + c

            @pl.when(jnp.logical_not(kg_mine(j)))
            def _(j=j):
                kg_copy(j).start()
        return carry

    lax.fori_loop(0, chunk + 1, kg_join, 0)

    @pl.when(par == core)
    def _():
        kg_recv[par, chunk] = kg_send[core, s]

    y_ent = mm_nt(read_v[...], entry) * ecx[...]
    q_sum = mm_nt(eb64, gy[...] * y_ent, HIGH)
    for p in range(nheads // 2):
        lanes = slice(128 * p, 128 * p + 128)
        xp = x_v[:, lanes]
        xm = jnp.concatenate([jnp.where(lane_lo, xp, 0.0), jnp.where(lane_lo, 0.0, xp)], axis=0).astype(BF16)
        y = mm(w_b[p], xm) + y_ent[:, lanes] + skip_row[:, lanes] * xp
        gg_o[:, lanes] = dsc[:, lanes] * y
    put(gg_o, gg_hbm.at[0])

    es_prod = exit_g.astype(F32) * entry.astype(F32)
    c_h = jnp.sum(mm(eb64, es_prod, HIGH), axis=1, keepdims=True) * jnp.exp(-cum_last)
    tail = jnp.where(row_i >= col_i, 1.0, 0.0).astype(F32)
    before = jnp.where(row_i < col_i, 1.0, 0.0).astype(F32)
    drate = mm(col_r - row_r - q_sum, tail, HIGH) - mm(r_s, before, HIGH) - c_h
    ddt = (col_r + r_s) / dt + drate * ea
    draw = ddt * sig_z
    gdt_o[...] = draw
    put(gdt_o, gdt_hbm.at[0])

    lane8 = lax.broadcasted_iota(jnp.int32, (nheads, 128), 1)
    pp_all[s] = jnp.where(
        lane8 == 0, jnp.sum(drate * rate, axis=1, keepdims=True),
        jnp.where(
            lane8 == 1, jnp.sum(gyx, axis=1, keepdims=True),
            jnp.where(lane8 == 2, jnp.sum(draw, axis=1, keepdims=True), 0.0),
        ),
    )

    def pa_copy(d):
        return rcopy(pp_all.at[s], pp_all.at[s], pa_ss.at[d], pa_rs.at[s], seq=lax.rem(s + d, nseq))

    for d in range(1, nseq):
        pa_copy(d).start()

    for d in range(1, ntp):
        j = lax.rem(z + d, ntp)
        rcopy(ps_recv.at[j], ps_recv.at[j], p1_ss.at[0, 0], p1_rs.at[j], tp=j).wait_recv()
    red = ps_recv[0].astype(F32)
    for j in range(1, ntp):
        red = red + ps_recv[j].astype(F32)
    ps_out[z] = red.astype(BF16)

    def p2_copy(d):
        return rcopy(ps_out.at[z], ps_out.at[z], p2_ss.at[d], p2_rs.at[z], tp=lax.rem(z + d, ntp))

    for d in range(1, ntp):
        p2_copy(d).start()

    wait_from(lambda j: rcopy(pp_all.at[j], pp_all.at[j], pa_ss.at[0], pa_rs.at[j], seq=j))
    pd = pp_all[0]
    for j in range(1, nseq):
        pd = pd + pp_all[j]
    pd_all[x] = pd

    def pb_copy(d):
        return rcopy(pd_all.at[x], pd_all.at[x], pb_ss.at[d], pb_rs.at[x], dp=lax.rem(x + d, ndp))

    for d in range(1, ndp):
        pb_copy(d).start()

    def kg_add(y, total):
        for p in range(2):
            @pl.when(jnp.logical_or(y != chunk, jnp.logical_or(p != par, par != core)))
            def _(p=p):
                rcopy(kg_recv.at[p, y], kg_recv.at[p, y], kg_ss.at[0], kg_rs.at[p, y], tp=other).wait_recv()
        return total + kg_recv[0, y].astype(F32) + kg_recv[1, y].astype(F32)

    kg = lax.fori_loop(chunk, nchip, kg_add, jnp.zeros((rows, 128), F32))
    gk_o[...] = kg[:64]
    gv_o[...] = kg[64:]
    put(gk_o, gk_hbm.at[0])
    put(gv_o, gv_hbm.at[0])

    for d in range(1, ndp):
        j = lax.rem(x + d, ndp)
        rcopy(pd_all.at[j], pd_all.at[j], pb_ss.at[0], pb_rs.at[j], dp=j).wait_recv()
    pd = pd_all[0]
    for j in range(1, ndp):
        pd = pd + pd_all[j]
    pf[...] = pd
    put(pf, pf_hbm)

    for d in range(1, ntp):
        j = lax.rem(z + d, ntp)
        rcopy(ps_out.at[j], ps_out.at[j], p2_ss.at[0], p2_rs.at[j], tp=j).wait_recv()
    for o in range(ntp // 2):
        gw_o[part * o:part * o + part, :] = ps_out[2 * o + 1].astype(F32)
        gr_o[part * o:part * o + part, :] = ps_out[2 * o].astype(F32)
    put(gw_o, gw_hbm.at[0])
    put(gr_o, gr_hbm.at[0])

    for d in range(1, nchip):
        @pl.when(chunk + d < nchip)
        def _(d=d):
            kv_along(d).wait_send()
    for y in range(nchip):
        @pl.when(y <= chunk)
        def _(y=y):
            kv_partner(y).wait_send()

        @pl.when(jnp.logical_or(y < chunk, jnp.logical_and(y == chunk, core == 0)))
        def _(y=y):
            kv_copy(2, y, par, 2 * y + core, seq=sibling).wait_send()
            kv_copy(3, y, 1 - par, 2 * y + core, seq=sibling).wait_send()
    for d in range(1, nseq):
        cl_copy(d, lax.rem(s + d, nseq)).wait_send()
        es_copy(d).wait_send()
        fs_copy(d).wait_send()
        pa_copy(d).wait_send()
    for i in range(nseq):
        @pl.when(s != i)
        def _(i=i):
            back_copy(es_out, ex_recv, ex_ss, ex_rs, i).wait_send()
            back_copy(fs_out, fi_recv, fi_ss, fi_rs, i).wait_send()

        @pl.when(jnp.logical_and(i <= 2 * chunk + 1, jnp.logical_not(kg_mine(i))))
        def _(i=i):
            kg_copy(i).wait_send()
    for d in range(1, ntp):
        p2_copy(d).wait_send()
    for o in range(ntp // 2):
        for odd, send in ((1, gw_send), (0, gr_send)):
            @pl.when(z != 2 * o + odd)
            def _(o=o, odd=odd, send=send):
                p1_copy(send, o, odd).wait_send()
    for d in range(1, ndp):
        pb_copy(d).wait_send()
    for copy in outs:
        copy.wait()


def body(
    dims, query_rows, key_rows, value_rows, gate_rows, write_vec, read_vec, dt_raw, a_log, skip_gain, dt_bias, out_grad
):
    nseq, ntp, ndp, nheads, nq = dims
    rows = 128
    wide = nheads * 64
    dma = pltpu.SemaphoreType.DMA

    def vm(shape, kind=F32):
        return pltpu.VMEM(shape, kind)

    any_spec = pl.BlockSpec(memory_space=pl.ANY)
    smem_spec = pl.BlockSpec(memory_space=pltpu.SMEM)
    outs = (
        (1, rows, wide), (1, 64, rows), (1, 64, rows), (1, rows, wide), (1, rows, 128), (1, rows, 128),
        (1, nheads, rows), (nheads, 128),
    )
    tall = nq * rows
    scratch = [
        vm((rows, wide), BF16), vm((64, rows), BF16), vm((64, rows), BF16), vm((rows, wide), BF16),
        vm((rows, 128), BF16), vm((rows, 128), BF16), vm((nheads, rows)), vm((rows, wide), BF16),
        vm((2, nseq, 128, rows), BF16), vm((nseq // 2, 128, 2 * rows), BF16), vm((nseq // 2, 128, 2 * rows), BF16),
        vm((tall, 128), BF16), vm((128, tall), BF16), vm((nseq // 2, tall, 256)), vm((tall, 128)), vm((tall, 128)), vm((tall, 128)),
        vm((tall, 128), BF16), vm((128, tall), BF16), vm((tall, 128)),
        vm((rows, wide)), vm((rows, wide)), vm((rows, wide)), vm((rows, wide)), vm((rows, wide)), vm((rows, wide)),
        vm((nheads // 2, 2 * rows, rows)), vm((nheads // 2, rows, 2 * rows), BF16),
        vm((nheads // 2, 2 * rows, 128), BF16),
        vm((nseq, nheads, 128)),
        vm((wide, 128), BF16), vm((nseq, 64, 128), BF16), vm((nseq, 64, 128), BF16), vm((wide, 128), BF16),
        vm((wide, 128), BF16), vm((nseq, 64, 128), BF16), vm((nseq, 64, 128), BF16), vm((wide, 128), BF16),
        vm((2, nseq, 128, rows), BF16), vm((nseq // 2, 2, 128, rows), BF16), vm((2, nseq // 2, 128, rows), BF16),
        vm((rows, 128), BF16), vm((rows, 128), BF16),
        vm((ntp, 2 * rows // ntp, 128), BF16), vm((ntp, 2 * rows // ntp, 128), BF16),
        vm((nseq, nheads, 128)), vm((ndp, nheads, 128)),
        vm((rows, wide)), vm((64, rows)), vm((64, rows)), vm((rows, wide)), vm((rows, 128)), vm((rows, 128)),
        vm((nheads, rows)), vm((nheads, 128)),
        pltpu.SemaphoreType.REGULAR((4,)), dma((8,)), dma((8,)), dma((4, max(nseq // 2, 4))), dma((2, nseq)), dma((nseq,)), dma((nseq,)),
        dma((nseq,)), dma((nseq,)), dma((nseq,)), dma((nseq,)),
        dma((nseq,)), dma((nseq,)), dma((nseq,)), dma((nseq,)),
        dma((nseq // 2,)), dma((nseq // 2,)), dma((nseq,)), dma((2, nseq // 2)), dma((2, ntp)), dma((ntp,)), dma((ntp,)), dma((ntp,)),
        dma((nseq,)), dma((nseq,)), dma((ndp,)), dma((ndp,)),
    ]
    results = pl.pallas_call(
        functools.partial(kernel, dims),
        out_shape=tuple(jax.ShapeDtypeStruct(o, F32) for o in outs),
        in_specs=[any_spec] * 8 + [smem_spec] * 3,
        out_specs=tuple([any_spec] * 8),
        scratch_shapes=scratch,
        compiler_params=pltpu.CompilerParams(
            collective_id=0, has_side_effects=True, vmem_limit_bytes=VMEM
        ),
    )(
        query_rows, jnp.swapaxes(key_rows, 1, 2), jnp.swapaxes(value_rows, 1, 2), gate_rows, write_vec, read_vec, dt_raw,
        out_grad, a_log, skip_gain, dt_bias,
    )
    per_head = jax.ShapeDtypeStruct((nheads,), F32)
    written = pl.pallas_call(
        functools.partial(write_out, nheads),
        out_shape=tuple([jax.ShapeDtypeStruct(o, F32) for o in outs[:7]] + [per_head] * 3),
        in_specs=[any_spec] * 8,
        out_specs=tuple([any_spec] * 7 + [smem_spec] * 3),
        scratch_shapes=[dma((8,)), dma((8,)), pltpu.SMEM((nheads, 128), F32)] + [vm(o) for o in outs[:7]],
        compiler_params=pltpu.CompilerParams(vmem_limit_bytes=VMEM),
    )(*results)
    return (
        written[0], jnp.swapaxes(written[1], 1, 2), jnp.swapaxes(written[2], 1, 2), *written[3:],
    )


def write_out(nheads, *refs):
    sources, targets, (load_sem, store_sem, small), staged = refs[:8], refs[8:18], refs[18:21], refs[21:]
    loads = [pltpu.make_async_copy(sources[7], small, load_sem.at[7])]
    loads += [pltpu.make_async_copy(sources[i], staged[i], load_sem.at[i]) for i in range(7)]
    for copy in loads:
        copy.start()
    stores = []
    for i in range(7):
        loads[1 + i].wait()
        stores.append(pltpu.make_async_copy(staged[i], targets[i], store_sem.at[i]))
        stores[i].start()
    loads[0].wait()
    for h in range(nheads):
        for i in range(3):
            targets[7 + i][h] = small[h, i]
    for copy in stores:
        copy.wait()


def solution(mesh):
    dims = (mesh.shape["seq"], mesh.shape["tp"], mesh.shape["dp"], 8, 4)
    wide = P("dp", "seq", "tp")
    shared = P("dp", "seq", None)
    steps = P("dp", "tp", "seq")
    head = P("tp")
    return jax.shard_map(
        functools.partial(body, dims),
        mesh=mesh,
        in_specs=(wide, wide, wide, wide, shared, shared, steps, head, head, head, wide),
        out_specs=(wide, wide, wide, wide, shared, shared, steps, head, head, head),
        check_vma=False,
    )
```

```python
import functools

import jax
import jax.numpy as jnp
from jax import lax
from jax.experimental import pallas as pl
from jax.experimental.pallas import tpu as pltpu
from jax.sharding import PartitionSpec as P

HIGH = lax.Precision.HIGHEST
MESH = pl.DeviceIdType.MESH
F32 = jnp.float32
BF16 = jnp.bfloat16
NEG_FILL = -1e30
VMEM = 40 * 1024 * 1024


def mm(a, b, precision=None):
    return lax.dot_general(a, b, (((1,), (0,)), ((), ())), precision=precision, preferred_element_type=F32)


def mm_nt(a, b, precision=None):
    return lax.dot_general(a, b, (((1,), (1,)), ((), ())), precision=precision, preferred_element_type=F32)


def mm_tn(a, b, precision=None):
    return lax.dot_general(a, b, (((0,), (0,)), ((), ())), precision=precision, preferred_element_type=F32)


def kernel(
    dims,
    q_hbm, k_hbm, v_hbm, gate_hbm, write_hbm, read_hbm, dt_hbm, cot_hbm,
    alog_s, skip_s, bias_s,
    gq_o, gk_o, gv_o, gg_o, gw_o, gr_o, gdt_o, pf,
    q_v, k_v, v_v, gate_v, write_v, read_v, dt_v, cot_v,
    kv_buf, kf, vf, q_st, q_t, s_buf, m_buf, l_buf, acc, gl_st, gl_t, delta_b,
    gy, dsc, ecx, w2x, dx, x_v, dtl_b, w_b, gym_b, gye_b, gr_part,
    cl_all, es_send, es_recv, es_out, ex_recv, fs_send, fs_recv, fs_out, fi_recv,
    kg_send, kg_sib, kg_recv, kg_sum, kg_give, kg_take, gw_send, gr_send, ps_recv, ps_out, pp_all, pd_all,
    far_sem, in_sem, kv_ss, kv_rs, cl_ss, cl_rs, es_ss, es_rs, ex_ss, ex_rs, fs_ss, fs_rs, fi_ss, fi_rs,
    sib_ss, sib_rs, kg_ss, kg_rs, kx_ss, kx_rs, p1_ss, p1_rs, p2_ss, p2_rs, pa_ss, pa_rs, pb_ss, pb_rs,
):
    nseq, ntp, ndp, nheads, nq = dims
    rows = 128
    s = lax.axis_index("seq")
    z = lax.axis_index("tp")
    x = lax.axis_index("dp")
    par = lax.rem(z, 2)
    base = z - par
    other = base + 1 - par
    chunk = lax.div(s, 2)
    core = lax.rem(s, 2)
    sibling = s + 1 - 2 * core
    nchip = nseq // 2
    scale = 128 ** (-0.5)

    def rcopy(src, dst, ssem, rsem, **where):
        return pltpu.make_async_remote_copy(
            src_ref=src, dst_ref=dst, send_sem=ssem, recv_sem=rsem, device_id=where, device_id_type=MESH
        )

    def seq_block(ref, i, n):
        return ref.at[pl.ds(pl.multiple_of(i * n, n), n)]

    loads = []
    for at, (src, dst) in enumerate((
        (k_hbm.at[0], k_v), (v_hbm.at[0], v_v), (dt_hbm.at[0], dt_v), (gate_hbm.at[0], gate_v),
        (cot_hbm.at[0], cot_v), (read_hbm.at[0], read_v), (write_hbm.at[0], write_v), (q_hbm.at[0], q_v),
    )):
        copy = pltpu.make_async_copy(src, dst, in_sem.at[at])
        copy.start()
        loads.append(copy)

    barrier = pltpu.get_barrier_semaphore()
    for d in range(1, nseq):
        to = lax.rem(s + d, nseq)
        pl.semaphore_signal(barrier, inc=1, device_id={"seq": to, "tp": z}, device_id_type=MESH)
        pl.semaphore_signal(barrier, inc=1, device_id={"seq": to, "tp": other}, device_id_type=MESH)
    for d in (1, ntp - 1):
        pl.semaphore_signal(barrier, inc=1, device_id={"tp": lax.rem(z + d, ntp)}, device_id_type=MESH)
    for d in range(1, ndp):
        pl.semaphore_signal(barrier, inc=1, device_id={"dp": lax.rem(x + d, ndp)}, device_id_type=MESH)

    loads[0].wait()
    loads[1].wait()
    kv_buf[par, s] = jnp.concatenate([k_v[...], v_v[...]], axis=0)

    @pl.when(lax.rem(s, 2) == 0)
    def _():
        kv_buf[0, s + 1] = jnp.zeros((rows, 128), BF16)
        kv_buf[1, s + 1] = jnp.zeros((rows, 128), BF16)

    pl.semaphore_wait(barrier, 2 * (nseq - 1) + 2 + (ndp - 1))

    rounds = [d for d in (1, 2, 4, 8) if d < ntp // 2]

    def tell(r):
        for d in (rounds[r], ntp - rounds[r]):
            pl.semaphore_signal(far_sem.at[r], inc=1, device_id={"tp": lax.rem(z + d, ntp)}, device_id_type=MESH)

    def hear(r):
        pl.semaphore_wait(far_sem.at[r], 2)

    if rounds:
        tell(0)

    def kv_copy(kind, at, p, j, **where):
        here = kv_buf.at[p, j]
        return rcopy(here, here, kv_ss.at[kind, at], kv_rs.at[p, j], **where)

    def kv_along(d):
        return kv_copy(0, d, par, s, seq=s + 2 * d)

    def kv_partner(y):
        return kv_copy(1, y, par, 2 * y + core, tp=other)

    for d in (2, 3, 1) if nchip == 4 else range(1, nchip):
        @pl.when(chunk + d < nchip)
        def _(d=d):
            kv_along(d).start()
    kv_partner(chunk).start()

    @pl.when(core == 0)
    def _():
        kv_copy(2, chunk, par, s, seq=sibling).start()

    row_i = lax.broadcasted_iota(jnp.int32, (rows, rows), 0)
    col_i = lax.broadcasted_iota(jnp.int32, (rows, rows), 1)
    causal = row_i >= col_i
    head_i = lax.broadcasted_iota(jnp.int32, (nheads, rows), 0)

    def head_rows(ref):
        out = jnp.zeros((nheads, rows), F32)
        for h in range(nheads):
            out = jnp.where(head_i == h, ref[h], out)
        return out

    wide = nheads * 64
    eb64 = jnp.where(
        lax.broadcasted_iota(jnp.int32, (nheads, wide), 1) // 64
        == lax.broadcasted_iota(jnp.int32, (nheads, wide), 0), 1.0, 0.0,
    ).astype(F32)
    eb128 = jnp.where(
        lax.broadcasted_iota(jnp.int32, (nheads, nheads * 128), 1) // 128
        == lax.broadcasted_iota(jnp.int32, (nheads, nheads * 128), 0), 1.0, 0.0,
    ).astype(F32)

    loads[2].wait()
    zdt = dt_v[...] + head_rows(bias_s)
    dt = jnp.maximum(zdt, 0.0) + jnp.log1p(jnp.exp(-jnp.abs(zdt)))
    sig_z = 1.0 / (1.0 + jnp.exp(-zdt))
    ea = jnp.exp(head_rows(alog_s))
    rate = dt * ea
    cum = mm(rate, jnp.where(row_i <= col_i, 1.0, 0.0).astype(F32), HIGH)
    cum_last = jnp.broadcast_to(cum[:, rows - 1:rows], (nheads, rows))
    cl_all[s] = cum_last

    def cl_copy(d, to):
        return rcopy(cl_all.at[s], cl_all.at[s], cl_ss.at[d], cl_rs.at[s], seq=to)

    for d in range(1, nseq):
        cl_copy(d, lax.rem(s + d, nseq)).start()

    ecum = jnp.exp(-cum)
    w2 = dt * jnp.exp(-(cum_last - cum))
    ecx[...] = mm_tn(ecum, eb64, HIGH)
    w2x[...] = mm_tn(w2, eb64, HIGH)
    cum_b = mm_tn(cum, eb128, HIGH)

    loads[3].wait()
    loads[4].wait()
    gate = gate_v[...].astype(F32)
    cot = cot_v[...].astype(F32)
    sig = 1.0 / (1.0 + jnp.exp(-gate))
    gy[...] = cot * gate * sig
    dsc[...] = cot * sig * (1.0 + gate * (1.0 - sig))
    loads[5].wait()
    gye = (gy[...] * ecx[...]).astype(BF16)
    gye_b[...] = gye
    es_send[...] = mm_tn(gye, read_v[...]).astype(BF16)

    def all_to_all(send, recv, ss, rs):
        def copy(d):
            to = lax.rem(s + d, nseq)
            return rcopy(seq_block(send, to, 64), recv.at[s], ss.at[d], rs.at[s], seq=to)
        for d in range(1, nseq):
            copy(d).start()
        recv[s] = send[pl.ds(pl.multiple_of(s * 64, 64), 64), :]
        return copy

    loads[6].wait()
    cb = mm_nt(read_v[...], write_v[...])
    lane_lo = lax.broadcasted_iota(jnp.int32, (rows, 128), 1) < 64
    skip_row = jnp.zeros((1, wide), F32)
    lane_head = lax.broadcasted_iota(jnp.int32, (1, wide), 1) // 64
    for h in range(nheads):
        skip_row = jnp.where(lane_head == h, skip_s[h], skip_row)
    for p in range(nheads // 2):
        lanes = slice(128 * p, 128 * p + 128)
        ws = []
        for c in range(2):
            h = 2 * p + c
            gap = cum_b[:, 128 * h:128 * h + 128] - cum[h:h + 1, :]
            dtl = jnp.where(causal, jnp.exp(-jnp.maximum(gap, 0.0)), 0.0) * dt[h:h + 1, :]
            dtl_b[p, 128 * c:128 * c + 128, :] = dtl
            ws.append((dtl * cb).astype(BF16))
        gp = gy[:, lanes]
        gym = jnp.concatenate([jnp.where(lane_lo, gp, 0.0), jnp.where(lane_lo, 0.0, gp)], axis=0).astype(BF16)
        gym_b[p] = gym
        w_b[p] = jnp.concatenate(ws, axis=1)
        dx[:, lanes] = mm_tn(jnp.concatenate(ws, axis=0), gym) + skip_row[:, lanes] * gp

    if len(rounds) > 1:
        hear(0)
        tell(1)

    for d in (1, 3, 2) if nchip == 4 else range(1, nchip):
        @pl.when(chunk >= d)
        def _(d=d):
            y = chunk - d
            kv_copy(0, 0, par, 2 * y + core, tp=other).wait_recv()
            kv_partner(y).start()
            kv_copy(2, y, par, 2 * y + core, seq=sibling).start()

    es_copy = all_to_all(es_send, es_recv, es_ss, es_rs)

    def wait_from(make, skip_self=True):
        for d in range(1, nseq):
            make(lax.rem(s + d, nseq)).wait_recv()

    def from_partner(y):
        kv_copy(0, 0, 1 - par, 2 * y + core, tp=other).wait_recv()

        @pl.when(jnp.logical_or(y < chunk, core == 0))
        def _():
            kv_copy(3, y, 1 - par, 2 * y + core, seq=sibling).start()

    def visited(turn):
        if nchip != 4:
            return chunk - turn
        return jnp.where(turn < 2, chunk - turn, turn - 2)

    from_partner(chunk)

    if len(rounds) > 2:
        hear(1)
        tell(2)

    loads[7].wait()
    for p in range(nq):
        q_st[128 * p:128 * p + 128, :] = q_v[:, 128 * p:128 * p + 128]
        q_t[:, 128 * p:128 * p + 128] = q_v[:, 128 * p:128 * p + 128].T
    m_buf[...] = jnp.full((nq * rows, 128), NEG_FILL, F32)
    l_buf[...] = jnp.zeros((nq * rows, 128), F32)
    acc[...] = jnp.zeros((nq * rows, 128), F32)

    def scores(turn, carry):
        i = visited(turn)

        @pl.when(turn < chunk)
        def _():
            from_partner(visited(turn + 1))

        @pl.when(jnp.logical_or(i < chunk, core == 1))
        def _():
            for p in range(2):
                kv_copy(0, 0, p, 2 * i + 1 - core, tp=other).wait_recv()

        lo = jnp.concatenate([kv_buf[0, 2 * i], kv_buf[0, 2 * i + 1]], axis=1)
        hi = jnp.concatenate([kv_buf[1, 2 * i], kv_buf[1, 2 * i + 1]], axis=1)
        kk = jnp.concatenate([lo[:64], hi[:64]], axis=0)
        kf[i] = kk
        vf[i] = jnp.concatenate([lo[64:], hi[64:]], axis=0)
        allowed = (
            i * 256 + lax.broadcasted_iota(jnp.int32, (rows, 256), 1)
            <= s * rows + lax.broadcasted_iota(jnp.int32, (rows, 256), 0)
        )
        for p in range(nq):
            r = slice(rows * p, rows * p + rows)
            sc = jnp.where(allowed, mm(q_st[r, :], kk) * scale, NEG_FILL)
            s_buf[i, r, :] = sc
            m_buf[r, :] = jnp.maximum(m_buf[r, :], jnp.maximum(sc[:, :128], sc[:, 128:]))
        return carry

    lax.fori_loop(0, chunk + 1, scores, 0)
    wait_from(lambda j: rcopy(cl_all.at[j], cl_all.at[j], cl_ss.at[0], cl_rs.at[j], seq=j))
    wait_from(lambda j: rcopy(es_recv.at[j], es_recv.at[j], es_ss.at[0], es_rs.at[j], seq=j))

    def back_copy(out, recv, ss, rs, i):
        here = seq_block(recv, s, 64)
        return rcopy(out.at[i], here, ss.at[i], rs.at[s], seq=i)

    own_head = pl.ds(pl.multiple_of(s * 64, 64), 64)

    def send_back(out, recv, ss, rs, i):
        @pl.when(s != i)
        def _():
            back_copy(out, recv, ss, rs, i).start()

        @pl.when(s == i)
        def _():
            recv[own_head, :] = out[i]

    state = jnp.zeros((64, 128), F32)
    for i in reversed(range(nseq)):
        es_out[i] = state.astype(BF16)
        send_back(es_out, ex_recv, ex_ss, ex_rs, i)
        state = es_recv[i].astype(F32) + jnp.exp(-cl_all[i, pl.ds(s, 1), :]) * state

    m_buf[...] = jnp.broadcast_to(jnp.max(m_buf[...], axis=1, keepdims=True), (nq * rows, 128))

    def weights(i, carry):
        vv = vf[i]
        for p in range(nq):
            r = slice(rows * p, rows * p + rows)
            m = m_buf[r, :]
            e = jnp.exp(s_buf[i, r, :] - jnp.concatenate([m, m], axis=1))
            s_buf[i, r, :] = e
            l_buf[r, :] += e[:, :128] + e[:, 128:]
            acc[r, :] += mm_nt(e.astype(BF16), vv)
        return carry

    lax.fori_loop(0, chunk + 1, weights, 0)
    total = jnp.sum(l_buf[...], axis=1, keepdims=True)
    inv = jnp.broadcast_to(1.0 / total, (nq * rows, 128))
    l_buf[...] = inv
    acc[...] = acc[...] * inv
    for p in range(nq):
        x_v[:, 128 * p:128 * p + 128] = acc[128 * p:128 * p + 128, :]

    xw = (x_v[...] * w2x[...]).astype(BF16)
    fs_send[...] = mm_tn(xw, write_v[...]).astype(BF16)
    fs_copy = all_to_all(fs_send, fs_recv, fs_ss, fs_rs)

    m_sum = jnp.zeros((rows, rows), F32)
    col_r = jnp.zeros((nheads, rows), F32)
    row_r = jnp.zeros((nheads, rows), F32)
    ones8 = jnp.ones((8, 128), F32)
    for p in range(nheads // 2):
        lanes = slice(128 * p, 128 * p + 128)
        xp = x_v[:, lanes]
        g = mm_nt(gym_b[p], xp.astype(BF16))
        mp = dtl_b[p] * g
        m_sum = m_sum + mp[:rows] + mp[rows:]
        r0 = mp[:rows] * cb
        r1 = mp[rows:] * cb
        rs = mm_nt(ones8, jnp.concatenate([r0, r1], axis=0), HIGH)
        col_r = jnp.where(head_i == 2 * p, jnp.sum(r0, axis=0, keepdims=True), col_r)
        col_r = jnp.where(head_i == 2 * p + 1, jnp.sum(r1, axis=0, keepdims=True), col_r)
        row_r = jnp.where(head_i == 2 * p, rs[0:1, :rows], row_r)
        row_r = jnp.where(head_i == 2 * p + 1, rs[0:1, rows:], row_r)

    wait_from(lambda j: rcopy(fs_recv.at[j], fs_recv.at[j], fs_ss.at[0], fs_rs.at[j], seq=j))
    state = jnp.zeros((64, 128), F32)
    for i in range(nseq):
        fs_out[i] = state.astype(BF16)
        send_back(fs_out, fi_recv, fi_ss, fi_rs, i)
        state = fs_recv[i].astype(F32) + jnp.exp(-cl_all[i, pl.ds(s, 1), :]) * state

    wait_from(lambda j: rcopy(seq_block(ex_recv, j, 64), seq_block(ex_recv, j, 64), ex_ss.at[0], ex_rs.at[j], seq=j))
    exit_g = ex_recv[...]
    dx_exit = mm_nt(write_v[...], exit_g) * w2x[...]
    r_s = mm_nt(eb64, x_v[...] * dx_exit, HIGH)
    gyx = mm_nt(eb64, x_v[...] * gy[...], HIGH)
    dx[...] = dx[...] + dx_exit
    grad_w = mm_tn(m_sum.astype(BF16), read_v[...]) + mm(xw, exit_g)
    gw_send[...] = grad_w.astype(BF16)
    gr_part[...] = mm(m_sum.astype(BF16), write_v[...])

    part = 2 * rows // ntp

    def p1_copy(send, o, odd):
        return rcopy(send.at[pl.ds(part * o, part)], ps_recv.at[z], p1_ss.at[odd, o], p1_rs.at[z], tp=2 * o + odd)

    def p1_start(send, odd):
        for o in range(ntp // 2):
            @pl.when(z != 2 * o + odd)
            def _(o=o):
                p1_copy(send, o, odd).start()

            @pl.when(z == 2 * o + odd)
            def _(o=o):
                ps_recv[z] = send[part * o:part * o + part, :]

    if rounds:
        hear(len(rounds) - 1)
    p1_start(gw_send, 1)

    for p in range(nq):
        r = slice(rows * p, rows * p + rows)
        ga = dx[:, 128 * p:128 * p + 128]
        gl_st[r, :] = ga.astype(BF16)
        gl_t[:, r] = ga.astype(BF16).T
        delta_b[r, :] = jnp.broadcast_to(
            jnp.sum(ga * x_v[:, 128 * p:128 * p + 128], axis=1, keepdims=True), (rows, 128)
        )
    acc[...] = jnp.zeros((nq * rows, 128), F32)

    def sib_copy(i):
        return rcopy(
            kg_send.at[1 - core, pl.ds(2 * i, 2)], kg_sib.at[i], sib_ss.at[i], sib_rs.at[i], seq=sibling
        )

    def kg_copy(j):
        return rcopy(kg_send.at[core, j], kg_recv.at[core, chunk], kg_ss.at[j], kg_rs.at[core, chunk], seq=j)

    def backward(i, carry):
        kk = kf[i]
        vv = vf[i]
        gk = jnp.zeros((128, 256), F32)
        gv = jnp.zeros((128, 256), F32)
        for p in range(nq):
            r = slice(rows * p, rows * p + rows)
            iv = l_buf[r, :]
            de = delta_b[r, :]
            pr = s_buf[i, r, :] * jnp.concatenate([iv, iv], axis=1)
            ds = (pr * (mm(gl_st[r, :], vv) - jnp.concatenate([de, de], axis=1))).astype(BF16)
            acc[r, :] += mm_nt(ds, kk)
            gv = gv + mm(gl_t[:, r], pr.astype(BF16))
            gk = gk + mm(q_t[:, r], ds)
        gk = (gk * scale).astype(BF16)
        gv = gv.astype(BF16)
        for c in range(2):
            for p in range(2):
                kg_send[p, 2 * i + c] = jnp.concatenate(
                    [gk[64 * p:64 * p + 64, 128 * c:128 * c + 128], gv[64 * p:64 * p + 64, 128 * c:128 * c + 128]], axis=0
                )
        sib_copy(i).start()
        return carry

    lax.fori_loop(0, chunk + 1, backward, 0)
    wait_from(lambda j: rcopy(seq_block(fi_recv, j, 64), seq_block(fi_recv, j, 64), fi_ss.at[0], fi_rs.at[j], seq=j))
    entry = fi_recv[...]
    grad_r = gr_part[...] + mm(gye_b[...], entry)
    gr_send[...] = grad_r.astype(BF16)
    p1_start(gr_send, 0)

    def kg_join(i, carry):
        sib_copy(i).wait()
        both = pl.ds(2 * i, 2)
        kg_send[core, both] = (kg_send[core, both].astype(F32) + kg_sib[i].astype(F32)).astype(BF16)
        for c in range(2):
            j = 2 * i + c

            @pl.when(j != s)
            def _(j=j):
                kg_copy(j).start()
        return carry

    lax.fori_loop(0, chunk + 1, kg_join, 0)

    kg_recv[core, chunk] = kg_send[core, s]

    for p in range(nq):
        gq_o[0, :, 128 * p:128 * p + 128] = acc[128 * p:128 * p + 128, :] * scale
    y_ent = mm_nt(read_v[...], entry) * ecx[...]
    q_sum = mm_nt(eb64, gy[...] * y_ent, HIGH)
    for p in range(nheads // 2):
        lanes = slice(128 * p, 128 * p + 128)
        xp = x_v[:, lanes]
        xm = jnp.concatenate([jnp.where(lane_lo, xp, 0.0), jnp.where(lane_lo, 0.0, xp)], axis=0).astype(BF16)
        y = mm(w_b[p], xm) + y_ent[:, lanes] + skip_row[:, lanes] * xp
        gg_o[0, :, lanes] = dsc[:, lanes] * y

    es_prod = exit_g.astype(F32) * entry.astype(F32)
    c_h = jnp.sum(mm(eb64, es_prod, HIGH), axis=1, keepdims=True) * jnp.exp(-cum_last)
    tail = jnp.where(row_i >= col_i, 1.0, 0.0).astype(F32)
    before = jnp.where(row_i < col_i, 1.0, 0.0).astype(F32)
    drate = mm(col_r - row_r - q_sum, tail, HIGH) - mm(r_s, before, HIGH) - c_h
    ddt = (col_r + r_s) / dt + drate * ea
    draw = ddt * sig_z
    gdt_o[0] = draw

    lane8 = lax.broadcasted_iota(jnp.int32, (nheads, 128), 1)
    pp_all[s] = jnp.where(
        lane8 == 0, jnp.sum(drate * rate, axis=1, keepdims=True),
        jnp.where(
            lane8 == 1, jnp.sum(gyx, axis=1, keepdims=True),
            jnp.where(lane8 == 2, jnp.sum(draw, axis=1, keepdims=True), 0.0),
        ),
    )

    def pa_copy(d):
        return rcopy(pp_all.at[s], pp_all.at[s], pa_ss.at[d], pa_rs.at[s], seq=lax.rem(s + d, nseq))

    for d in range(1, nseq):
        pa_copy(d).start()

    for d in range(1, ntp):
        j = lax.rem(z + d, ntp)
        rcopy(ps_recv.at[j], ps_recv.at[j], p1_ss.at[0, 0], p1_rs.at[j], tp=j).wait_recv()
    red = ps_recv[0].astype(F32)
    for j in range(1, ntp):
        red = red + ps_recv[j].astype(F32)
    ps_out[z] = red.astype(BF16)

    def p2_copy(d):
        return rcopy(ps_out.at[z], ps_out.at[z], p2_ss.at[d], p2_rs.at[z], tp=lax.rem(z + d, ntp))

    for d in range(1, ntp):
        p2_copy(d).start()

    wait_from(lambda j: rcopy(pp_all.at[j], pp_all.at[j], pa_ss.at[0], pa_rs.at[j], seq=j))
    pd = pp_all[0]
    for j in range(1, nseq):
        pd = pd + pp_all[j]
    pd_all[x] = pd

    def pb_copy(d):
        return rcopy(pd_all.at[x], pd_all.at[x], pb_ss.at[d], pb_rs.at[x], dp=lax.rem(x + d, ndp))

    for d in range(1, ndp):
        pb_copy(d).start()

    def kg_add(y, total):
        for c in range(2):
            @pl.when(jnp.logical_or(y != chunk, core != c))
            def _(c=c):
                rcopy(kg_recv.at[c, y], kg_recv.at[c, y], kg_ss.at[0], kg_rs.at[c, y], tp=other).wait_recv()
        return tuple(total[c] + kg_recv[c, y].astype(F32) for c in range(2))

    blank = jnp.zeros((128, rows), F32)
    half = lax.fori_loop(chunk, nchip, kg_add, (blank, blank))
    for c in range(2):
        kg_sum[c] = half[c]
    kg_give[...] = kg_sum[1 - par].astype(BF16)
    kx_copy = rcopy(kg_give, kg_take, kx_ss, kx_rs, tp=other)
    kx_copy.start()
    kx_copy.wait()
    kg = kg_sum[par] + kg_take[...].astype(F32)
    gk_o[0] = kg[:64]
    gv_o[0] = kg[64:]

    for d in range(1, ndp):
        j = lax.rem(x + d, ndp)
        rcopy(pd_all.at[j], pd_all.at[j], pb_ss.at[0], pb_rs.at[j], dp=j).wait_recv()
    pd = pd_all[0]
    for j in range(1, ndp):
        pd = pd + pd_all[j]
    pf[...] = pd

    for d in range(1, ntp):
        j = lax.rem(z + d, ntp)
        rcopy(ps_out.at[j], ps_out.at[j], p2_ss.at[0], p2_rs.at[j], tp=j).wait_recv()
    for o in range(ntp // 2):
        gw_o[0, part * o:part * o + part, :] = ps_out[2 * o + 1].astype(F32)
        gr_o[0, part * o:part * o + part, :] = ps_out[2 * o].astype(F32)

    for d in range(1, nchip):
        @pl.when(chunk + d < nchip)
        def _(d=d):
            kv_along(d).wait_send()
    for y in range(nchip):
        @pl.when(y <= chunk)
        def _(y=y):
            kv_partner(y).wait_send()

        @pl.when(jnp.logical_or(y < chunk, jnp.logical_and(y == chunk, core == 0)))
        def _(y=y):
            kv_copy(2, y, par, 2 * y + core, seq=sibling).wait_send()
            kv_copy(3, y, 1 - par, 2 * y + core, seq=sibling).wait_send()
    for d in range(1, nseq):
        cl_copy(d, lax.rem(s + d, nseq)).wait_send()
        es_copy(d).wait_send()
        fs_copy(d).wait_send()
        pa_copy(d).wait_send()
    for i in range(nseq):
        @pl.when(s != i)
        def _(i=i):
            back_copy(es_out, ex_recv, ex_ss, ex_rs, i).wait_send()
            back_copy(fs_out, fi_recv, fi_ss, fi_rs, i).wait_send()

        @pl.when(jnp.logical_and(i <= 2 * chunk + 1, i != s))
        def _(i=i):
            kg_copy(i).wait_send()
    for d in range(1, ntp):
        p2_copy(d).wait_send()
    for o in range(ntp // 2):
        for odd, send in ((1, gw_send), (0, gr_send)):
            @pl.when(z != 2 * o + odd)
            def _(o=o, odd=odd, send=send):
                p1_copy(send, o, odd).wait_send()
    for d in range(1, ndp):
        pb_copy(d).wait_send()


def body(
    dims, query_rows, key_rows, value_rows, gate_rows, write_vec, read_vec, dt_raw, a_log, skip_gain, dt_bias, out_grad
):
    nseq, ntp, ndp, nheads, nq = dims
    rows = 128
    wide = nheads * 64
    dma = pltpu.SemaphoreType.DMA

    def vm(shape, kind=F32):
        return pltpu.VMEM(shape, kind)

    any_spec = pl.BlockSpec(memory_space=pl.ANY)
    smem_spec = pl.BlockSpec(memory_space=pltpu.SMEM)
    outs = (
        (1, rows, wide), (1, 64, rows), (1, 64, rows), (1, rows, wide), (1, rows, 128), (1, rows, 128),
        (1, nheads, rows), (nheads, 128),
    )
    tall = nq * rows
    scratch = [
        vm((rows, wide), BF16), vm((64, rows), BF16), vm((64, rows), BF16), vm((rows, wide), BF16),
        vm((rows, 128), BF16), vm((rows, 128), BF16), vm((nheads, rows)), vm((rows, wide), BF16),
        vm((2, nseq, 128, rows), BF16), vm((nseq // 2, 128, 2 * rows), BF16), vm((nseq // 2, 128, 2 * rows), BF16),
        vm((tall, 128), BF16), vm((128, tall), BF16), vm((nseq // 2, tall, 256)), vm((tall, 128)), vm((tall, 128)), vm((tall, 128)),
        vm((tall, 128), BF16), vm((128, tall), BF16), vm((tall, 128)),
        vm((rows, wide)), vm((rows, wide)), vm((rows, wide)), vm((rows, wide)), vm((rows, wide)), vm((rows, wide)),
        vm((nheads // 2, 2 * rows, rows)), vm((nheads // 2, rows, 2 * rows), BF16),
        vm((nheads // 2, 2 * rows, 128), BF16), vm((rows, wide), BF16), vm((rows, 128)),
        vm((nseq, nheads, 128)),
        vm((wide, 128), BF16), vm((nseq, 64, 128), BF16), vm((nseq, 64, 128), BF16), vm((wide, 128), BF16),
        vm((wide, 128), BF16), vm((nseq, 64, 128), BF16), vm((nseq, 64, 128), BF16), vm((wide, 128), BF16),
        vm((2, nseq, 128, rows), BF16), vm((nseq // 2, 2, 128, rows), BF16), vm((2, nseq // 2, 128, rows), BF16),
        vm((2, 128, rows)), vm((128, rows), BF16), vm((128, rows), BF16),
        vm((rows, 128), BF16), vm((rows, 128), BF16),
        vm((ntp, 2 * rows // ntp, 128), BF16), vm((ntp, 2 * rows // ntp, 128), BF16),
        vm((nseq, nheads, 128)), vm((ndp, nheads, 128)),
        pltpu.SemaphoreType.REGULAR((4,)), dma((8,)), dma((4, max(nseq // 2, 4))), dma((2, nseq)), dma((nseq,)), dma((nseq,)),
        dma((nseq,)), dma((nseq,)), dma((nseq,)), dma((nseq,)),
        dma((nseq,)), dma((nseq,)), dma((nseq,)), dma((nseq,)),
        dma((nseq // 2,)), dma((nseq // 2,)), dma((nseq,)), dma((2, nseq // 2)), dma(()), dma(()), dma((2, ntp)), dma((ntp,)), dma((ntp,)), dma((ntp,)),
        dma((nseq,)), dma((nseq,)), dma((ndp,)), dma((ndp,)),
    ]
    results = pl.pallas_call(
        functools.partial(kernel, dims),
        out_shape=tuple(pltpu.VMEM(o, F32) for o in outs),
        in_specs=[any_spec] * 8 + [smem_spec] * 3,
        out_specs=tuple([pl.BlockSpec(memory_space=pltpu.VMEM)] * 8),
        scratch_shapes=scratch,
        compiler_params=pltpu.CompilerParams(
            collective_id=0, has_side_effects=True, vmem_limit_bytes=VMEM
        ),
    )(
        *(
            pltpu.with_memory_space_constraint(a, pltpu.HBM)
            for a in (
                query_rows, jnp.swapaxes(key_rows, 1, 2), jnp.swapaxes(value_rows, 1, 2), gate_rows, write_vec, read_vec,
                dt_raw, out_grad, a_log, skip_gain, dt_bias,
            )
        )
    )
    per_head = jax.ShapeDtypeStruct((nheads,), F32)
    written = pl.pallas_call(
        functools.partial(write_out, nheads),
        out_shape=tuple([jax.ShapeDtypeStruct(o, F32) for o in outs[:7]] + [per_head] * 3),
        in_specs=[any_spec] * 8,
        out_specs=tuple([any_spec] * 7 + [smem_spec] * 3),
        scratch_shapes=[dma(()), dma((8,)), pltpu.SMEM((nheads, 128), F32)],
        compiler_params=pltpu.CompilerParams(vmem_limit_bytes=VMEM),
    )(*results)
    return (
        written[0], jnp.swapaxes(written[1], 1, 2), jnp.swapaxes(written[2], 1, 2), *written[3:],
    )


def write_out(nheads, *refs):
    sources, targets, (load_sem, store_sem, small) = refs[:8], refs[8:18], refs[18:]
    load = pltpu.make_async_copy(sources[7], small, load_sem)
    load.start()
    stores = [pltpu.make_async_copy(a, b, store_sem.at[i]) for i, (a, b) in enumerate(zip(sources[:7], targets[:7]))]
    for copy in stores:
        copy.start()
    load.wait()
    for h in range(nheads):
        for i in range(3):
            targets[7 + i][h] = small[h, i]
    for copy in stores:
        copy.wait()


def solution(mesh):
    dims = (mesh.shape["seq"], mesh.shape["tp"], mesh.shape["dp"], 8, 4)
    wide = P("dp", "seq", "tp")
    shared = P("dp", "seq", None)
    steps = P("dp", "tp", "seq")
    head = P("tp")
    return jax.shard_map(
        functools.partial(body, dims),
        mesh=mesh,
        in_specs=(wide, wide, wide, wide, shared, shared, steps, head, head, head, wide),
        out_specs=(wide, wide, wide, wide, shared, shared, steps, head, head, head),
        check_vma=False,
    )
```

```python
import functools

import jax
import jax.numpy as jnp
from jax import lax
from jax.experimental import pallas as pl
from jax.experimental.pallas import tpu as pltpu
from jax.sharding import PartitionSpec as P

HIGH = lax.Precision.HIGHEST
MESH = pl.DeviceIdType.MESH
F32 = jnp.float32
BF16 = jnp.bfloat16
NEG_FILL = -1e30
VMEM = 40 * 1024 * 1024


def mm(a, b, precision=None):
    return lax.dot_general(a, b, (((1,), (0,)), ((), ())), precision=precision, preferred_element_type=F32)


def mm_nt(a, b, precision=None):
    return lax.dot_general(a, b, (((1,), (1,)), ((), ())), precision=precision, preferred_element_type=F32)


def mm_tn(a, b, precision=None):
    return lax.dot_general(a, b, (((0,), (0,)), ((), ())), precision=precision, preferred_element_type=F32)


def kernel(
    dims,
    q_hbm, k_hbm, v_hbm, gate_hbm, write_hbm, read_hbm, dt_hbm, cot_hbm,
    alog_s, skip_s, bias_s,
    gq_o, gk_o, gv_o, gg_o, gw_o, gr_o, gdt_o, pf,
    q_v, k_v, v_v, gate_v, write_v, read_v, dt_v, cot_v,
    kv_buf, kf, vf, q_st, q_t, s_buf, m_buf, l_buf, acc, gl_st, gl_t, delta_b,
    gy, dsc, ecx, w2x, dx, x_v, dtl_b, w_b, gym_b, gye_b, gr_part,
    cl_all, es_send, es_recv, es_out, ex_recv, fs_send, fs_recv, fs_out, fi_recv,
    kg_send, kg_sib, kg_recv, kg_sum, kg_give, kg_take, gw_send, gr_send, ps_recv, ps_out, pp_all, pd_all,
    far_sem, in_sem, kv_ss, kv_rs, cl_ss, cl_rs, es_ss, es_rs, ex_ss, ex_rs, fs_ss, fs_rs, fi_ss, fi_rs,
    sib_ss, sib_rs, kg_ss, kg_rs, kx_ss, kx_rs, p1_ss, p1_rs, p2_ss, p2_rs, pa_ss, pa_rs, pb_ss, pb_rs,
):
    nseq, ntp, ndp, nheads, nq = dims
    rows = 128
    s = lax.axis_index("seq")
    z = lax.axis_index("tp")
    x = lax.axis_index("dp")
    par = lax.rem(z, 2)
    base = z - par
    other = base + 1 - par
    chunk = lax.div(s, 2)
    core = lax.rem(s, 2)
    sibling = s + 1 - 2 * core
    nchip = nseq // 2
    scale = 128 ** (-0.5)

    def rcopy(src, dst, ssem, rsem, **where):
        return pltpu.make_async_remote_copy(
            src_ref=src, dst_ref=dst, send_sem=ssem, recv_sem=rsem, device_id=where, device_id_type=MESH
        )

    def seq_block(ref, i, n):
        return ref.at[pl.ds(pl.multiple_of(i * n, n), n)]

    far_first = sorted(range(1, nseq), key=lambda d: abs(d - nseq // 2))

    loads = []
    for at, (src, dst) in enumerate((
        (k_hbm.at[0], k_v), (v_hbm.at[0], v_v), (dt_hbm.at[0], dt_v), (gate_hbm.at[0], gate_v),
        (cot_hbm.at[0], cot_v), (read_hbm.at[0], read_v), (write_hbm.at[0], write_v), (q_hbm.at[0], q_v),
    )):
        copy = pltpu.make_async_copy(src, dst, in_sem.at[at])
        copy.start()
        loads.append(copy)

    barrier = pltpu.get_barrier_semaphore()
    for d in range(1, nseq):
        to = lax.rem(s + d, nseq)
        pl.semaphore_signal(barrier, inc=1, device_id={"seq": to, "tp": z}, device_id_type=MESH)
        pl.semaphore_signal(barrier, inc=1, device_id={"seq": to, "tp": other}, device_id_type=MESH)
    for d in (1, ntp - 1):
        pl.semaphore_signal(barrier, inc=1, device_id={"tp": lax.rem(z + d, ntp)}, device_id_type=MESH)
    for d in range(1, ndp):
        pl.semaphore_signal(barrier, inc=1, device_id={"dp": lax.rem(x + d, ndp)}, device_id_type=MESH)

    loads[0].wait()
    loads[1].wait()
    kv_buf[par, s] = jnp.concatenate([k_v[...], v_v[...]], axis=0)

    @pl.when(lax.rem(s, 2) == 0)
    def _():
        kv_buf[0, s + 1] = jnp.zeros((rows, 128), BF16)
        kv_buf[1, s + 1] = jnp.zeros((rows, 128), BF16)

    pl.semaphore_wait(barrier, 2 * (nseq - 1) + 2 + (ndp - 1))

    rounds = [d for d in (1, 2, 4, 8) if d < ntp // 2]

    def tell(r):
        for d in (rounds[r], ntp - rounds[r]):
            pl.semaphore_signal(far_sem.at[r], inc=1, device_id={"tp": lax.rem(z + d, ntp)}, device_id_type=MESH)

    def hear(r):
        pl.semaphore_wait(far_sem.at[r], 2)

    if rounds:
        tell(0)

    def kv_copy(kind, at, p, j, **where):
        here = kv_buf.at[p, j]
        return rcopy(here, here, kv_ss.at[kind, at], kv_rs.at[p, j], **where)

    def kv_along(d):
        return kv_copy(0, d, par, s, seq=s + 2 * d)

    def kv_partner(y):
        return kv_copy(1, y, par, 2 * y + core, tp=other)

    for d in (2, 3, 1) if nchip == 4 else range(1, nchip):
        @pl.when(chunk + d < nchip)
        def _(d=d):
            kv_along(d).start()
    kv_partner(chunk).start()

    @pl.when(core == 0)
    def _():
        kv_copy(2, chunk, par, s, seq=sibling).start()

    row_i = lax.broadcasted_iota(jnp.int32, (rows, rows), 0)
    col_i = lax.broadcasted_iota(jnp.int32, (rows, rows), 1)
    causal = row_i >= col_i
    head_i = lax.broadcasted_iota(jnp.int32, (nheads, rows), 0)

    def head_rows(ref):
        out = jnp.zeros((nheads, rows), F32)
        for h in range(nheads):
            out = jnp.where(head_i == h, ref[h], out)
        return out

    wide = nheads * 64
    eb64 = jnp.where(
        lax.broadcasted_iota(jnp.int32, (nheads, wide), 1) // 64
        == lax.broadcasted_iota(jnp.int32, (nheads, wide), 0), 1.0, 0.0,
    ).astype(F32)
    eb128 = jnp.where(
        lax.broadcasted_iota(jnp.int32, (nheads, nheads * 128), 1) // 128
        == lax.broadcasted_iota(jnp.int32, (nheads, nheads * 128), 0), 1.0, 0.0,
    ).astype(F32)

    loads[2].wait()
    zdt = dt_v[...] + head_rows(bias_s)
    dt = jnp.maximum(zdt, 0.0) + jnp.log1p(jnp.exp(-jnp.abs(zdt)))
    sig_z = 1.0 / (1.0 + jnp.exp(-zdt))
    ea = jnp.exp(head_rows(alog_s))
    rate = dt * ea
    cum = mm(rate, jnp.where(row_i <= col_i, 1.0, 0.0).astype(F32), HIGH)
    cum_last = jnp.broadcast_to(cum[:, rows - 1:rows], (nheads, rows))
    cl_all[s] = cum_last

    def cl_copy(d, to):
        return rcopy(cl_all.at[s], cl_all.at[s], cl_ss.at[d], cl_rs.at[s], seq=to)

    for d in range(1, nseq):
        cl_copy(d, lax.rem(s + d, nseq)).start()

    ecum = jnp.exp(-cum)
    w2 = dt * jnp.exp(-(cum_last - cum))
    ecx[...] = mm_tn(ecum, eb64, HIGH)
    w2x[...] = mm_tn(w2, eb64, HIGH)
    cum_b = mm_tn(cum, eb128, HIGH)

    loads[3].wait()
    loads[4].wait()
    gate = gate_v[...].astype(F32)
    cot = cot_v[...].astype(F32)
    sig = 1.0 / (1.0 + jnp.exp(-gate))
    gy[...] = cot * gate * sig
    dsc[...] = cot * sig * (1.0 + gate * (1.0 - sig))
    loads[5].wait()
    gye = (gy[...] * ecx[...]).astype(BF16)
    gye_b[...] = gye
    es_send[...] = mm_tn(gye, read_v[...]).astype(BF16)

    def all_to_all(send, recv, ss, rs):
        def copy(d):
            to = lax.rem(s + d, nseq)
            return rcopy(seq_block(send, to, 64), recv.at[s], ss.at[d], rs.at[s], seq=to)
        for d in far_first:
            copy(d).start()
        recv[s] = send[pl.ds(pl.multiple_of(s * 64, 64), 64), :]
        return copy

    loads[6].wait()
    cb = mm_nt(read_v[...], write_v[...])
    lane_lo = lax.broadcasted_iota(jnp.int32, (rows, 128), 1) < 64
    skip_row = jnp.zeros((1, wide), F32)
    lane_head = lax.broadcasted_iota(jnp.int32, (1, wide), 1) // 64
    for h in range(nheads):
        skip_row = jnp.where(lane_head == h, skip_s[h], skip_row)
    for p in range(nheads // 2):
        lanes = slice(128 * p, 128 * p + 128)
        ws = []
        for c in range(2):
            h = 2 * p + c
            gap = cum_b[:, 128 * h:128 * h + 128] - cum[h:h + 1, :]
            dtl = jnp.where(causal, jnp.exp(-jnp.maximum(gap, 0.0)), 0.0) * dt[h:h + 1, :]
            dtl_b[p, 128 * c:128 * c + 128, :] = dtl
            ws.append((dtl * cb).astype(BF16))
        gp = gy[:, lanes]
        gym = jnp.concatenate([jnp.where(lane_lo, gp, 0.0), jnp.where(lane_lo, 0.0, gp)], axis=0).astype(BF16)
        gym_b[p] = gym
        w_b[p] = jnp.concatenate(ws, axis=1)
        dx[:, lanes] = mm_tn(jnp.concatenate(ws, axis=0), gym) + skip_row[:, lanes] * gp

    if len(rounds) > 1:
        hear(0)
        tell(1)

    for d in (1, 3, 2) if nchip == 4 else range(1, nchip):
        @pl.when(chunk >= d)
        def _(d=d):
            y = chunk - d
            kv_copy(0, 0, par, 2 * y + core, tp=other).wait_recv()
            kv_partner(y).start()
            kv_copy(2, y, par, 2 * y + core, seq=sibling).start()

    es_copy = all_to_all(es_send, es_recv, es_ss, es_rs)

    def wait_from(make, skip_self=True):
        for d in range(1, nseq):
            make(lax.rem(s + d, nseq)).wait_recv()

    def from_partner(y):
        kv_copy(0, 0, 1 - par, 2 * y + core, tp=other).wait_recv()

        @pl.when(jnp.logical_or(y < chunk, core == 0))
        def _():
            kv_copy(3, y, 1 - par, 2 * y + core, seq=sibling).start()

    def visited(turn):
        if nchip != 4:
            return chunk - turn
        return jnp.where(turn < 2, chunk - turn, turn - 2)

    from_partner(chunk)

    if len(rounds) > 2:
        hear(1)
        tell(2)

    loads[7].wait()
    for p in range(nq):
        q_st[128 * p:128 * p + 128, :] = q_v[:, 128 * p:128 * p + 128]
        q_t[:, 128 * p:128 * p + 128] = q_v[:, 128 * p:128 * p + 128].T
    m_buf[...] = jnp.full((nq * rows, 128), NEG_FILL, F32)
    l_buf[...] = jnp.zeros((nq * rows, 128), F32)
    acc[...] = jnp.zeros((nq * rows, 128), F32)

    def scores(turn, carry):
        i = visited(turn)

        @pl.when(turn < chunk)
        def _():
            from_partner(visited(turn + 1))

        @pl.when(jnp.logical_or(i < chunk, core == 1))
        def _():
            for p in range(2):
                kv_copy(0, 0, p, 2 * i + 1 - core, tp=other).wait_recv()

        lo = jnp.concatenate([kv_buf[0, 2 * i], kv_buf[0, 2 * i + 1]], axis=1)
        hi = jnp.concatenate([kv_buf[1, 2 * i], kv_buf[1, 2 * i + 1]], axis=1)
        kk = jnp.concatenate([lo[:64], hi[:64]], axis=0)
        kf[i] = kk
        vf[i] = jnp.concatenate([lo[64:], hi[64:]], axis=0)
        allowed = (
            i * 256 + lax.broadcasted_iota(jnp.int32, (rows, 256), 1)
            <= s * rows + lax.broadcasted_iota(jnp.int32, (rows, 256), 0)
        )
        for p in range(nq):
            r = slice(rows * p, rows * p + rows)
            sc = jnp.where(allowed, mm(q_st[r, :], kk) * scale, NEG_FILL)
            s_buf[i, r, :] = sc
            m_buf[r, :] = jnp.maximum(m_buf[r, :], jnp.maximum(sc[:, :128], sc[:, 128:]))
        return carry

    lax.fori_loop(0, chunk + 1, scores, 0)
    wait_from(lambda j: rcopy(cl_all.at[j], cl_all.at[j], cl_ss.at[0], cl_rs.at[j], seq=j))
    wait_from(lambda j: rcopy(es_recv.at[j], es_recv.at[j], es_ss.at[0], es_rs.at[j], seq=j))

    def back_copy(out, recv, ss, rs, i):
        here = seq_block(recv, s, 64)
        return rcopy(out.at[i], here, ss.at[i], rs.at[s], seq=i)

    own_head = pl.ds(pl.multiple_of(s * 64, 64), 64)

    def send_back(out, recv, ss, rs):
        for d in far_first:
            back_copy(out, recv, ss, rs, lax.rem(s + d, nseq)).start()
        recv[own_head, :] = out[s]

    state = jnp.zeros((64, 128), F32)
    for i in reversed(range(nseq)):
        es_out[i] = state.astype(BF16)
        state = es_recv[i].astype(F32) + jnp.exp(-cl_all[i, pl.ds(s, 1), :]) * state
    send_back(es_out, ex_recv, ex_ss, ex_rs)

    m_buf[...] = jnp.broadcast_to(jnp.max(m_buf[...], axis=1, keepdims=True), (nq * rows, 128))

    def weights(i, carry):
        vv = vf[i]
        for p in range(nq):
            r = slice(rows * p, rows * p + rows)
            m = m_buf[r, :]
            e = jnp.exp(s_buf[i, r, :] - jnp.concatenate([m, m], axis=1))
            s_buf[i, r, :] = e
            l_buf[r, :] += e[:, :128] + e[:, 128:]
            acc[r, :] += mm_nt(e.astype(BF16), vv)
        return carry

    lax.fori_loop(0, chunk + 1, weights, 0)
    total = jnp.sum(l_buf[...], axis=1, keepdims=True)
    inv = jnp.broadcast_to(1.0 / total, (nq * rows, 128))
    l_buf[...] = inv
    acc[...] = acc[...] * inv
    for p in range(nq):
        x_v[:, 128 * p:128 * p + 128] = acc[128 * p:128 * p + 128, :]

    xw = (x_v[...] * w2x[...]).astype(BF16)
    fs_send[...] = mm_tn(xw, write_v[...]).astype(BF16)
    fs_copy = all_to_all(fs_send, fs_recv, fs_ss, fs_rs)

    m_sum = jnp.zeros((rows, rows), F32)
    col_r = jnp.zeros((nheads, rows), F32)
    row_r = jnp.zeros((nheads, rows), F32)
    ones8 = jnp.ones((8, 128), F32)
    for p in range(nheads // 2):
        lanes = slice(128 * p, 128 * p + 128)
        xp = x_v[:, lanes]
        g = mm_nt(gym_b[p], xp.astype(BF16))
        mp = dtl_b[p] * g
        m_sum = m_sum + mp[:rows] + mp[rows:]
        r0 = mp[:rows] * cb
        r1 = mp[rows:] * cb
        rs = mm_nt(ones8, jnp.concatenate([r0, r1], axis=0), HIGH)
        col_r = jnp.where(head_i == 2 * p, jnp.sum(r0, axis=0, keepdims=True), col_r)
        col_r = jnp.where(head_i == 2 * p + 1, jnp.sum(r1, axis=0, keepdims=True), col_r)
        row_r = jnp.where(head_i == 2 * p, rs[0:1, :rows], row_r)
        row_r = jnp.where(head_i == 2 * p + 1, rs[0:1, rows:], row_r)

    wait_from(lambda j: rcopy(fs_recv.at[j], fs_recv.at[j], fs_ss.at[0], fs_rs.at[j], seq=j))
    state = jnp.zeros((64, 128), F32)
    for i in range(nseq):
        fs_out[i] = state.astype(BF16)
        state = fs_recv[i].astype(F32) + jnp.exp(-cl_all[i, pl.ds(s, 1), :]) * state
    send_back(fs_out, fi_recv, fi_ss, fi_rs)

    wait_from(lambda j: rcopy(seq_block(ex_recv, j, 64), seq_block(ex_recv, j, 64), ex_ss.at[0], ex_rs.at[j], seq=j))
    exit_g = ex_recv[...]
    dx_exit = mm_nt(write_v[...], exit_g) * w2x[...]
    r_s = mm_nt(eb64, x_v[...] * dx_exit, HIGH)
    gyx = mm_nt(eb64, x_v[...] * gy[...], HIGH)
    dx[...] = dx[...] + dx_exit
    grad_w = mm_tn(m_sum.astype(BF16), read_v[...]) + mm(xw, exit_g)
    gw_send[...] = grad_w.astype(BF16)
    gr_part[...] = mm(m_sum.astype(BF16), write_v[...])

    parts = ntp // 2
    part = rows // parts
    mine = lax.rem(z, parts)

    def p1_copy(send, kind, d):
        to = lax.rem(z + d, ntp)
        return rcopy(
            seq_block(send, lax.rem(to, parts), part), ps_recv.at[kind, z], p1_ss.at[kind, d], p1_rs.at[kind, z], tp=to
        )

    def p1_start(send, kind):
        for d in sorted(range(1, ntp), key=lambda d: abs(d - parts)):
            p1_copy(send, kind, d).start()
        ps_recv[kind, z] = send[pl.ds(pl.multiple_of(mine * part, part), part), :]

    reach = sorted([d for d in range(-((parts - 1) // 2), parts // 2 + 1) if d], key=lambda d: -abs(d))

    def p2_copy(kind, at):
        return rcopy(
            ps_out.at[kind, mine], ps_out.at[kind, mine], p2_ss.at[kind, at], p2_rs.at[kind, mine],
            tp=lax.rem(z + reach[at] + ntp, ntp),
        )

    def p1_finish(kind):
        for d in range(1, ntp):
            j = lax.rem(z + d, ntp)
            rcopy(ps_recv.at[kind, j], ps_recv.at[kind, j], p1_ss.at[0, 0], p1_rs.at[kind, j], tp=j).wait_recv()
        red = ps_recv[kind, 0].astype(F32)
        for j in range(1, ntp):
            red = red + ps_recv[kind, j].astype(F32)
        ps_out[kind, mine] = red.astype(BF16)
        for at in range(len(reach)):
            p2_copy(kind, at).start()

    def p2_finish(kind, out):
        for d in reach:
            c = lax.rem(z - d + ntp, parts)
            rcopy(ps_out.at[kind, c], ps_out.at[kind, c], p2_ss.at[0, 0], p2_rs.at[kind, c], tp=other).wait_recv()
        for c in range(parts):
            out[0, part * c:part * c + part, :] = ps_out[kind, c].astype(F32)

    if rounds:
        hear(len(rounds) - 1)
    p1_start(gw_send, 0)

    for p in range(nq):
        r = slice(rows * p, rows * p + rows)
        ga = dx[:, 128 * p:128 * p + 128]
        gl_st[r, :] = ga.astype(BF16)
        gl_t[:, r] = ga.astype(BF16).T
        delta_b[r, :] = jnp.broadcast_to(
            jnp.sum(ga * x_v[:, 128 * p:128 * p + 128], axis=1, keepdims=True), (rows, 128)
        )
    acc[...] = jnp.zeros((nq * rows, 128), F32)

    def sib_copy(i):
        return rcopy(
            kg_send.at[1 - core, pl.ds(2 * i, 2)], kg_sib.at[i], sib_ss.at[i], sib_rs.at[i], seq=sibling
        )

    def kg_copy(j):
        return rcopy(kg_send.at[core, j], kg_recv.at[core, chunk], kg_ss.at[j], kg_rs.at[core, chunk], seq=j)

    def backward(i, carry):
        kk = kf[i]
        vv = vf[i]
        gk = jnp.zeros((128, 256), F32)
        gv = jnp.zeros((128, 256), F32)
        for p in range(nq):
            r = slice(rows * p, rows * p + rows)
            iv = l_buf[r, :]
            de = delta_b[r, :]
            pr = s_buf[i, r, :] * jnp.concatenate([iv, iv], axis=1)
            ds = (pr * (mm(gl_st[r, :], vv) - jnp.concatenate([de, de], axis=1))).astype(BF16)
            acc[r, :] += mm_nt(ds, kk)
            gv = gv + mm(gl_t[:, r], pr.astype(BF16))
            gk = gk + mm(q_t[:, r], ds)
        gk = (gk * scale).astype(BF16)
        gv = gv.astype(BF16)
        for c in range(2):
            for p in range(2):
                kg_send[p, 2 * i + c] = jnp.concatenate(
                    [gk[64 * p:64 * p + 64, 128 * c:128 * c + 128], gv[64 * p:64 * p + 64, 128 * c:128 * c + 128]], axis=0
                )
        sib_copy(i).start()
        return carry

    lax.fori_loop(0, chunk + 1, backward, 0)
    wait_from(lambda j: rcopy(seq_block(fi_recv, j, 64), seq_block(fi_recv, j, 64), fi_ss.at[0], fi_rs.at[j], seq=j))
    entry = fi_recv[...]
    grad_r = gr_part[...] + mm(gye_b[...], entry)
    gr_send[...] = grad_r.astype(BF16)
    p1_start(gr_send, 1)

    def kg_join(i, carry):
        sib_copy(i).wait()
        both = pl.ds(2 * i, 2)
        kg_send[core, both] = (kg_send[core, both].astype(F32) + kg_sib[i].astype(F32)).astype(BF16)
        for c in range(2):
            j = 2 * i + c

            @pl.when(j != s)
            def _(j=j):
                kg_copy(j).start()
        return carry

    lax.fori_loop(0, chunk + 1, kg_join, 0)

    kg_recv[core, chunk] = kg_send[core, s]

    for p in range(nq):
        gq_o[0, :, 128 * p:128 * p + 128] = acc[128 * p:128 * p + 128, :] * scale
    y_ent = mm_nt(read_v[...], entry) * ecx[...]
    q_sum = mm_nt(eb64, gy[...] * y_ent, HIGH)
    for p in range(nheads // 2):
        lanes = slice(128 * p, 128 * p + 128)
        xp = x_v[:, lanes]
        xm = jnp.concatenate([jnp.where(lane_lo, xp, 0.0), jnp.where(lane_lo, 0.0, xp)], axis=0).astype(BF16)
        y = mm(w_b[p], xm) + y_ent[:, lanes] + skip_row[:, lanes] * xp
        gg_o[0, :, lanes] = dsc[:, lanes] * y

    es_prod = exit_g.astype(F32) * entry.astype(F32)
    c_h = jnp.sum(mm(eb64, es_prod, HIGH), axis=1, keepdims=True) * jnp.exp(-cum_last)
    tail = jnp.where(row_i >= col_i, 1.0, 0.0).astype(F32)
    before = jnp.where(row_i < col_i, 1.0, 0.0).astype(F32)
    drate = mm(col_r - row_r - q_sum, tail, HIGH) - mm(r_s, before, HIGH) - c_h
    ddt = (col_r + r_s) / dt + drate * ea
    draw = ddt * sig_z
    gdt_o[0] = draw

    lane8 = lax.broadcasted_iota(jnp.int32, (nheads, 128), 1)
    pp_all[s] = jnp.where(
        lane8 == 0, jnp.sum(drate * rate, axis=1, keepdims=True),
        jnp.where(
            lane8 == 1, jnp.sum(gyx, axis=1, keepdims=True),
            jnp.where(lane8 == 2, jnp.sum(draw, axis=1, keepdims=True), 0.0),
        ),
    )

    def pa_copy(d):
        return rcopy(pp_all.at[s], pp_all.at[s], pa_ss.at[d], pa_rs.at[s], seq=lax.rem(s + d, nseq))

    for d in far_first:
        pa_copy(d).start()

    p1_finish(0)
    p1_finish(1)

    wait_from(lambda j: rcopy(pp_all.at[j], pp_all.at[j], pa_ss.at[0], pa_rs.at[j], seq=j))
    pd = pp_all[0]
    for j in range(1, nseq):
        pd = pd + pp_all[j]
    pd_all[x] = pd

    def pb_copy(d):
        return rcopy(pd_all.at[x], pd_all.at[x], pb_ss.at[d], pb_rs.at[x], dp=lax.rem(x + d, ndp))

    for d in range(1, ndp):
        pb_copy(d).start()

    def kg_add(y, total):
        for c in range(2):
            @pl.when(jnp.logical_or(y != chunk, core != c))
            def _(c=c):
                rcopy(kg_recv.at[c, y], kg_recv.at[c, y], kg_ss.at[0], kg_rs.at[c, y], tp=other).wait_recv()
        return tuple(total[c] + kg_recv[c, y].astype(F32) for c in range(2))

    blank = jnp.zeros((128, rows), F32)
    half = lax.fori_loop(chunk, nchip, kg_add, (blank, blank))
    for c in range(2):
        kg_sum[c] = half[c]
    kg_give[...] = kg_sum[1 - par].astype(BF16)
    kx_copy = rcopy(kg_give, kg_take, kx_ss, kx_rs, tp=other)
    kx_copy.start()
    kx_copy.wait()
    kg = kg_sum[par] + kg_take[...].astype(F32)
    gk_o[0] = kg[:64]
    gv_o[0] = kg[64:]

    for d in range(1, ndp):
        j = lax.rem(x + d, ndp)
        rcopy(pd_all.at[j], pd_all.at[j], pb_ss.at[0], pb_rs.at[j], dp=j).wait_recv()
    pd = pd_all[0]
    for j in range(1, ndp):
        pd = pd + pd_all[j]
    pf[...] = pd

    p2_finish(0, gw_o)
    p2_finish(1, gr_o)

    for d in range(1, nchip):
        @pl.when(chunk + d < nchip)
        def _(d=d):
            kv_along(d).wait_send()
    for y in range(nchip):
        @pl.when(y <= chunk)
        def _(y=y):
            kv_partner(y).wait_send()

        @pl.when(jnp.logical_or(y < chunk, jnp.logical_and(y == chunk, core == 0)))
        def _(y=y):
            kv_copy(2, y, par, 2 * y + core, seq=sibling).wait_send()
            kv_copy(3, y, 1 - par, 2 * y + core, seq=sibling).wait_send()
    for d in range(1, nseq):
        cl_copy(d, lax.rem(s + d, nseq)).wait_send()
        es_copy(d).wait_send()
        fs_copy(d).wait_send()
        pa_copy(d).wait_send()
    for i in range(nseq):
        @pl.when(s != i)
        def _(i=i):
            back_copy(es_out, ex_recv, ex_ss, ex_rs, i).wait_send()
            back_copy(fs_out, fi_recv, fi_ss, fi_rs, i).wait_send()

        @pl.when(jnp.logical_and(i <= 2 * chunk + 1, i != s))
        def _(i=i):
            kg_copy(i).wait_send()
    for kind, send in ((0, gw_send), (1, gr_send)):
        for d in range(1, ntp):
            p1_copy(send, kind, d).wait_send()
        for at in range(len(reach)):
            p2_copy(kind, at).wait_send()
    for d in range(1, ndp):
        pb_copy(d).wait_send()


def body(
    dims, query_rows, key_rows, value_rows, gate_rows, write_vec, read_vec, dt_raw, a_log, skip_gain, dt_bias, out_grad
):
    nseq, ntp, ndp, nheads, nq = dims
    rows = 128
    wide = nheads * 64
    dma = pltpu.SemaphoreType.DMA

    def vm(shape, kind=F32):
        return pltpu.VMEM(shape, kind)

    any_spec = pl.BlockSpec(memory_space=pl.ANY)
    smem_spec = pl.BlockSpec(memory_space=pltpu.SMEM)
    outs = (
        (1, rows, wide), (1, 64, rows), (1, 64, rows), (1, rows, wide), (1, rows, 128), (1, rows, 128),
        (1, nheads, rows), (nheads, 128),
    )
    tall = nq * rows
    scratch = [
        vm((rows, wide), BF16), vm((64, rows), BF16), vm((64, rows), BF16), vm((rows, wide), BF16),
        vm((rows, 128), BF16), vm((rows, 128), BF16), vm((nheads, rows)), vm((rows, wide), BF16),
        vm((2, nseq, 128, rows), BF16), vm((nseq // 2, 128, 2 * rows), BF16), vm((nseq // 2, 128, 2 * rows), BF16),
        vm((tall, 128), BF16), vm((128, tall), BF16), vm((nseq // 2, tall, 256)), vm((tall, 128)), vm((tall, 128)), vm((tall, 128)),
        vm((tall, 128), BF16), vm((128, tall), BF16), vm((tall, 128)),
        vm((rows, wide)), vm((rows, wide)), vm((rows, wide)), vm((rows, wide)), vm((rows, wide)), vm((rows, wide)),
        vm((nheads // 2, 2 * rows, rows)), vm((nheads // 2, rows, 2 * rows), BF16),
        vm((nheads // 2, 2 * rows, 128), BF16), vm((rows, wide), BF16), vm((rows, 128)),
        vm((nseq, nheads, 128)),
        vm((wide, 128), BF16), vm((nseq, 64, 128), BF16), vm((nseq, 64, 128), BF16), vm((wide, 128), BF16),
        vm((wide, 128), BF16), vm((nseq, 64, 128), BF16), vm((nseq, 64, 128), BF16), vm((wide, 128), BF16),
        vm((2, nseq, 128, rows), BF16), vm((nseq // 2, 2, 128, rows), BF16), vm((2, nseq // 2, 128, rows), BF16),
        vm((2, 128, rows)), vm((128, rows), BF16), vm((128, rows), BF16),
        vm((rows, 128), BF16), vm((rows, 128), BF16),
        vm((2, ntp, 2 * rows // ntp, 128), BF16), vm((2, ntp // 2, 2 * rows // ntp, 128), BF16),
        vm((nseq, nheads, 128)), vm((ndp, nheads, 128)),
        pltpu.SemaphoreType.REGULAR((4,)), dma((8,)), dma((4, max(nseq // 2, 4))), dma((2, nseq)), dma((nseq,)), dma((nseq,)),
        dma((nseq,)), dma((nseq,)), dma((nseq,)), dma((nseq,)),
        dma((nseq,)), dma((nseq,)), dma((nseq,)), dma((nseq,)),
        dma((nseq // 2,)), dma((nseq // 2,)), dma((nseq,)), dma((2, nseq // 2)), dma(()), dma(()), dma((2, ntp)), dma((2, ntp)), dma((2, ntp)), dma((2, ntp)),
        dma((nseq,)), dma((nseq,)), dma((ndp,)), dma((ndp,)),
    ]
    results = pl.pallas_call(
        functools.partial(kernel, dims),
        out_shape=tuple(pltpu.VMEM(o, F32) for o in outs),
        in_specs=[any_spec] * 8 + [smem_spec] * 3,
        out_specs=tuple([pl.BlockSpec(memory_space=pltpu.VMEM)] * 8),
        scratch_shapes=scratch,
        compiler_params=pltpu.CompilerParams(
            collective_id=0, has_side_effects=True, vmem_limit_bytes=VMEM
        ),
    )(
        *(
            pltpu.with_memory_space_constraint(a, pltpu.HBM)
            for a in (
                query_rows, jnp.swapaxes(key_rows, 1, 2), jnp.swapaxes(value_rows, 1, 2), gate_rows, write_vec, read_vec,
                dt_raw, out_grad, a_log, skip_gain, dt_bias,
            )
        )
    )
    per_head = jax.ShapeDtypeStruct((nheads,), F32)
    written = pl.pallas_call(
        functools.partial(write_out, nheads),
        out_shape=tuple([jax.ShapeDtypeStruct(o, F32) for o in outs[:7]] + [per_head] * 3),
        in_specs=[any_spec] * 8,
        out_specs=tuple([any_spec] * 7 + [smem_spec] * 3),
        scratch_shapes=[dma(()), dma((8,)), pltpu.SMEM((nheads, 128), F32)],
        compiler_params=pltpu.CompilerParams(vmem_limit_bytes=VMEM),
    )(*results)
    return (
        written[0], jnp.swapaxes(written[1], 1, 2), jnp.swapaxes(written[2], 1, 2), *written[3:],
    )


def write_out(nheads, *refs):
    sources, targets, (load_sem, store_sem, small) = refs[:8], refs[8:18], refs[18:]
    load = pltpu.make_async_copy(sources[7], small, load_sem)
    load.start()
    stores = [pltpu.make_async_copy(a, b, store_sem.at[i]) for i, (a, b) in enumerate(zip(sources[:7], targets[:7]))]
    for copy in stores:
        copy.start()
    load.wait()
    for h in range(nheads):
        for i in range(3):
            targets[7 + i][h] = small[h, i]
    for copy in stores:
        copy.wait()


def solution(mesh):
    dims = (mesh.shape["seq"], mesh.shape["tp"], mesh.shape["dp"], 8, 4)
    wide = P("dp", "seq", "tp")
    shared = P("dp", "seq", None)
    steps = P("dp", "tp", "seq")
    head = P("tp")
    return jax.shard_map(
        functools.partial(body, dims),
        mesh=mesh,
        in_specs=(wide, wide, wide, wide, shared, shared, steps, head, head, head, wide),
        out_specs=(wide, wide, wide, wide, shared, shared, steps, head, head, head),
        check_vma=False,
    )
```

```python
import functools

import jax
import jax.numpy as jnp
from jax import lax
from jax.experimental import pallas as pl
from jax.experimental.pallas import tpu as pltpu
from jax.sharding import PartitionSpec as P

HIGH = lax.Precision.HIGHEST
MESH = pl.DeviceIdType.MESH
F32 = jnp.float32
BF16 = jnp.bfloat16
NEG_FILL = -1e30
VMEM = 40 * 1024 * 1024


def mm(a, b, precision=None):
    return lax.dot_general(a, b, (((1,), (0,)), ((), ())), precision=precision, preferred_element_type=F32)


def mm_nt(a, b, precision=None):
    return lax.dot_general(a, b, (((1,), (1,)), ((), ())), precision=precision, preferred_element_type=F32)


def mm_tn(a, b, precision=None):
    return lax.dot_general(a, b, (((0,), (0,)), ((), ())), precision=precision, preferred_element_type=F32)


def kernel(
    dims,
    q_hbm, k_hbm, v_hbm, gate_hbm, write_hbm, read_hbm, dt_hbm, cot_hbm,
    alog_s, skip_s, bias_s,
    gq_o, gk_o, gv_o, gg_o, gw_o, gr_o, gdt_o, pf,
    q_v, k_v, v_v, gate_v, write_v, read_v, dt_v, cot_v,
    kv_buf, kf, vf, q_st, q_t, s_buf, m_buf, l_buf, acc, gl_st, gl_t, delta_b,
    gy, dsc, ecx, w2x, dx, x_v, dtl_b, w_b, gym_b, gye_b, gr_part,
    cl_all, es_send, es_recv, es_out, ex_recv, fs_send, fs_recv, fs_out, fi_recv,
    kg_send, kg_sib, kg_recv, kg_sum, kg_give, kg_take, gw_send, gr_send, ps_recv, ps_out, pp_all, pd_all,
    far_sem, in_sem, kv_ss, kv_rs, cl_ss, cl_rs, es_ss, es_rs, ex_ss, ex_rs, fs_ss, fs_rs, fi_ss, fi_rs,
    sib_ss, sib_rs, kg_ss, kg_rs, kx_ss, kx_rs, p1_ss, p1_rs, p2_ss, p2_rs, pa_ss, pa_rs, pb_ss, pb_rs,
):
    nseq, ntp, ndp, nheads, nq = dims
    rows = 128
    s = lax.axis_index("seq")
    z = lax.axis_index("tp")
    x = lax.axis_index("dp")
    par = lax.rem(z, 2)
    base = z - par
    other = base + 1 - par
    chunk = lax.div(s, 2)
    core = lax.rem(s, 2)
    sibling = s + 1 - 2 * core
    nchip = nseq // 2
    scale = 128 ** (-0.5)

    def rcopy(src, dst, ssem, rsem, **where):
        return pltpu.make_async_remote_copy(
            src_ref=src, dst_ref=dst, send_sem=ssem, recv_sem=rsem, device_id=where, device_id_type=MESH
        )

    def seq_block(ref, i, n):
        return ref.at[pl.ds(pl.multiple_of(i * n, n), n)]

    far_first = sorted(range(1, nseq), key=lambda d: abs(d - nseq // 2))

    loads = []
    for at, (src, dst) in enumerate((
        (k_hbm.at[0], k_v), (v_hbm.at[0], v_v), (dt_hbm.at[0], dt_v), (gate_hbm.at[0], gate_v),
        (cot_hbm.at[0], cot_v), (read_hbm.at[0], read_v), (write_hbm.at[0], write_v), (q_hbm.at[0], q_v),
    )):
        copy = pltpu.make_async_copy(src, dst, in_sem.at[at])
        copy.start()
        loads.append(copy)

    barrier = pltpu.get_barrier_semaphore()
    for d in range(1, nseq):
        to = lax.rem(s + d, nseq)
        pl.semaphore_signal(barrier, inc=1, device_id={"seq": to, "tp": z}, device_id_type=MESH)
        pl.semaphore_signal(barrier, inc=1, device_id={"seq": to, "tp": other}, device_id_type=MESH)
    for d in (1, ntp - 1):
        pl.semaphore_signal(barrier, inc=1, device_id={"tp": lax.rem(z + d, ntp)}, device_id_type=MESH)
    for d in range(1, ndp):
        pl.semaphore_signal(barrier, inc=1, device_id={"dp": lax.rem(x + d, ndp)}, device_id_type=MESH)

    loads[0].wait()
    loads[1].wait()
    kv_buf[par, s] = jnp.concatenate([k_v[...], v_v[...]], axis=0)

    @pl.when(lax.rem(s, 2) == 0)
    def _():
        kv_buf[0, s + 1] = jnp.zeros((rows, 128), BF16)
        kv_buf[1, s + 1] = jnp.zeros((rows, 128), BF16)

    pl.semaphore_wait(barrier, 2 * (nseq - 1) + 2 + (ndp - 1))

    rounds = [d for d in (1, 2, 4, 8) if d < ntp // 2]

    def tell(r):
        for d in (rounds[r], ntp - rounds[r]):
            pl.semaphore_signal(far_sem.at[r], inc=1, device_id={"tp": lax.rem(z + d, ntp)}, device_id_type=MESH)

    def hear(r):
        pl.semaphore_wait(far_sem.at[r], 2)

    if rounds:
        tell(0)

    def kv_copy(kind, at, p, j, **where):
        here = kv_buf.at[p, j]
        return rcopy(here, here, kv_ss.at[kind, at], kv_rs.at[p, j], **where)

    def kv_along(d):
        return kv_copy(0, d, par, s, seq=s + 2 * d)

    def kv_partner(y):
        return kv_copy(1, y, par, 2 * y + core, tp=other)

    for d in (2, 3, 1) if nchip == 4 else range(1, nchip):
        @pl.when(chunk + d < nchip)
        def _(d=d):
            kv_along(d).start()
    kv_partner(chunk).start()

    @pl.when(core == 0)
    def _():
        kv_copy(2, chunk, par, s, seq=sibling).start()

    row_i = lax.broadcasted_iota(jnp.int32, (rows, rows), 0)
    col_i = lax.broadcasted_iota(jnp.int32, (rows, rows), 1)
    causal = row_i >= col_i
    head_i = lax.broadcasted_iota(jnp.int32, (nheads, rows), 0)

    def head_rows(ref):
        out = jnp.zeros((nheads, rows), F32)
        for h in range(nheads):
            out = jnp.where(head_i == h, ref[h], out)
        return out

    wide = nheads * 64
    eb64 = jnp.where(
        lax.broadcasted_iota(jnp.int32, (nheads, wide), 1) // 64
        == lax.broadcasted_iota(jnp.int32, (nheads, wide), 0), 1.0, 0.0,
    ).astype(F32)
    eb128 = jnp.where(
        lax.broadcasted_iota(jnp.int32, (nheads, nheads * 128), 1) // 128
        == lax.broadcasted_iota(jnp.int32, (nheads, nheads * 128), 0), 1.0, 0.0,
    ).astype(F32)

    loads[2].wait()
    zdt = dt_v[...] + head_rows(bias_s)
    dt = jnp.maximum(zdt, 0.0) + jnp.log1p(jnp.exp(-jnp.abs(zdt)))
    sig_z = 1.0 / (1.0 + jnp.exp(-zdt))
    ea = jnp.exp(head_rows(alog_s))
    rate = dt * ea
    cum = mm(rate, jnp.where(row_i <= col_i, 1.0, 0.0).astype(F32), HIGH)
    cum_last = jnp.broadcast_to(cum[:, rows - 1:rows], (nheads, rows))
    cl_all[s] = cum_last

    def cl_copy(d, to):
        return rcopy(cl_all.at[s], cl_all.at[s], cl_ss.at[d], cl_rs.at[s], seq=to)

    for d in range(1, nseq):
        cl_copy(d, lax.rem(s + d, nseq)).start()

    ecum = jnp.exp(-cum)
    w2 = dt * jnp.exp(-(cum_last - cum))
    ecx[...] = mm_tn(ecum, eb64, HIGH)
    w2x[...] = mm_tn(w2, eb64, HIGH)
    cum_b = mm_tn(cum, eb128, HIGH)

    loads[3].wait()
    loads[4].wait()
    gate = gate_v[...].astype(F32)
    cot = cot_v[...].astype(F32)
    sig = 1.0 / (1.0 + jnp.exp(-gate))
    gy[...] = cot * gate * sig
    dsc[...] = cot * sig * (1.0 + gate * (1.0 - sig))
    loads[5].wait()
    gye = (gy[...] * ecx[...]).astype(BF16)
    gye_b[...] = gye
    es_send[...] = mm_tn(gye, read_v[...]).astype(BF16)

    def all_to_all(send, recv, ss, rs, unused=None):
        def copy(d):
            to = lax.rem(s + d, nseq)
            return rcopy(seq_block(send, to, 64), recv.at[s], ss.at[d], rs.at[s], seq=to)
        if unused is None:
            for d in far_first:
                copy(d).start()
        else:
            @pl.when(s != unused)
            def _():
                for d in far_first:
                    copy(d).start()
        recv[s] = send[pl.ds(pl.multiple_of(s * 64, 64), 64), :]
        return copy

    loads[6].wait()
    cb = mm_nt(read_v[...], write_v[...])
    lane_lo = lax.broadcasted_iota(jnp.int32, (rows, 128), 1) < 64
    skip_row = jnp.zeros((1, wide), F32)
    lane_head = lax.broadcasted_iota(jnp.int32, (1, wide), 1) // 64
    for h in range(nheads):
        skip_row = jnp.where(lane_head == h, skip_s[h], skip_row)
    for p in range(nheads // 2):
        lanes = slice(128 * p, 128 * p + 128)
        ws = []
        for c in range(2):
            h = 2 * p + c
            gap = cum_b[:, 128 * h:128 * h + 128] - cum[h:h + 1, :]
            dtl = jnp.where(causal, jnp.exp(-jnp.maximum(gap, 0.0)), 0.0) * dt[h:h + 1, :]
            dtl_b[p, 128 * c:128 * c + 128, :] = dtl
            ws.append((dtl * cb).astype(BF16))
        gp = gy[:, lanes]
        gym = jnp.concatenate([jnp.where(lane_lo, gp, 0.0), jnp.where(lane_lo, 0.0, gp)], axis=0).astype(BF16)
        gym_b[p] = gym
        w_b[p] = jnp.concatenate(ws, axis=1)
        dx[:, lanes] = mm_tn(jnp.concatenate(ws, axis=0), gym) + skip_row[:, lanes] * gp

    if len(rounds) > 1:
        hear(0)
        tell(1)

    for d in (1, 3, 2) if nchip == 4 else range(1, nchip):
        @pl.when(chunk >= d)
        def _(d=d):
            y = chunk - d
            kv_copy(0, 0, par, 2 * y + core, tp=other).wait_recv()
            kv_partner(y).start()
            kv_copy(2, y, par, 2 * y + core, seq=sibling).start()

    es_copy = all_to_all(es_send, es_recv, es_ss, es_rs)

    def wait_from(make, skip_self=True):
        for d in range(1, nseq):
            make(lax.rem(s + d, nseq)).wait_recv()

    def from_partner(y):
        kv_copy(0, 0, 1 - par, 2 * y + core, tp=other).wait_recv()

        @pl.when(jnp.logical_or(y < chunk, core == 0))
        def _():
            kv_copy(3, y, 1 - par, 2 * y + core, seq=sibling).start()

    def visited(turn):
        if nchip != 4:
            return chunk - turn
        return jnp.where(turn < 2, chunk - turn, turn - 2)

    from_partner(chunk)

    if len(rounds) > 2:
        hear(1)
        tell(2)

    loads[7].wait()
    for p in range(nq):
        q_st[128 * p:128 * p + 128, :] = q_v[:, 128 * p:128 * p + 128]
        q_t[:, 128 * p:128 * p + 128] = q_v[:, 128 * p:128 * p + 128].T
    m_buf[...] = jnp.full((nq * rows, 128), NEG_FILL, F32)
    l_buf[...] = jnp.zeros((nq * rows, 128), F32)
    acc[...] = jnp.zeros((nq * rows, 128), F32)

    def scores(turn, carry):
        i = visited(turn)

        @pl.when(turn < chunk)
        def _():
            from_partner(visited(turn + 1))

        @pl.when(jnp.logical_or(i < chunk, core == 1))
        def _():
            for p in range(2):
                kv_copy(0, 0, p, 2 * i + 1 - core, tp=other).wait_recv()

        lo = jnp.concatenate([kv_buf[0, 2 * i], kv_buf[0, 2 * i + 1]], axis=1)
        hi = jnp.concatenate([kv_buf[1, 2 * i], kv_buf[1, 2 * i + 1]], axis=1)
        kk = jnp.concatenate([lo[:64], hi[:64]], axis=0)
        kf[i] = kk
        vf[i] = jnp.concatenate([lo[64:], hi[64:]], axis=0)
        allowed = (
            i * 256 + lax.broadcasted_iota(jnp.int32, (rows, 256), 1)
            <= s * rows + lax.broadcasted_iota(jnp.int32, (rows, 256), 0)
        )
        for p in range(nq):
            r = slice(rows * p, rows * p + rows)
            sc = jnp.where(allowed, mm(q_st[r, :], kk) * scale, NEG_FILL)
            s_buf[i, r, :] = sc
            m_buf[r, :] = jnp.maximum(m_buf[r, :], jnp.maximum(sc[:, :128], sc[:, 128:]))
        return carry

    lax.fori_loop(0, chunk + 1, scores, 0)
    wait_from(lambda j: rcopy(cl_all.at[j], cl_all.at[j], cl_ss.at[0], cl_rs.at[j], seq=j))
    wait_from(lambda j: rcopy(es_recv.at[j], es_recv.at[j], es_ss.at[0], es_rs.at[j], seq=j))

    def back_copy(out, recv, ss, rs, i):
        here = seq_block(recv, s, 64)
        return rcopy(out.at[i], here, ss.at[i], rs.at[s], seq=i)

    own_head = pl.ds(pl.multiple_of(s * 64, 64), 64)

    def send_back(out, recv, ss, rs):
        for d in far_first:
            back_copy(out, recv, ss, rs, lax.rem(s + d, nseq)).start()
        recv[own_head, :] = out[s]

    state = jnp.zeros((64, 128), F32)
    for i in reversed(range(nseq)):
        es_out[i] = state.astype(BF16)
        state = es_recv[i].astype(F32) + jnp.exp(-cl_all[i, pl.ds(s, 1), :]) * state
    send_back(es_out, ex_recv, ex_ss, ex_rs)

    m_buf[...] = jnp.broadcast_to(jnp.max(m_buf[...], axis=1, keepdims=True), (nq * rows, 128))

    def weights(i, carry):
        vv = vf[i]
        for p in range(nq):
            r = slice(rows * p, rows * p + rows)
            m = m_buf[r, :]
            e = jnp.exp(s_buf[i, r, :] - jnp.concatenate([m, m], axis=1))
            s_buf[i, r, :] = e
            l_buf[r, :] += e[:, :128] + e[:, 128:]
            acc[r, :] += mm_nt(e.astype(BF16), vv)
        return carry

    lax.fori_loop(0, chunk + 1, weights, 0)
    total = jnp.sum(l_buf[...], axis=1, keepdims=True)
    inv = jnp.broadcast_to(1.0 / total, (nq * rows, 128))
    l_buf[...] = inv
    acc[...] = acc[...] * inv
    for p in range(nq):
        x_v[:, 128 * p:128 * p + 128] = acc[128 * p:128 * p + 128, :]

    xw = (x_v[...] * w2x[...]).astype(BF16)
    fs_send[...] = mm_tn(xw, write_v[...]).astype(BF16)
    fs_copy = all_to_all(fs_send, fs_recv, fs_ss, fs_rs, nseq - 1)

    m_sum = jnp.zeros((rows, rows), F32)
    col_r = jnp.zeros((nheads, rows), F32)
    row_r = jnp.zeros((nheads, rows), F32)
    ones8 = jnp.ones((8, 128), F32)
    for p in range(nheads // 2):
        lanes = slice(128 * p, 128 * p + 128)
        xp = x_v[:, lanes]
        g = mm_nt(gym_b[p], xp.astype(BF16))
        mp = dtl_b[p] * g
        m_sum = m_sum + mp[:rows] + mp[rows:]
        r0 = mp[:rows] * cb
        r1 = mp[rows:] * cb
        rs = mm_nt(ones8, jnp.concatenate([r0, r1], axis=0), HIGH)
        col_r = jnp.where(head_i == 2 * p, jnp.sum(r0, axis=0, keepdims=True), col_r)
        col_r = jnp.where(head_i == 2 * p + 1, jnp.sum(r1, axis=0, keepdims=True), col_r)
        row_r = jnp.where(head_i == 2 * p, rs[0:1, :rows], row_r)
        row_r = jnp.where(head_i == 2 * p + 1, rs[0:1, rows:], row_r)

    for j in range(nseq - 1):
        @pl.when(s != j)
        def _(j=j):
            rcopy(fs_recv.at[j], fs_recv.at[j], fs_ss.at[0], fs_rs.at[j], seq=j).wait_recv()
    state = jnp.zeros((64, 128), F32)
    for i in range(nseq):
        fs_out[i] = state.astype(BF16)
        if i < nseq - 1:
            state = fs_recv[i].astype(F32) + jnp.exp(-cl_all[i, pl.ds(s, 1), :]) * state
    send_back(fs_out, fi_recv, fi_ss, fi_rs)

    wait_from(lambda j: rcopy(seq_block(ex_recv, j, 64), seq_block(ex_recv, j, 64), ex_ss.at[0], ex_rs.at[j], seq=j))
    exit_g = ex_recv[...]
    dx_exit = mm_nt(write_v[...], exit_g) * w2x[...]
    r_s = mm_nt(eb64, x_v[...] * dx_exit, HIGH)
    gyx = mm_nt(eb64, x_v[...] * gy[...], HIGH)
    dx[...] = dx[...] + dx_exit
    grad_w = mm_tn(m_sum.astype(BF16), read_v[...]) + mm(xw, exit_g)
    gw_send[...] = grad_w.astype(BF16)
    gr_part[...] = mm(m_sum.astype(BF16), write_v[...])

    parts = ntp // 2
    part = rows // parts
    mine = lax.rem(z, parts)

    def p1_copy(send, kind, d):
        to = lax.rem(z + d, ntp)
        return rcopy(
            seq_block(send, lax.rem(to, parts), part), ps_recv.at[kind, z], p1_ss.at[kind, d], p1_rs.at[kind, z], tp=to
        )

    def p1_start(send, kind):
        for d in sorted(range(1, ntp), key=lambda d: abs(d - parts)):
            p1_copy(send, kind, d).start()
        ps_recv[kind, z] = send[pl.ds(pl.multiple_of(mine * part, part), part), :]

    reach = sorted([d for d in range(-((parts - 1) // 2), parts // 2 + 1) if d], key=lambda d: -abs(d))

    def p2_copy(kind, at):
        return rcopy(
            ps_out.at[kind, mine], ps_out.at[kind, mine], p2_ss.at[kind, at], p2_rs.at[kind, mine],
            tp=lax.rem(z + reach[at] + ntp, ntp),
        )

    def p1_finish(kind):
        for d in range(1, ntp):
            j = lax.rem(z + d, ntp)
            rcopy(ps_recv.at[kind, j], ps_recv.at[kind, j], p1_ss.at[0, 0], p1_rs.at[kind, j], tp=j).wait_recv()
        red = ps_recv[kind, 0].astype(F32)
        for j in range(1, ntp):
            red = red + ps_recv[kind, j].astype(F32)
        ps_out[kind, mine] = red.astype(BF16)
        for at in range(len(reach)):
            p2_copy(kind, at).start()

    def p2_finish(kind, out):
        for d in reach:
            c = lax.rem(z - d + ntp, parts)
            rcopy(ps_out.at[kind, c], ps_out.at[kind, c], p2_ss.at[0, 0], p2_rs.at[kind, c], tp=other).wait_recv()
        for c in range(parts):
            out[0, part * c:part * c + part, :] = ps_out[kind, c].astype(F32)

    if rounds:
        hear(len(rounds) - 1)
    p1_start(gw_send, 0)

    for p in range(nq):
        r = slice(rows * p, rows * p + rows)
        ga = dx[:, 128 * p:128 * p + 128]
        gl_st[r, :] = ga.astype(BF16)
        gl_t[:, r] = ga.astype(BF16).T
        delta_b[r, :] = jnp.broadcast_to(
            jnp.sum(ga * x_v[:, 128 * p:128 * p + 128], axis=1, keepdims=True), (rows, 128)
        )
    acc[...] = jnp.zeros((nq * rows, 128), F32)

    def sib_copy(i):
        return rcopy(
            kg_send.at[1 - core, pl.ds(2 * i, 2)], kg_sib.at[i], sib_ss.at[i], sib_rs.at[i], seq=sibling
        )

    def kg_copy(j):
        return rcopy(kg_send.at[core, j], kg_recv.at[core, chunk], kg_ss.at[j], kg_rs.at[core, chunk], seq=j)

    def backward(i, carry):
        kk = kf[i]
        vv = vf[i]
        gk = jnp.zeros((128, 256), F32)
        gv = jnp.zeros((128, 256), F32)
        for p in range(nq):
            r = slice(rows * p, rows * p + rows)
            iv = l_buf[r, :]
            de = delta_b[r, :]
            pr = s_buf[i, r, :] * jnp.concatenate([iv, iv], axis=1)
            ds = (pr * (mm(gl_st[r, :], vv) - jnp.concatenate([de, de], axis=1))).astype(BF16)
            acc[r, :] += mm_nt(ds, kk)
            gv = gv + mm(gl_t[:, r], pr.astype(BF16))
            gk = gk + mm(q_t[:, r], ds)
        gk = (gk * scale).astype(BF16)
        gv = gv.astype(BF16)
        for c in range(2):
            for p in range(2):
                kg_send[p, 2 * i + c] = jnp.concatenate(
                    [gk[64 * p:64 * p + 64, 128 * c:128 * c + 128], gv[64 * p:64 * p + 64, 128 * c:128 * c + 128]], axis=0
                )
        sib_copy(i).start()
        return carry

    lax.fori_loop(0, chunk + 1, backward, 0)
    wait_from(lambda j: rcopy(seq_block(fi_recv, j, 64), seq_block(fi_recv, j, 64), fi_ss.at[0], fi_rs.at[j], seq=j))
    entry = fi_recv[...]
    grad_r = gr_part[...] + mm(gye_b[...], entry)
    gr_send[...] = grad_r.astype(BF16)
    p1_start(gr_send, 1)

    def kg_join(i, carry):
        sib_copy(i).wait()
        both = pl.ds(2 * i, 2)
        kg_send[core, both] = (kg_send[core, both].astype(F32) + kg_sib[i].astype(F32)).astype(BF16)
        for c in range(2):
            j = 2 * i + c

            @pl.when(j != s)
            def _(j=j):
                kg_copy(j).start()
        return carry

    lax.fori_loop(0, chunk + 1, kg_join, 0)

    kg_recv[core, chunk] = kg_send[core, s]

    for p in range(nq):
        gq_o[0, :, 128 * p:128 * p + 128] = acc[128 * p:128 * p + 128, :] * scale
    y_ent = mm_nt(read_v[...], entry) * ecx[...]
    q_sum = mm_nt(eb64, gy[...] * y_ent, HIGH)
    for p in range(nheads // 2):
        lanes = slice(128 * p, 128 * p + 128)
        xp = x_v[:, lanes]
        xm = jnp.concatenate([jnp.where(lane_lo, xp, 0.0), jnp.where(lane_lo, 0.0, xp)], axis=0).astype(BF16)
        y = mm(w_b[p], xm) + y_ent[:, lanes] + skip_row[:, lanes] * xp
        gg_o[0, :, lanes] = dsc[:, lanes] * y

    es_prod = exit_g.astype(F32) * entry.astype(F32)
    c_h = jnp.sum(mm(eb64, es_prod, HIGH), axis=1, keepdims=True) * jnp.exp(-cum_last)
    tail = jnp.where(row_i >= col_i, 1.0, 0.0).astype(F32)
    before = jnp.where(row_i < col_i, 1.0, 0.0).astype(F32)
    drate = mm(col_r - row_r - q_sum, tail, HIGH) - mm(r_s, before, HIGH) - c_h
    ddt = (col_r + r_s) / dt + drate * ea
    draw = ddt * sig_z
    gdt_o[0] = draw

    lane8 = lax.broadcasted_iota(jnp.int32, (nheads, 128), 1)
    pp_all[s] = jnp.where(
        lane8 == 0, jnp.sum(drate * rate, axis=1, keepdims=True),
        jnp.where(
            lane8 == 1, jnp.sum(gyx, axis=1, keepdims=True),
            jnp.where(lane8 == 2, jnp.sum(draw, axis=1, keepdims=True), 0.0),
        ),
    )

    def pa_copy(d):
        return rcopy(pp_all.at[s], pp_all.at[s], pa_ss.at[d], pa_rs.at[s], seq=lax.rem(s + d, nseq))

    for d in far_first:
        pa_copy(d).start()

    p1_finish(0)
    p1_finish(1)

    wait_from(lambda j: rcopy(pp_all.at[j], pp_all.at[j], pa_ss.at[0], pa_rs.at[j], seq=j))
    pd = pp_all[0]
    for j in range(1, nseq):
        pd = pd + pp_all[j]
    pd_all[x] = pd

    def pb_copy(d):
        return rcopy(pd_all.at[x], pd_all.at[x], pb_ss.at[d], pb_rs.at[x], dp=lax.rem(x + d, ndp))

    for d in range(1, ndp):
        pb_copy(d).start()

    def kg_add(y, total):
        for c in range(2):
            @pl.when(jnp.logical_or(y != chunk, core != c))
            def _(c=c):
                rcopy(kg_recv.at[c, y], kg_recv.at[c, y], kg_ss.at[0], kg_rs.at[c, y], tp=other).wait_recv()
        return tuple(total[c] + kg_recv[c, y].astype(F32) for c in range(2))

    blank = jnp.zeros((128, rows), F32)
    half = lax.fori_loop(chunk, nchip, kg_add, (blank, blank))
    for c in range(2):
        kg_sum[c] = half[c]
    kg_give[...] = kg_sum[1 - par].astype(BF16)
    kx_copy = rcopy(kg_give, kg_take, kx_ss, kx_rs, tp=other)
    kx_copy.start()
    kx_copy.wait()
    kg = kg_sum[par] + kg_take[...].astype(F32)
    gk_o[0] = kg[:64]
    gv_o[0] = kg[64:]

    for d in range(1, ndp):
        j = lax.rem(x + d, ndp)
        rcopy(pd_all.at[j], pd_all.at[j], pb_ss.at[0], pb_rs.at[j], dp=j).wait_recv()
    pd = pd_all[0]
    for j in range(1, ndp):
        pd = pd + pd_all[j]
    pf[...] = pd

    p2_finish(0, gw_o)
    p2_finish(1, gr_o)

    for d in range(1, nchip):
        @pl.when(chunk + d < nchip)
        def _(d=d):
            kv_along(d).wait_send()
    for y in range(nchip):
        @pl.when(y <= chunk)
        def _(y=y):
            kv_partner(y).wait_send()

        @pl.when(jnp.logical_or(y < chunk, jnp.logical_and(y == chunk, core == 0)))
        def _(y=y):
            kv_copy(2, y, par, 2 * y + core, seq=sibling).wait_send()
            kv_copy(3, y, 1 - par, 2 * y + core, seq=sibling).wait_send()
    for d in range(1, nseq):
        cl_copy(d, lax.rem(s + d, nseq)).wait_send()
        es_copy(d).wait_send()

        @pl.when(s != nseq - 1)
        def _(d=d):
            fs_copy(d).wait_send()

        pa_copy(d).wait_send()
    for i in range(nseq):
        @pl.when(s != i)
        def _(i=i):
            back_copy(es_out, ex_recv, ex_ss, ex_rs, i).wait_send()
            back_copy(fs_out, fi_recv, fi_ss, fi_rs, i).wait_send()

        @pl.when(jnp.logical_and(i <= 2 * chunk + 1, i != s))
        def _(i=i):
            kg_copy(i).wait_send()
    for kind, send in ((0, gw_send), (1, gr_send)):
        for d in range(1, ntp):
            p1_copy(send, kind, d).wait_send()
        for at in range(len(reach)):
            p2_copy(kind, at).wait_send()
    for d in range(1, ndp):
        pb_copy(d).wait_send()


def body(
    dims, query_rows, key_rows, value_rows, gate_rows, write_vec, read_vec, dt_raw, a_log, skip_gain, dt_bias, out_grad
):
    nseq, ntp, ndp, nheads, nq = dims
    rows = 128
    wide = nheads * 64
    dma = pltpu.SemaphoreType.DMA

    def vm(shape, kind=F32):
        return pltpu.VMEM(shape, kind)

    any_spec = pl.BlockSpec(memory_space=pl.ANY)
    smem_spec = pl.BlockSpec(memory_space=pltpu.SMEM)
    outs = (
        (1, rows, wide), (1, 64, rows), (1, 64, rows), (1, rows, wide), (1, rows, 128), (1, rows, 128),
        (1, nheads, rows), (nheads, 128),
    )
    tall = nq * rows
    scratch = [
        vm((rows, wide), BF16), vm((64, rows), BF16), vm((64, rows), BF16), vm((rows, wide), BF16),
        vm((rows, 128), BF16), vm((rows, 128), BF16), vm((nheads, rows)), vm((rows, wide), BF16),
        vm((2, nseq, 128, rows), BF16), vm((nseq // 2, 128, 2 * rows), BF16), vm((nseq // 2, 128, 2 * rows), BF16),
        vm((tall, 128), BF16), vm((128, tall), BF16), vm((nseq // 2, tall, 256)), vm((tall, 128)), vm((tall, 128)), vm((tall, 128)),
        vm((tall, 128), BF16), vm((128, tall), BF16), vm((tall, 128)),
        vm((rows, wide)), vm((rows, wide)), vm((rows, wide)), vm((rows, wide)), vm((rows, wide)), vm((rows, wide)),
        vm((nheads // 2, 2 * rows, rows)), vm((nheads // 2, rows, 2 * rows), BF16),
        vm((nheads // 2, 2 * rows, 128), BF16), vm((rows, wide), BF16), vm((rows, 128)),
        vm((nseq, nheads, 128)),
        vm((wide, 128), BF16), vm((nseq, 64, 128), BF16), vm((nseq, 64, 128), BF16), vm((wide, 128), BF16),
        vm((wide, 128), BF16), vm((nseq, 64, 128), BF16), vm((nseq, 64, 128), BF16), vm((wide, 128), BF16),
        vm((2, nseq, 128, rows), BF16), vm((nseq // 2, 2, 128, rows), BF16), vm((2, nseq // 2, 128, rows), BF16),
        vm((2, 128, rows)), vm((128, rows), BF16), vm((128, rows), BF16),
        vm((rows, 128), BF16), vm((rows, 128), BF16),
        vm((2, ntp, 2 * rows // ntp, 128), BF16), vm((2, ntp // 2, 2 * rows // ntp, 128), BF16),
        vm((nseq, nheads, 128)), vm((ndp, nheads, 128)),
        pltpu.SemaphoreType.REGULAR((4,)), dma((8,)), dma((4, max(nseq // 2, 4))), dma((2, nseq)), dma((nseq,)), dma((nseq,)),
        dma((nseq,)), dma((nseq,)), dma((nseq,)), dma((nseq,)),
        dma((nseq,)), dma((nseq,)), dma((nseq,)), dma((nseq,)),
        dma((nseq // 2,)), dma((nseq // 2,)), dma((nseq,)), dma((2, nseq // 2)), dma(()), dma(()), dma((2, ntp)), dma((2, ntp)), dma((2, ntp)), dma((2, ntp)),
        dma((nseq,)), dma((nseq,)), dma((ndp,)), dma((ndp,)),
    ]
    results = pl.pallas_call(
        functools.partial(kernel, dims),
        out_shape=tuple(pltpu.VMEM(o, F32) for o in outs),
        in_specs=[any_spec] * 8 + [smem_spec] * 3,
        out_specs=tuple([pl.BlockSpec(memory_space=pltpu.VMEM)] * 8),
        scratch_shapes=scratch,
        compiler_params=pltpu.CompilerParams(
            collective_id=0, has_side_effects=True, vmem_limit_bytes=VMEM
        ),
    )(
        *(
            pltpu.with_memory_space_constraint(a, pltpu.HBM)
            for a in (
                query_rows, jnp.swapaxes(key_rows, 1, 2), jnp.swapaxes(value_rows, 1, 2), gate_rows, write_vec, read_vec,
                dt_raw, out_grad, a_log, skip_gain, dt_bias,
            )
        )
    )
    per_head = jax.ShapeDtypeStruct((nheads,), F32)
    written = pl.pallas_call(
        functools.partial(write_out, nheads),
        out_shape=tuple([jax.ShapeDtypeStruct(o, F32) for o in outs[:7]] + [per_head] * 3),
        in_specs=[any_spec] * 8,
        out_specs=tuple([any_spec] * 7 + [smem_spec] * 3),
        scratch_shapes=[dma(()), dma((8,)), pltpu.SMEM((nheads, 128), F32)],
        compiler_params=pltpu.CompilerParams(vmem_limit_bytes=VMEM),
    )(*results)
    return (
        written[0], jnp.swapaxes(written[1], 1, 2), jnp.swapaxes(written[2], 1, 2), *written[3:],
    )


def write_out(nheads, *refs):
    sources, targets, (load_sem, store_sem, small) = refs[:8], refs[8:18], refs[18:]
    load = pltpu.make_async_copy(sources[7], small, load_sem)
    load.start()
    stores = [pltpu.make_async_copy(a, b, store_sem.at[i]) for i, (a, b) in enumerate(zip(sources[:7], targets[:7]))]
    for copy in stores:
        copy.start()
    load.wait()
    for h in range(nheads):
        for i in range(3):
            targets[7 + i][h] = small[h, i]
    for copy in stores:
        copy.wait()


def solution(mesh):
    dims = (mesh.shape["seq"], mesh.shape["tp"], mesh.shape["dp"], 8, 4)
    wide = P("dp", "seq", "tp")
    shared = P("dp", "seq", None)
    steps = P("dp", "tp", "seq")
    head = P("tp")
    return jax.shard_map(
        functools.partial(body, dims),
        mesh=mesh,
        in_specs=(wide, wide, wide, wide, shared, shared, steps, head, head, head, wide),
        out_specs=(wide, wide, wide, wide, shared, shared, steps, head, head, head),
        check_vma=False,
    )
```
